128 devices in a mesh: blk: 16 (over x, y_lo, core), req: 2 (over y_hi), head: 4 (over z).
Axes of the slice: x: 4, y: 4 (y_hi: 2, y_lo: 2; y = y_hi * 2 + y_lo), z: 4, core: 2. Of those that a mesh axis runs over, the one named last changes fastest.
Arguments:
- query: bfloat16 [8192, 4096], P(('blk', 'req'), 'head'), may hold values from -6 to 6
- key_comp: bfloat16 [8192, 512], P(('blk', 'req'), 'head'), may hold values from -5 to 5
- value_comp: bfloat16 [8192, 512], P(('blk', 'req'), 'head'), may hold values from -5 to 5
- key_prompt: bfloat16 [6144, 512], P('blk', 'head'), may hold values from -6 to 6
- value_prompt: bfloat16 [6144, 512], P('blk', 'head'), may hold values from -5 to 5
- out: bfloat16 [8192, 4096], P(('blk', 'req'), 'head'), may hold values from -5 to 5
- d_out: bfloat16 [8192, 4096], P(('blk', 'req'), 'head'), may hold values from -80 to 80
- steps: int32 [8192], P(('blk', 'req')), may hold values from 0 to 63
Outputs:
- grad_query: bfloat16 [8192, 4096], P(('blk', 'req'), 'head')
- grad_key_comp: bfloat16 [8192, 512], P(('blk', 'req'), 'head')
- grad_value_comp: bfloat16 [8192, 512], P(('blk', 'req'), 'head')
- grad_key_prompt: bfloat16 [6144, 512], P(('blk', 'req'), 'head')
- grad_value_prompt: bfloat16 [6144, 512], P(('blk', 'req'), 'head')
The draws below stay inside these ranges and needn't reach their ends.
All inputs are finite; a program needn't handle non-finite values.
Results may differ from the reference program's by a relative error of at most 0.012.
Values may be sent and summed in bfloat16 or wider, within the bound.
No kernel may reach another device: no remote copies, remote signals or barrier semaphores. Data moves between devices by JAX's collectives and lax.ppermute only.
A program may use at most 192 MiB of HBM per device.

```python
import jax
import jax.numpy as jnp
from jax import lax

HD = 128
KVH = 4
GROUP = 8
QH = 32
CTOK = 256
STEPS = 64
PROMPT = 6144
COMPLETIONS = 32


def draw_query(key, part):
    key = jax.random.fold_in(key, 11)
    shape = (COMPLETIONS * CTOK, QH * HD)
    return jnp.clip(jax.random.normal(key, shape, jnp.float32), -5.0, 5.0).astype(jnp.bfloat16)


def draw_key_prompt(key, part):
    key = jax.random.fold_in(key, 12)
    shape = (PROMPT, KVH * HD)
    return jnp.clip(jax.random.normal(key, shape, jnp.float32), -5.0, 5.0).astype(jnp.bfloat16)


def set_ends(drawn, rng, least, top_value):
    longest = drawn.shape.index(max(drawn.shape))
    spots = []
    for shift in (0, 1):
        where = [jax.random.randint(jax.random.fold_in(rng, axis), (), 0, length) for axis, length in enumerate(drawn.shape)]
        where[longest] = (where[longest] + shift) % drawn.shape[longest]
        spots.append(tuple(where))
    return drawn.at[spots[0]].set(least).at[spots[1]].set(top_value)


def block_levels(rng, extent, cuts, low, largest):
    def one(axis_at, blocks):
        heights = jax.random.uniform(jax.random.fold_in(jax.random.fold_in(rng, 6), axis_at), (blocks,), jnp.float32, low / len(cuts), largest / len(cuts))
        return jnp.repeat(jnp.exp(heights), extent[axis_at] // blocks).reshape((-1,) + (1,) * (len(extent) - axis_at - 1))

    gain = one(*cuts[0])
    for cut in cuts[1:]:
        gain = gain * one(*cut)
    return gain


def scatter_about(stream_key, extent, width, most, shards=(), held_as=jnp.bfloat16):
    values = jax.random.normal(stream_key, extent, jnp.float32) * width
    if len(shards) > 0:
        values = block_levels(stream_key, extent, shards, -0.22, 0.18) * values
    return jnp.clip(values, min=-most, max=most).astype(held_as)


def setup_inputs(seed: int = 0) -> dict:
    key_of = jax.random.split(jax.random.key(seed), 9)
    return {
        "query": draw_query(jax.random.fold_in(key_of[8], 71), 0),
        "key_comp": scatter_about(key_of[1], (COMPLETIONS * CTOK, KVH * HD), 1.0, 5.0, ((0, 32), (1, 4))),
        "value_comp": scatter_about(key_of[2], (COMPLETIONS * CTOK, KVH * HD), 1.0, 5.0, ((0, 32), (1, 4))),
        "key_prompt": draw_key_prompt(jax.random.fold_in(key_of[8], 71), 0),
        "value_prompt": scatter_about(key_of[4], (PROMPT, KVH * HD), 1.0, 5.0, ((0, 16), (1, 4))),
        "out": scatter_about(key_of[5], (COMPLETIONS * CTOK, QH * HD), 1.0, 5.0, ((0, 32), (1, 4))),
        "d_out": scatter_about(key_of[6], (COMPLETIONS * CTOK, QH * HD), 16.0, 80.0, ((0, 32), (1, 4))),
        "steps": set_ends(jax.random.randint(key_of[7], (COMPLETIONS * CTOK,), 0, STEPS), jax.random.fold_in(key_of[7], 1), 0, STEPS - 1).astype(jnp.int32),
    }


def reference(query, key_comp, value_comp, key_prompt, value_prompt, out, d_out, steps):
    score_scale = HD ** -0.5
    num_comp = query.shape[0] // CTOK
    query_all = query.reshape(num_comp, CTOK, KVH, GROUP, HD)
    grad_all = d_out.reshape(num_comp, CTOK, KVH, GROUP, HD)
    out_all = out.reshape(num_comp, CTOK, KVH, GROUP, HD)
    keys_all = key_comp.reshape(num_comp, CTOK, KVH, HD)
    values_all = value_comp.reshape(num_comp, CTOK, KVH, HD)
    step_ids = steps.reshape(num_comp, CTOK)
    prompt_keys = key_prompt.reshape(PROMPT, KVH, HD).astype(jnp.float32)
    prompt_values = value_prompt.reshape(PROMPT, KVH, HD).astype(jnp.float32)

    def per_completion(running, members):
        acc_key, acc_value = running
        query_one, keys_one, values_one, out_one, grad_one, step_one = members
        query_wide = query_one.astype(jnp.float32)
        grad_wide = grad_one.astype(jnp.float32)
        keys_wide = keys_one.astype(jnp.float32)
        values_wide = values_one.astype(jnp.float32)
        prompt_scores = jnp.einsum("tgnd,pgd->tgnp", query_wide, prompt_keys) * score_scale
        self_scores = jnp.einsum("tgnd,jgd->tgnj", query_wide, keys_wide) * score_scale
        visible = step_one[None, :] <= step_one[:, None]
        self_scores = jnp.where(visible[:, None, None, :], self_scores, -jnp.inf)
        row_max = jnp.maximum(prompt_scores.max(-1), self_scores.max(-1))
        row_total = jnp.exp(prompt_scores - row_max[..., None]).sum(-1) + jnp.exp(self_scores - row_max[..., None]).sum(-1)
        log_total = row_max + jnp.log(row_total)
        prompt_probs = jnp.exp(prompt_scores - log_total[..., None])
        self_probs = jnp.exp(self_scores - log_total[..., None])
        out_dot = jnp.sum(grad_wide * out_one.astype(jnp.float32), -1)
        prompt_dprob = jnp.einsum("tgnd,pgd->tgnp", grad_wide, prompt_values)
        self_dprob = jnp.einsum("tgnd,jgd->tgnj", grad_wide, values_wide)
        prompt_dscore = (prompt_probs * (prompt_dprob - out_dot[..., None])).astype(jnp.bfloat16).astype(jnp.float32)
        self_dscore = (self_probs * (self_dprob - out_dot[..., None])).astype(jnp.bfloat16).astype(jnp.float32)
        prompt_low = prompt_probs.astype(jnp.bfloat16).astype(jnp.float32)
        self_low = self_probs.astype(jnp.bfloat16).astype(jnp.float32)
        grad_q = score_scale * (jnp.einsum("tgnp,pgd->tgnd", prompt_dscore, prompt_keys) + jnp.einsum("tgnj,jgd->tgnd", self_dscore, keys_wide))
        grad_kc = score_scale * jnp.einsum("tgnj,tgnd->jgd", self_dscore, query_wide)
        grad_vc = jnp.einsum("tgnj,tgnd->jgd", self_low, grad_wide)
        acc_key = acc_key + jnp.einsum("tgnp,tgnd->pgd", prompt_dscore, query_wide)
        acc_value = acc_value + jnp.einsum("tgnp,tgnd->pgd", prompt_low, grad_wide)
        return (acc_key, acc_value), (grad_q.astype(jnp.bfloat16), grad_kc.astype(jnp.bfloat16), grad_vc.astype(jnp.bfloat16))

    zero_grads = jnp.zeros((PROMPT, KVH, HD), jnp.float32)
    (acc_key, acc_value), (grad_q, grad_kc, grad_vc) = lax.scan(per_completion, (zero_grads, zero_grads), (query_all, keys_all, values_all, out_all, grad_all, step_ids))
    grad_query = grad_q.reshape(num_comp * CTOK, QH * HD)
    grad_key_comp = grad_kc.reshape(num_comp * CTOK, KVH * HD)
    grad_value_comp = grad_vc.reshape(num_comp * CTOK, KVH * HD)
    grad_key_prompt = (score_scale * acc_key).reshape(PROMPT, KVH * HD).astype(jnp.bfloat16)
    grad_value_prompt = acc_value.reshape(PROMPT, KVH * HD).astype(jnp.bfloat16)
    return (grad_query, grad_key_comp, grad_value_comp, grad_key_prompt, grad_value_prompt)
```

```python
import functools

import jax
import jax.numpy as jnp
from jax import lax
from jax.experimental import pallas as pl
from jax.experimental.pallas import tpu as pltpu
from jax.sharding import PartitionSpec as P

HD = 128
GROUP = 8
CTOK = 256
ROWS = 384
TILE = 2 * ROWS
X, Y, CORES = 4, 4, 2
SCALE = HD ** (-0.5)
EXP2_SCALE = SCALE * 1.4426950408889634
VMEM_LIMIT = 56 * 1024 * 1024
F32 = jnp.float32
BF16 = jnp.bfloat16


def place(x, y, core):
    return ((x * 2 + y % 2) * CORES + core) * 2 + y // 2


def send(block, dx=0, dy=0, dc=0):
    route = []
    for x in range(X):
        for y in range(Y):
            for core in range(CORES):
                there = place((x + dx) % X, (y + dy) % Y, core ^ dc)
                route.append((place(x, y, core), there))
    return lax.ppermute(block, ("blk", "req"), route)


def head(ref, n, width):
    return ref[:, n * width : (n + 1) * width]


def dot(a, b, contract):
    return lax.dot_general(a, b, (contract, ((), ())), preferred_element_type=F32)


def fold_scores(scores, n, m_ref, l_ref, e_ref, mt_ref):
    m_old = m_ref[n : n + 1, :]
    m_new = jnp.maximum(m_old, jnp.max(scores, axis=0, keepdims=True))
    e = jnp.exp2(scores - m_new)
    total = jnp.sum(e, axis=0, keepdims=True)
    l_ref[n : n + 1, :] = l_ref[n : n + 1, :] * jnp.exp2(m_old - m_new) + total
    m_ref[n : n + 1, :] = m_new
    mt_ref[0, n : n + 1, :] = m_new
    e_ref[:, n * CTOK : (n + 1) * CTOK] = e.astype(BF16)


def self_scores_kernel(q_ref, k_ref, out_ref, do_ref, col_ref, row_ref, e_ref, mt_ref, m_ref, l_ref, d_ref):
    keys = k_ref[...]
    visible = col_ref[...] <= row_ref[...]
    m_ref[...] = jnp.full((GROUP, CTOK), -1e30, F32)
    l_ref[...] = jnp.zeros((GROUP, CTOK), F32)
    for n in range(GROUP):
        product = head(do_ref, n, HD).astype(F32) * head(out_ref, n, HD).astype(F32)
        d_ref[n : n + 1, :] = jnp.sum(product.T, axis=0, keepdims=True)
        scores = dot(keys, head(q_ref, n, HD), ((1,), (1,))) * EXP2_SCALE
        scores = jnp.where(visible, scores, -jnp.inf)
        fold_scores(scores, n, m_ref, l_ref, e_ref, mt_ref)


def prompt_scores_kernel(q_ref, k_ref, m_in, l_in, e_ref, mt_ref, m_ref, l_ref):
    @pl.when(pl.program_id(0) == 0)
    def _():
        m_ref[...] = m_in[...]
        l_ref[...] = l_in[...]

    keys = k_ref[...]
    for n in range(GROUP):
        scores = dot(keys, head(q_ref, n, HD), ((1,), (1,))) * EXP2_SCALE
        fold_scores(scores, n, m_ref, l_ref, e_ref, mt_ref)


def back_tile(keys, values, q_ref, do_ref, e_ref, mt_ref, log_total, d_ref, dq_ref):
    grad_keys = None
    for n in range(GROUP):
        weight = jnp.exp2(mt_ref[0, n : n + 1, :] - log_total[n : n + 1, :])
        probs = head(e_ref, n, CTOK).astype(F32) * weight
        do_n, q_n = head(do_ref, n, HD), head(q_ref, n, HD)
        grad_prob = dot(values, do_n, ((1,), (1,)))
        grad_score = (probs * (grad_prob - d_ref[n : n + 1, :])).astype(BF16)
        part_value = dot(probs.astype(BF16), do_n, ((1,), (0,)))
        part_key = dot(grad_score, q_n, ((1,), (0,)))
        dq_ref[n] += dot(keys, grad_score, ((0,), (0,)))
        if grad_keys is None:
            grad_keys, grad_values = part_key, part_value
        else:
            grad_keys, grad_values = grad_keys + part_key, grad_values + part_value
    return grad_keys * SCALE, grad_values


def prompt_back_kernel(first, *refs):
    if first:
        q_ref, do_ref, kv_ref, e_ref, mt_ref, m_ref, l_ref, d_ref, here_ref, there_ref, dq_ref = refs
    else:
        q_ref, do_ref, kv_ref, e_ref, mt_ref, m_ref, l_ref, d_ref, dq_in, here_ref, there_ref, dq_ref = refs

    @pl.when(pl.program_id(0) == 0)
    def _():
        dq_ref[...] = jnp.zeros_like(dq_ref) if first else dq_in[...]

    log_total = m_ref[...] + jnp.log2(l_ref[...])
    grad_keys, grad_values = back_tile(
        kv_ref[:, :HD], kv_ref[:, HD:], q_ref, do_ref, e_ref, mt_ref, log_total, d_ref, dq_ref
    )
    here_ref[:, :HD] = grad_keys[:ROWS]
    here_ref[:, HD:] = grad_values[:ROWS]
    there_ref[:, :HD] = grad_keys[ROWS:].astype(BF16)
    there_ref[:, HD:] = grad_values[ROWS:].astype(BF16)


def self_back_kernel(q_ref, do_ref, k_ref, v_ref, e_ref, mt_ref, m_ref, l_ref, d_ref, dq_in, dk_ref, dv_ref, out_ref, dq_ref):
    dq_ref[...] = dq_in[...]
    log_total = m_ref[...] + jnp.log2(l_ref[...])
    grad_keys, grad_values = back_tile(
        k_ref[...], v_ref[...], q_ref, do_ref, e_ref, mt_ref, log_total, d_ref, dq_ref
    )
    dk_ref[...] = grad_keys.astype(BF16)
    dv_ref[...] = grad_values.astype(BF16)
    for n in range(GROUP):
        out_ref[:, n * HD : (n + 1) * HD] = (dq_ref[n] * SCALE).T.astype(BF16)


def whole(shape):
    return pl.BlockSpec(shape, lambda *_: (0,) * len(shape))


PARAMS = pltpu.CompilerParams(vmem_limit_bytes=VMEM_LIMIT)
STAT = (GROUP, CTOK)
WIDE = GROUP * CTOK
DQ = (GROUP, HD, CTOK)


def cost(rows, matmuls, exps, stored):
    return pl.CostEstimate(
        flops=2 * 2 * rows * WIDE * HD * matmuls,
        bytes_accessed=rows * WIDE * 2 * stored,
        transcendentals=rows * WIDE * exps,
    )


def self_scores(query, key_comp, out, d_out, col, row):
    return pl.pallas_call(
        self_scores_kernel,
        out_shape=(
            jax.ShapeDtypeStruct((CTOK, WIDE), BF16),
            jax.ShapeDtypeStruct((1,) + STAT, F32),
            jax.ShapeDtypeStruct(STAT, F32),
            jax.ShapeDtypeStruct(STAT, F32),
            jax.ShapeDtypeStruct(STAT, F32),
        ),
        compiler_params=PARAMS,
        cost_estimate=cost(CTOK, 1, 1, 1),
        name="self_scores",
    )(query, key_comp, out, d_out, col, row)


def prompt_scores(query, kv, m, l):
    tiles = kv.shape[0] // TILE
    return pl.pallas_call(
        prompt_scores_kernel,
        grid=(tiles,),
        in_specs=[
            whole((CTOK, GROUP * HD)),
            pl.BlockSpec((TILE, HD), lambda t: (t, 0)),
            whole(STAT),
            whole(STAT),
        ],
        out_specs=(
            pl.BlockSpec((TILE, WIDE), lambda t: (t, 0)),
            pl.BlockSpec((1,) + STAT, lambda t: (t, 0, 0)),
            whole(STAT),
            whole(STAT),
        ),
        out_shape=(
            jax.ShapeDtypeStruct((tiles * TILE, WIDE), BF16),
            jax.ShapeDtypeStruct((tiles,) + STAT, F32),
            jax.ShapeDtypeStruct(STAT, F32),
            jax.ShapeDtypeStruct(STAT, F32),
        ),
        compiler_params=PARAMS,
        cost_estimate=cost(tiles * TILE, 1, 1, 1),
        name="prompt_scores",
    )(query, kv, m, l)


def prompt_back(query, d_out, kv, e, mt, m, l, d, dq):
    tiles = kv.shape[0] // TILE
    first = dq is None
    return pl.pallas_call(
        functools.partial(prompt_back_kernel, first),
        grid=(tiles,),
        in_specs=[
            whole((CTOK, GROUP * HD)),
            whole((CTOK, GROUP * HD)),
            pl.BlockSpec((TILE, 2 * HD), lambda t: (t, 0)),
            pl.BlockSpec((TILE, WIDE), lambda t: (t, 0)),
            pl.BlockSpec((1,) + STAT, lambda t: (t, 0, 0)),
            whole(STAT),
            whole(STAT),
            whole(STAT),
        ]
        + ([] if first else [whole(DQ)]),
        out_specs=(
            pl.BlockSpec((ROWS, 2 * HD), lambda t: (t, 0)),
            pl.BlockSpec((ROWS, 2 * HD), lambda t: (t, 0)),
            whole(DQ),
        ),
        out_shape=(
            jax.ShapeDtypeStruct((tiles * ROWS, 2 * HD), F32),
            jax.ShapeDtypeStruct((tiles * ROWS, 2 * HD), BF16),
            jax.ShapeDtypeStruct(DQ, F32),
        ),
        compiler_params=PARAMS,
        cost_estimate=cost(tiles * TILE, 4, 0, 1),
        name="prompt_back",
    )(query, d_out, kv, e, mt, m, l, d, *([] if first else [dq]))


def self_back(query, d_out, key_comp, value_comp, e, mt, m, l, d, dq):
    return pl.pallas_call(
        self_back_kernel,
        out_shape=(
            jax.ShapeDtypeStruct((CTOK, HD), BF16),
            jax.ShapeDtypeStruct((CTOK, HD), BF16),
            jax.ShapeDtypeStruct((CTOK, GROUP * HD), BF16),
        ),
        scratch_shapes=[pltpu.VMEM(DQ, F32)],
        compiler_params=PARAMS,
        cost_estimate=cost(CTOK, 4, 0, 1),
        name="self_back",
    )(query, d_out, key_comp, value_comp, e, mt, m, l, d, dq)


def shards(query, key_comp, value_comp, key_prompt, value_prompt, out, d_out, steps):
    here = jnp.concatenate([key_prompt, value_prompt], axis=1)
    low, high = slice(0, ROWS // 2), slice(ROWS // 2, ROWS)

    beside = send(here, dc=1)
    left = send(here, dx=1)
    right = send(here, dx=-1)
    here_y = send(here, dy=1)
    far_low = send(left[low], dx=1)
    far_high = send(right[high], dx=-1)
    left_y = send(left, dy=1)
    right_y = send(right, dy=-1)
    far = jnp.concatenate([far_low, far_high], axis=0)
    far_y = send(far, dy=-1)
    near = jnp.concatenate([here, beside, here_y, send(here_y, dc=1)], axis=0)
    sides = jnp.concatenate(
        [right, send(right, dc=1), right_y, send(right_y, dc=1), left, send(left, dc=1), left_y, send(left_y, dc=1)],
        axis=0,
    )
    opposite = jnp.concatenate([far, send(far, dc=1), far_y, send(far_y, dc=1)], axis=0)

    e_self, mt_self, m, l, d = self_scores(
        query, key_comp, out, d_out, steps.reshape(CTOK, 1), steps.reshape(1, CTOK)
    )
    e_near, mt_near, m, l = prompt_scores(query, near, m, l)
    e_sides, mt_sides, m, l = prompt_scores(query, sides, m, l)
    e_opposite, mt_opposite, m, l = prompt_scores(query, opposite, m, l)

    back = functools.partial(prompt_back, query, d_out)
    mine, theirs, dq = back(opposite, e_opposite, mt_opposite, m, l, d, None)
    total = mine + send(theirs, dc=1).astype(F32)
    total_low = send(total[:, :HD].astype(BF16), dx=1)
    total_high = send(total[:, HD:].astype(BF16), dx=-1)

    mine, theirs, dq = back(sides, e_sides, mt_sides, m, l, d, dq)
    total = mine + send(theirs, dc=1).astype(F32)
    to_right = jnp.concatenate([total[:TILE, :HD] + total_low.astype(F32), total[:TILE, HD:]], axis=1)
    to_left = jnp.concatenate([total[TILE:, :HD], total[TILE:, HD:] + total_high.astype(F32)], axis=1)
    from_left = send(to_right.astype(BF16), dx=1)
    from_right = send(to_left.astype(BF16), dx=-1)

    mine, theirs, dq = back(near, e_near, mt_near, m, l, d, dq)
    total = mine + send(theirs, dc=1).astype(F32) + from_left.astype(F32) + from_right.astype(F32)
    grad_key_comp, grad_value_comp, grad_query = self_back(
        query, d_out, key_comp, value_comp, e_self, mt_self, m, l, d, dq
    )

    total = total.reshape(2, 2, ROWS // 2, 2 * HD)
    y_high = lax.axis_index("req")
    y_low = (lax.axis_index("blk") // CORES) % 2
    up = y_high ^ y_low
    pick = lambda rows, half: lax.dynamic_index_in_dim(rows, half, 0, keepdims=False)
    across = send(pick(total[0], 1 - y_high).astype(BF16), dy=2)
    above = send(pick(total[1], up).astype(BF16), dy=1)
    below = send(pick(total[1], 1 - up).astype(BF16), dy=-1)
    total = pick(total[0], y_high) + across.astype(F32) + above.astype(F32) + below.astype(F32)
    return (
        grad_query,
        grad_key_comp,
        grad_value_comp,
        total[:, :HD].astype(BF16),
        total[:, HD:].astype(BF16),
    )


def solution(mesh):
    rows = P(("blk", "req"), "head")
    return jax.shard_map(
        shards,
        mesh=mesh,
        in_specs=(rows, rows, rows, P("blk", "head"), P("blk", "head"), rows, rows, P(("blk", "req"))),
        out_specs=(rows,) * 5,
        check_vma=False,
    )
```

```python
import functools

import jax
import jax.numpy as jnp
from jax import lax
from jax.experimental import pallas as pl
from jax.experimental.pallas import tpu as pltpu
from jax.sharding import PartitionSpec as P

HD = 128
GROUP = 8
CTOK = 256
ROWS = 384
TILE = 2 * ROWS
X, Y, CORES = 4, 4, 2
SCALE = HD ** (-0.5)
EXP2_SCALE = SCALE * 1.4426950408889634
PLAIN = 60.0
STAT = (GROUP, CTOK)
WIDE = GROUP * CTOK
DQ = (GROUP, HD, CTOK)
F32 = jnp.float32
BF16 = jnp.bfloat16


def place(x, y, core):
    return ((x * 2 + y % 2) * CORES + core) * 2 + y // 2


def send(block, dx=0, dy=0, dc=0):
    route = []
    for x in range(X):
        for y in range(Y):
            for core in range(CORES):
                there = place((x + dx) % X, (y + dy) % Y, core ^ dc)
                route.append((place(x, y, core), there))
    return lax.ppermute(block, ("blk", "req"), route)


def part(ref, n, width):
    return ref[:, n * width : (n + 1) * width]


def dot(a, b, contract):
    return lax.dot_general(a, b, (contract, ((), ())), preferred_element_type=F32)


def largest_norm(rows):
    wide = rows.astype(F32)
    return jnp.max(jnp.sum(wide * wide, axis=1, keepdims=True))


def within(query_norm, key_norm):
    return query_norm * key_norm * (EXP2_SCALE * EXP2_SCALE) <= PLAIN * PLAIN


def plain_tile(keys, q_ref, visible, l_ref, e_ref, rows, mt_ref, tile):
    mt_ref[tile] = jnp.zeros(STAT, F32)
    for n in range(GROUP):
        e = jnp.exp2(dot(keys, part(q_ref, n, HD), ((1,), (1,))) * EXP2_SCALE)
        if visible is not None:
            e = jnp.where(visible, e, 0.0)
        l_ref[n : n + 1, :] += jnp.sum(e, axis=0, keepdims=True)
        e_ref[rows, n * CTOK : (n + 1) * CTOK] = e.astype(BF16)


def general_tile(keys, q_ref, visible, m_ref, l_ref, e_ref, rows, mt_ref, tile):
    for n in range(GROUP):
        scores = dot(keys, part(q_ref, n, HD), ((1,), (1,))) * EXP2_SCALE
        if visible is not None:
            scores = jnp.where(visible, scores, -jnp.inf)
        m_old = m_ref[n : n + 1, :]
        m_new = jnp.maximum(m_old, jnp.max(scores, axis=0, keepdims=True))
        e = jnp.exp2(scores - m_new)
        total = jnp.sum(e, axis=0, keepdims=True)
        l_ref[n : n + 1, :] = l_ref[n : n + 1, :] * jnp.exp2(m_old - m_new) + total
        m_ref[n : n + 1, :] = m_new
        mt_ref[tile, n : n + 1, :] = m_new
        e_ref[rows, n * CTOK : (n + 1) * CTOK] = e.astype(BF16)


def fetch(pairs, sems):
    copies = [pltpu.make_async_copy(far, near, sems.at[at]) for at, (far, near) in enumerate(pairs)]
    for copy in copies:
        copy.start()
    for copy in copies:
        copy.wait()


def pack_kernel(k_hbm, v_hbm, kv_ref, sems):
    fetch([(k_hbm, kv_ref.at[:, :HD]), (v_hbm, kv_ref.at[:, HD:])], sems)


def self_scores_kernel(
    q_hbm, k_hbm, out_hbm, do_hbm, step_hbm, *refs
):
    e_ref, mt_ref, m_ref, l_ref, q_out, do_out, norm_ref, k_ref, out_ref, do_ref, step_ref, sems = refs
    q_ref = q_out
    fetch(
        [(k_hbm, k_ref), (step_hbm, step_ref), (q_hbm, q_ref), (do_hbm, do_ref), (out_hbm, out_ref)], sems
    )
    keys = k_ref[...]
    step = jnp.broadcast_to(step_ref[...].astype(F32), (CTOK, CTOK))
    visible = step.T <= step
    lane = lax.broadcasted_iota(jnp.int32, (CTOK, HD), 1)
    norm = None
    for n in range(GROUP):
        do_n = part(do_ref, n, HD)
        left = jnp.sum(do_n.astype(F32) * part(out_ref, n, HD).astype(F32), axis=1, keepdims=True)
        terms = jnp.zeros((CTOK, HD), F32)
        for place_at in range(3):
            term = left.astype(BF16).astype(F32)
            terms = jnp.where(lane == place_at, -term, terms)
            left = left - term
        do_out[n * CTOK : (n + 1) * CTOK, :HD] = do_n
        do_out[n * CTOK : (n + 1) * CTOK, HD:] = terms.astype(BF16)
        rows = largest_norm(part(q_ref, n, HD))
        norm = rows if norm is None else jnp.maximum(norm, rows)
    norm_ref[0] = norm
    plain = within(norm, largest_norm(keys))
    l_ref[...] = jnp.zeros(STAT, F32)
    rows = slice(0, CTOK)

    @pl.when(plain)
    def _():
        m_ref[...] = jnp.zeros(STAT, F32)
        plain_tile(keys, q_ref, visible, l_ref, e_ref, rows, mt_ref, 0)

    @pl.when(jnp.logical_not(plain))
    def _():
        m_ref[...] = jnp.full(STAT, -1e30, F32)
        general_tile(keys, q_ref, visible, m_ref, l_ref, e_ref, rows, mt_ref, 0)


def prompt_scores_kernel(last, *refs):
    if last:
        norm_ref, q_ref, kv_ref, m_in, l_in, do_ref, e_ref, mt_ref, m_ref, l_ref, wq_ref, wdo_ref = refs
    else:
        norm_ref, q_ref, kv_ref, m_in, l_in, e_ref, mt_ref, m_ref, l_ref = refs
    tile = pl.program_id(0)

    @pl.when(tile == 0)
    def _():
        m_ref[...] = m_in[...]
        l_ref[...] = l_in[...]

    rows = pl.ds(pl.multiple_of(tile * TILE, TILE), TILE)
    keys = kv_ref[rows, :HD]
    plain = within(norm_ref[0], largest_norm(keys)) & (jnp.max(jnp.abs(m_ref[...])) == 0.0)

    @pl.when(plain)
    def _():
        plain_tile(keys, q_ref, None, l_ref, e_ref, rows, mt_ref, tile)

    @pl.when(jnp.logical_not(plain))
    def _():
        general_tile(keys, q_ref, None, m_ref, l_ref, e_ref, rows, mt_ref, tile)

    if last:

        @pl.when(tile == pl.num_programs(0) - 1)
        def _():
            for n in range(GROUP):
                weight = jnp.broadcast_to(1.0 / l_ref[n : n + 1, :], (HD, CTOK)).T
                heads = slice(n * CTOK, (n + 1) * CTOK)
                wq_ref[heads, :] = (part(q_ref, n, HD).astype(F32) * weight).astype(BF16)
                wdo_ref[heads, :] = (do_ref[heads, :HD].astype(F32) * weight).astype(BF16)


def back_tile(keys, values, do_ref, wq_ref, wdo_ref, e_ref, rows, mt_ref, tile, m_ref, dq_ref, give):
    count = keys.shape[0]
    lane = lax.broadcasted_iota(jnp.int32, (count, HD), 1)
    ones = jnp.where(lane < 3, 1.0, 0.0).astype(BF16)
    values = jnp.concatenate([values, ones], axis=1)
    keys_t = keys.T

    def work(changed):
        grad_keys = grad_values = None
        for n in range(GROUP):
            columns = slice(n * CTOK, (n + 1) * CTOK)
            e = e_ref[rows, columns]
            if changed:
                change = jnp.exp2(mt_ref[tile, n : n + 1, :] - m_ref[n : n + 1, :])
                e = (e.astype(F32) * change).astype(BF16)
            grad_prob = dot(values, do_ref[columns, :], ((1,), (1,)))
            part_value = dot(e, wdo_ref[columns, :], ((1,), (0,)))
            grad_score = e * grad_prob.astype(BF16)
            part_key = dot(grad_score, wq_ref[columns, :], ((1,), (0,)))
            dq_ref[n] += dot(keys_t, grad_score, ((1,), (0,)))
            grad_keys = part_key if n == 0 else grad_keys + part_key
            grad_values = part_value if n == 0 else grad_values + part_value
        give(grad_keys * SCALE, grad_values)

    plain = jnp.max(jnp.abs(mt_ref[tile] - m_ref[...])) == 0.0
    pl.when(plain)(lambda: work(False))
    pl.when(jnp.logical_not(plain))(lambda: work(True))


def prompt_back_kernel(first, last, *refs):
    do_ref, wq_ref, wdo_ref, kv_ref, e_ref, mt_ref, m_ref, *refs = refs
    if last:
        l_ref, *refs = refs
    if not first:
        dq_in, *refs = refs
    if last:
        here_ref, there_ref, out_ref, dq_ref = refs[-4:]
    else:
        here_ref, there_ref, dq_ref = refs[-3:]
    step = pl.program_id(0)
    tile = 1 - step

    @pl.when(step == 0)
    def _():
        dq_ref[...] = jnp.zeros_like(dq_ref) if first else dq_in[...]

    rows = pl.ds(pl.multiple_of(tile * TILE, TILE), TILE)

    def give(grad_keys, grad_values):
        @pl.when(step == 0)
        def _():
            there_ref[:, :HD] = grad_keys.astype(BF16)
            there_ref[:, HD:] = grad_values.astype(BF16)

        @pl.when(step == 1)
        def _():
            here_ref[:, :HD] = grad_keys
            here_ref[:, HD:] = grad_values

    back_tile(
        kv_ref[rows, :HD], kv_ref[rows, HD:], do_ref, wq_ref, wdo_ref, e_ref, rows, mt_ref, tile, m_ref, dq_ref, give
    )
    if last:

        @pl.when(step == 1)
        def _():
            for n in range(GROUP):
                weight = SCALE / l_ref[n : n + 1, :]
                out_ref[:, n * HD : (n + 1) * HD] = (dq_ref[n] * weight).T.astype(BF16)


def self_back_kernel(do_ref, wq_ref, wdo_ref, k_ref, v_ref, e_ref, mt_ref, m_ref, dq_in, dk_ref, dv_ref, dq_ref):
    dq_ref[...] = dq_in[...]

    def give(grad_keys, grad_values):
        dk_ref[...] = grad_keys.astype(BF16)
        dv_ref[...] = grad_values.astype(BF16)

    back_tile(
        k_ref[...], v_ref[...], do_ref, wq_ref, wdo_ref, e_ref, slice(0, CTOK), mt_ref, 0, m_ref, dq_ref, give
    )


def params(mib):
    return pltpu.CompilerParams(vmem_limit_bytes=mib * 1024 * 1024)


VMEM = pl.BlockSpec(memory_space=pltpu.VMEM)
HBM = pl.BlockSpec(memory_space=pltpu.HBM)
SMEM = pl.BlockSpec(memory_space=pltpu.SMEM)
UNREAD = pl.BlockSpec(memory_space=pl.ANY)


def whole(dims):
    return pl.BlockSpec(dims, lambda *_: (0,) * len(dims))


def cost(rows, matmuls, exps, stored):
    return pl.CostEstimate(
        flops=2 * rows * WIDE * HD * matmuls,
        bytes_accessed=rows * WIDE * 2 * stored,
        transcendentals=rows * WIDE * exps,
    )


def shape(dims, dtype=F32):
    return jax.ShapeDtypeStruct(dims, dtype)


def pack(keys, values):
    return pl.pallas_call(
        pack_kernel,
        in_specs=[HBM] * 2,
        out_specs=VMEM,
        out_shape=shape((ROWS, 2 * HD), BF16),
        scratch_shapes=[pltpu.SemaphoreType.DMA((2,))],
        compiler_params=params(60),
        name="pack",
    )(keys, values)


def self_scores(query, key_comp, out, d_out, steps):
    return pl.pallas_call(
        self_scores_kernel,
        in_specs=[HBM] * 5,
        out_specs=(VMEM,) * 6 + (SMEM,),
        scratch_shapes=[
            pltpu.VMEM((CTOK, HD), BF16),
            pltpu.VMEM((CTOK, GROUP * HD), BF16),
            pltpu.VMEM((CTOK, GROUP * HD), BF16),
            pltpu.VMEM((1, CTOK), jnp.int32),
            pltpu.SemaphoreType.DMA((5,)),
        ],
        out_shape=(
            shape((CTOK, WIDE), BF16),
            shape((1,) + STAT),
            shape(STAT),
            shape(STAT),
            shape((CTOK, GROUP * HD), BF16),
            shape((WIDE, 2 * HD), BF16),
            shape((1,)),
        ),
        compiler_params=params(57),
        cost_estimate=cost(CTOK, 1, 1, 1),
        name="self_scores",
    )(query, key_comp, out, d_out, steps)


def prompt_scores(norm, query, kv, m, l, d_out=None):
    last = d_out is not None
    return pl.pallas_call(
        functools.partial(prompt_scores_kernel, last),
        grid=(2,),
        in_specs=[SMEM] + [VMEM] * (5 if last else 4),
        out_specs=(VMEM,) * (6 if last else 4),
        out_shape=(
            shape((2 * TILE, WIDE), BF16),
            shape((2,) + STAT),
            shape(STAT),
            shape(STAT),
        )
        + ((shape((WIDE, HD), BF16),) * 2 if last else ()),
        compiler_params=params(16),
        cost_estimate=cost(2 * TILE, 1, 1, 1),
        name="prompt_scores",
    )(norm, query, kv, m, l, *([d_out] if last else []))


def prompt_back(d_out, wq, wdo, kv, e, mt, m, l=None, dq=None, after=()):
    first, last = dq is None, l is not None
    operands = [d_out, wq, wdo, kv, e, mt, m] + ([l] if last else []) + ([] if first else [dq])
    return pl.pallas_call(
        functools.partial(prompt_back_kernel, first, last),
        grid=(2,),
        in_specs=[VMEM] * len(operands) + [UNREAD] * len(after),
        out_specs=(VMEM, VMEM, VMEM),
        out_shape=(
            shape((TILE, 2 * HD)),
            shape((TILE, 2 * HD), BF16),
            shape((CTOK, GROUP * HD), BF16) if last else shape(DQ),
        ),
        scratch_shapes=[pltpu.VMEM(DQ, F32)] if last else [],
        compiler_params=params(20),
        cost_estimate=cost(2 * TILE, 4, 0, 1),
        name="prompt_back",
    )(*operands, *after)


def self_back(d_out, wq, wdo, key_comp, value_comp, e, mt, m, dq):
    return pl.pallas_call(
        self_back_kernel,
        grid=(1,),
        in_specs=[VMEM] * 3 + [whole((CTOK, HD))] * 2 + [VMEM] * 4,
        out_specs=(VMEM, VMEM, VMEM),
        out_shape=(
            shape((CTOK, HD), BF16),
            shape((CTOK, HD), BF16),
            shape(DQ),
        ),
        compiler_params=params(20),
        cost_estimate=cost(CTOK, 4, 0, 1),
        name="self_back",
    )(d_out, wq, wdo, key_comp, value_comp, e, mt, m, dq)


def behind(block, *results):
    return lax.optimization_barrier((block,) + results)[0]


def shards(query, key_comp, value_comp, key_prompt, value_prompt, out, d_out, steps):
    here = pack(key_prompt, value_prompt)
    low, high = slice(0, ROWS // 2), slice(ROWS // 2, ROWS)

    def with_pair(both):
        return jnp.concatenate([both, send(both, dc=1)], axis=0)

    def stack(rows, rows_y):
        return jnp.concatenate([rows, rows_y], axis=0)

    here_y = send(here, dy=1)
    left = send(here, dx=1)
    right = send(here, dx=-1)
    e_self, mt_self, m, l, query, d_out, norm = self_scores(query, key_comp, out, d_out, steps.reshape(1, CTOK))
    near = with_pair(stack(here, here_y))
    far_low = send(left[low], dx=1)
    far_high = send(right[high], dx=-1)
    left_y = send(left, dy=1)
    right_y = send(right, dy=-1)
    e_near, mt_near, m, l = prompt_scores(norm, query, near, m, l)
    far = stack(far_low, far_high)
    far_y = send(behind(far, m), dy=-1)
    on_right = with_pair(behind(stack(right, right_y), m))
    on_left = with_pair(behind(stack(left, left_y), m))
    e_right, mt_right, m, l = prompt_scores(norm, query, on_right, m, l)
    opposite = with_pair(behind(stack(far, far_y), m))
    e_left, mt_left, m, l = prompt_scores(norm, query, on_left, m, l)
    e_far, mt_far, m, l, wq, wdo = prompt_scores(norm, query, opposite, m, l, d_out)

    back = functools.partial(prompt_back, d_out, wq, wdo)
    mine, theirs, dq = back(opposite, e_far, mt_far, m)
    pair_opposite = send(theirs, dc=1)
    mine_right, theirs, dq = back(on_right, e_right, mt_right, m, dq=dq)
    pair_right = send(theirs, dc=1)

    total = mine + pair_opposite.astype(F32)
    total_keys = send(total[:, :HD].astype(BF16), dx=1)
    total_values = send(total[:, HD:].astype(BF16), dx=-1)

    mine_left, theirs, dq = back(on_left, e_left, mt_left, m, dq=dq, after=(pair_opposite, pair_right))
    pair_left = send(theirs, dc=1)
    total = mine_right + pair_right.astype(F32)
    total = jnp.concatenate([total[:, :HD] + total_keys.astype(F32), total[:, HD:]], axis=1)
    from_left = send(total.astype(BF16), dx=1)

    grad_key_comp, grad_value_comp, dq = self_back(d_out, wq, wdo, key_comp, value_comp, e_self, mt_self, m, dq)
    total = mine_left + pair_left.astype(F32)
    total = jnp.concatenate([total[:, :HD], total[:, HD:] + total_values.astype(F32)], axis=1)
    from_right = send(total.astype(BF16), dx=-1)

    mine, theirs, grad_query = back(near, e_near, mt_near, m, l=l, dq=dq, after=(total_keys, total_values, pair_left))
    total = mine + send(theirs, dc=1).astype(F32) + from_left.astype(F32) + from_right.astype(F32)

    total = total.reshape(2, 2, ROWS // 2, 2 * HD)
    y_high = lax.axis_index("req")
    y_low = (lax.axis_index("blk") // CORES) % 2
    up = y_high ^ y_low
    pick = lambda rows, half: lax.dynamic_index_in_dim(rows, half, 0, keepdims=False)
    across = send(pick(total[0], 1 - y_high).astype(BF16), dy=2)
    above = send(pick(total[1], up).astype(BF16), dy=1)
    below = send(pick(total[1], 1 - up).astype(BF16), dy=-1)
    total = pick(total[0], y_high) + across.astype(F32) + above.astype(F32) + below.astype(F32)
    return (
        grad_query,
        grad_key_comp,
        grad_value_comp,
        total[:, :HD].astype(BF16),
        total[:, HD:].astype(BF16),
    )


def solution(mesh):
    rows = P(("blk", "req"), "head")
    return jax.shard_map(
        shards,
        mesh=mesh,
        in_specs=(rows, rows, rows, P("blk", "head"), P("blk", "head"), rows, rows, P(("blk", "req"))),
        out_specs=(rows,) * 5,
        check_vma=False,
    )
```

```python
import functools

import jax
import jax.numpy as jnp
from jax import lax
from jax.experimental import pallas as pl
from jax.experimental.pallas import tpu as pltpu
from jax.sharding import PartitionSpec as P

HD = 128
GROUP = 8
CTOK = 256
ROWS = 384
TILE = 2 * ROWS
X, Y, CORES = 4, 4, 2
SCALE = HD ** (-0.5)
EXP2_SCALE = SCALE * 1.4426950408889634
PLAIN = 60.0
STAT = (GROUP, CTOK)
WIDE = GROUP * CTOK
DQ = (HD, WIDE)
HEADS = 4
F32 = jnp.float32
BF16 = jnp.bfloat16


def place(x, y, core):
    return ((x * 2 + y % 2) * CORES + core) * 2 + y // 2


def send(block, dx=0, dy=0, dc=0):
    route = []
    for x in range(X):
        for y in range(Y):
            for core in range(CORES):
                there = place((x + dx) % X, (y + dy) % Y, core ^ dc)
                route.append((place(x, y, core), there))
    return lax.ppermute(block, ("blk", "req"), route)


def part(ref, n, width):
    return ref[:, n * width : (n + 1) * width]


def dot(a, b, contract):
    return lax.dot_general(a, b, (contract, ((), ())), preferred_element_type=F32)


def largest_norm(rows):
    wide = rows.astype(F32)
    return jnp.max(jnp.sum(wide * wide, axis=1, keepdims=True))


def within(query_norm, key_norm):
    return query_norm * key_norm * (EXP2_SCALE * EXP2_SCALE) <= PLAIN * PLAIN


def plain_tile(keys, q_ref, visible, l_ref, e_ref, rows, mt_ref, tile):
    mt_ref[tile] = jnp.zeros(STAT, F32)
    keys = jnp.concatenate([keys, keys], axis=1)
    for n in range(GROUP):
        e = jnp.exp2(dot(keys, q_ref[n * CTOK : (n + 1) * CTOK, :], ((1,), (1,))))
        if visible is not None:
            e = jnp.where(visible, e, 0.0)
        l_ref[n : n + 1, :] += jnp.sum(e, axis=0, keepdims=True)
        e_ref[rows, n * CTOK : (n + 1) * CTOK] = e.astype(BF16)


def general_tile(keys, q_ref, visible, m_ref, l_ref, e_ref, rows, mt_ref, tile):
    keys = jnp.concatenate([keys, keys], axis=1)
    for n in range(GROUP):
        scores = dot(keys, q_ref[n * CTOK : (n + 1) * CTOK, :], ((1,), (1,)))
        if visible is not None:
            scores = jnp.where(visible, scores, -jnp.inf)
        m_old = m_ref[n : n + 1, :]
        m_new = jnp.maximum(m_old, jnp.max(scores, axis=0, keepdims=True))
        e = jnp.exp2(scores - m_new)
        total = jnp.sum(e, axis=0, keepdims=True)
        l_ref[n : n + 1, :] = l_ref[n : n + 1, :] * jnp.exp2(m_old - m_new) + total
        m_ref[n : n + 1, :] = m_new
        mt_ref[tile, n : n + 1, :] = m_new
        e_ref[rows, n * CTOK : (n + 1) * CTOK] = e.astype(BF16)


def fetch(pairs, sems):
    copies = [pltpu.make_async_copy(far, near, sems.at[at]) for at, (far, near) in enumerate(pairs)]
    for copy in copies:
        copy.start()
    for copy in copies:
        copy.wait()


def pack_kernel(k_hbm, v_hbm, kv_ref, sems):
    fetch([(k_hbm, kv_ref.at[:, :HD]), (v_hbm, kv_ref.at[:, HD:])], sems)


def self_scores_kernel(
    q_hbm, k_hbm, out_hbm, do_hbm, step_hbm, *refs
):
    e_ref, mt_ref, m_ref, l_ref, q_out, do_out, norm_ref, q_ref, k_ref, out_ref, do_ref, step_ref, sems = refs
    fetch(
        [(k_hbm, k_ref), (step_hbm, step_ref), (q_hbm, q_ref), (do_hbm, do_ref), (out_hbm, out_ref)], sems
    )
    keys = k_ref[...]
    step = jnp.broadcast_to(step_ref[...].astype(F32), (CTOK, CTOK))
    visible = step.T <= step
    lane = lax.broadcasted_iota(jnp.int32, (CTOK, HD), 1)
    norm = None
    for n in range(GROUP):
        do_n = part(do_ref, n, HD)
        left = jnp.sum(do_n.astype(F32) * part(out_ref, n, HD).astype(F32), axis=1, keepdims=True)
        terms = jnp.zeros((CTOK, HD), F32)
        for place_at in range(3):
            term = left.astype(BF16).astype(F32)
            terms = jnp.where(lane == place_at, -term, terms)
            left = left - term
        do_out[n * CTOK : (n + 1) * CTOK, :HD] = do_n
        do_out[n * CTOK : (n + 1) * CTOK, HD:] = terms.astype(BF16)
        scaled = part(q_ref, n, HD).astype(F32) * EXP2_SCALE
        high = scaled.astype(BF16)
        q_out[n * CTOK : (n + 1) * CTOK, :HD] = high
        q_out[n * CTOK : (n + 1) * CTOK, HD:] = (scaled - high.astype(F32)).astype(BF16)
        rows = largest_norm(part(q_ref, n, HD))
        norm = rows if norm is None else jnp.maximum(norm, rows)
    norm_ref[0] = norm
    plain = within(norm, largest_norm(keys))
    l_ref[...] = jnp.zeros(STAT, F32)
    rows = slice(0, CTOK)

    @pl.when(plain)
    def _():
        m_ref[...] = jnp.zeros(STAT, F32)
        plain_tile(keys, q_out, visible, l_ref, e_ref, rows, mt_ref, 0)

    @pl.when(jnp.logical_not(plain))
    def _():
        m_ref[...] = jnp.full(STAT, -1e30, F32)
        general_tile(keys, q_out, visible, m_ref, l_ref, e_ref, rows, mt_ref, 0)


def prompt_scores_kernel(last, *refs):
    if last:
        norm_ref, q_ref, kv_ref, m_in, l_in, do_ref, e_ref, mt_ref, m_ref, l_ref, wq_ref, wdo_ref = refs
    else:
        norm_ref, q_ref, kv_ref, m_in, l_in, e_ref, mt_ref, m_ref, l_ref = refs
    tile = pl.program_id(0)

    @pl.when(tile == 0)
    def _():
        m_ref[...] = m_in[...]
        l_ref[...] = l_in[...]

    rows = pl.ds(pl.multiple_of(tile * TILE, TILE), TILE)
    keys = kv_ref[rows, :HD]
    plain = within(norm_ref[0], largest_norm(keys)) & (jnp.max(jnp.abs(m_ref[...])) == 0.0)

    @pl.when(plain)
    def _():
        plain_tile(keys, q_ref, None, l_ref, e_ref, rows, mt_ref, tile)

    @pl.when(jnp.logical_not(plain))
    def _():
        general_tile(keys, q_ref, None, m_ref, l_ref, e_ref, rows, mt_ref, tile)

    if last:

        @pl.when(tile == pl.num_programs(0) - 1)
        def _():
            for n in range(GROUP):
                weight = jnp.broadcast_to(1.0 / l_ref[n : n + 1, :], (HD, CTOK)).T
                heads = slice(n * CTOK, (n + 1) * CTOK)
                q_n = (q_ref[heads, :HD].astype(F32) + q_ref[heads, HD:].astype(F32)) * (1.0 / EXP2_SCALE)
                wq_ref[heads, :] = (q_n * weight).astype(BF16)
                wdo_ref[heads, :] = (do_ref[heads, :HD].astype(F32) * weight).astype(BF16)


def back_rows(kv_parts, e_ref, spans, do_ref, wq_ref, wdo_ref, mt_ref, tile, m_ref, dq_ref, changed):
    stack = lambda parts: parts[0] if len(parts) == 1 else jnp.concatenate(parts, axis=0)
    keys = stack([keys for keys, _ in kv_parts])
    values = stack([values for _, values in kv_parts])
    lane = lax.broadcasted_iota(jnp.int32, values.shape, 1)
    ones = jnp.where(lane < 3, 1.0, 0.0).astype(BF16)
    values = jnp.concatenate([values, ones], axis=1)
    keys_t = keys.T
    grad_keys = grad_values = None
    for n in range(0, GROUP, HEADS):
        columns = slice(n * CTOK, (n + HEADS) * CTOK)
        e = stack([e_ref[span, columns] for span in spans])
        if changed:
            log_change = [mt_ref[tile, h : h + 1, :] - m_ref[h : h + 1, :] for h in range(n, n + HEADS)]
            e = (e.astype(F32) * jnp.exp2(jnp.concatenate(log_change, axis=1))).astype(BF16)
        grad_prob = dot(values, do_ref[columns, :], ((1,), (1,)))
        part_value = dot(e, wdo_ref[columns, :], ((1,), (0,)))
        grad_score = e * grad_prob.astype(BF16)
        part_key = dot(grad_score, wq_ref[columns, :], ((1,), (0,)))
        dq_ref[:, columns] += dot(keys_t, grad_score, ((1,), (0,)))
        grad_keys = part_key if n == 0 else grad_keys + part_key
        grad_values = part_value if n == 0 else grad_values + part_value
    return grad_keys * SCALE, grad_values


def either_way(mt_ref, m_ref, work):
    change = functools.reduce(jnp.maximum, [jnp.abs(mt_ref[t] - m_ref[...]) for t in range(mt_ref.shape[0])])
    plain = jnp.max(change) == 0.0
    pl.when(plain)(lambda: work(False))
    pl.when(jnp.logical_not(plain))(lambda: work(True))


def prompt_back_kernel(first, tiles, *refs):
    do_ref, wq_ref, wdo_ref, kv_ref, e_ref, mt_ref, m_ref, *refs = refs
    here_ref, there_ref, dq_ref = refs[-3:]
    dq_ref[...] = jnp.zeros_like(dq_ref) if first else refs[0][...]

    def work(changed):
        for tile, spans in tiles:
            kv_parts = [(kv_ref[span, :HD], kv_ref[span, HD:]) for span in spans]
            grad_keys, grad_values = back_rows(
                kv_parts, e_ref, spans, do_ref, wq_ref, wdo_ref, mt_ref, tile, m_ref, dq_ref, changed
            )
            middle = 0
            if len(tiles) == 1:
                middle = here_ref.shape[0]
            if tile == 0 or len(tiles) == 1:
                rows = here_ref.shape[0]
                here_ref[:, :HD] = grad_keys[:rows]
                here_ref[:, HD:] = grad_values[:rows]
            if tile == 1 or len(tiles) == 1:
                there_ref[:, :HD] = grad_keys[middle:].astype(BF16)
                there_ref[:, HD:] = grad_values[middle:].astype(BF16)

    either_way(mt_ref, m_ref, work)


def self_back_kernel(
    do_ref, wq_ref, wdo_ref, k_ref, v_ref, e_ref, mt_ref, m_ref, l_ref, dq_in, dk_ref, dv_ref, out_ref, dq_ref
):
    dq_ref[...] = dq_in[...]

    def work(changed):
        grad_keys, grad_values = back_rows(
            [(k_ref[...], v_ref[...])],
            e_ref,
            [slice(0, CTOK)],
            do_ref,
            wq_ref,
            wdo_ref,
            mt_ref,
            0,
            m_ref,
            dq_ref,
            changed,
        )
        dk_ref[...] = grad_keys.astype(BF16)
        dv_ref[...] = grad_values.astype(BF16)

    either_way(mt_ref, m_ref, work)
    for n in range(GROUP):
        weight = SCALE / l_ref[n : n + 1, :]
        out_ref[:, n * HD : (n + 1) * HD] = (part(dq_ref, n, CTOK) * weight).T.astype(BF16)


def params(mib):
    return pltpu.CompilerParams(vmem_limit_bytes=mib * 1024 * 1024)


VMEM = pl.BlockSpec(memory_space=pltpu.VMEM)
HBM = pl.BlockSpec(memory_space=pltpu.HBM)
SMEM = pl.BlockSpec(memory_space=pltpu.SMEM)
UNREAD = pl.BlockSpec(memory_space=pl.ANY)


def whole(dims):
    return pl.BlockSpec(dims, lambda *_: (0,) * len(dims))


def cost(rows, matmuls, exps, stored):
    return pl.CostEstimate(
        flops=2 * rows * WIDE * HD * matmuls,
        bytes_accessed=rows * WIDE * 2 * stored,
        transcendentals=rows * WIDE * exps,
    )


def shape(dims, dtype=F32):
    return jax.ShapeDtypeStruct(dims, dtype)


def pack(keys, values):
    return pl.pallas_call(
        pack_kernel,
        in_specs=[HBM] * 2,
        out_specs=VMEM,
        out_shape=shape((ROWS, 2 * HD), BF16),
        scratch_shapes=[pltpu.SemaphoreType.DMA((2,))],
        compiler_params=params(60),
        name="pack",
    )(keys, values)


def self_scores(query, key_comp, out, d_out, steps):
    return pl.pallas_call(
        self_scores_kernel,
        in_specs=[HBM] * 5,
        out_specs=(VMEM,) * 6 + (SMEM,),
        scratch_shapes=[
            pltpu.VMEM((CTOK, GROUP * HD), BF16),
            pltpu.VMEM((CTOK, HD), BF16),
            pltpu.VMEM((CTOK, GROUP * HD), BF16),
            pltpu.VMEM((CTOK, GROUP * HD), BF16),
            pltpu.VMEM((1, CTOK), jnp.int32),
            pltpu.SemaphoreType.DMA((5,)),
        ],
        out_shape=(
            shape((CTOK, WIDE), BF16),
            shape((1,) + STAT),
            shape(STAT),
            shape(STAT),
            shape((WIDE, 2 * HD), BF16),
            shape((WIDE, 2 * HD), BF16),
            shape((1,)),
        ),
        compiler_params=params(57),
        cost_estimate=cost(CTOK, 1, 1, 1),
        name="self_scores",
    )(query, key_comp, out, d_out, steps)


def prompt_scores(norm, query, kv, m, l, d_out=None):
    last = d_out is not None
    return pl.pallas_call(
        functools.partial(prompt_scores_kernel, last),
        grid=(2,),
        in_specs=[SMEM] + [VMEM] * (5 if last else 4),
        out_specs=(VMEM,) * (6 if last else 4),
        out_shape=(
            shape((2 * TILE, WIDE), BF16),
            shape((2,) + STAT),
            shape(STAT),
            shape(STAT),
        )
        + ((shape((WIDE, HD), BF16),) * 2 if last else ()),
        compiler_params=params(16),
        cost_estimate=cost(2 * TILE, 1, 1, 1),
        name="prompt_scores",
    )(norm, query, kv, m, l, *([d_out] if last else []))


def prompt_back(d_out, wq, wdo, tiles, kv, e, mt, m, dq=None, after=()):
    operands = [d_out, wq, wdo, kv, e, mt, m] + ([] if dq is None else [dq])
    rows = sum(span.stop - span.start for _, spans in tiles for span in spans)
    return pl.pallas_call(
        functools.partial(prompt_back_kernel, dq is None, tiles),
        in_specs=[VMEM] * len(operands) + [UNREAD] * len(after),
        out_specs=(VMEM, VMEM, VMEM),
        out_shape=(
            shape((rows // 2, 2 * HD)),
            shape((rows // 2, 2 * HD), BF16),
            shape(DQ),
        ),
        compiler_params=params(20),
        cost_estimate=cost(rows, 4, 0, 1),
        name="prompt_back",
    )(*operands, *after)


def self_back(d_out, wq, wdo, key_comp, value_comp, e, mt, m, l, dq):
    return pl.pallas_call(
        self_back_kernel,
        grid=(1,),
        in_specs=[VMEM] * 3 + [whole((CTOK, HD))] * 2 + [VMEM] * 5,
        out_specs=(VMEM, VMEM, VMEM),
        out_shape=(
            shape((CTOK, HD), BF16),
            shape((CTOK, HD), BF16),
            shape((CTOK, GROUP * HD), BF16),
        ),
        scratch_shapes=[pltpu.VMEM(DQ, F32)],
        compiler_params=params(20),
        cost_estimate=cost(CTOK, 4, 0, 1),
        name="self_back",
    )(d_out, wq, wdo, key_comp, value_comp, e, mt, m, l, dq)


def behind(block, *results):
    return lax.optimization_barrier((block,) + results)[0]


def shards(query, key_comp, value_comp, key_prompt, value_prompt, out, d_out, steps):
    here = pack(key_prompt, value_prompt)
    def with_pair(both):
        return jnp.concatenate([both, send(both, dc=1)], axis=0)

    def stack(rows, rows_y):
        return jnp.concatenate([rows, rows_y], axis=0)

    left = send(here, dx=1)
    right = send(here, dx=-1)
    here_y = send(here, dy=1)
    e_self, mt_self, m, l, query, d_out, norm = self_scores(query, key_comp, out, d_out, steps.reshape(1, CTOK))
    near = with_pair(stack(here, behind(here_y, m)))
    far = send(left, dx=1)
    left_y = send(left, dy=1)
    right_y = send(right, dy=-1)
    e_near, mt_near, m, l = prompt_scores(norm, query, near, m, l)
    far_y = send(far, dy=-1)
    on_right = with_pair(stack(right, behind(right_y, m)))
    on_left = with_pair(stack(left, behind(left_y, m)))
    e_right, mt_right, m, l = prompt_scores(norm, query, on_right, m, l)
    opposite = with_pair(stack(far, behind(far_y, m)))
    e_left, mt_left, m, l = prompt_scores(norm, query, on_left, m, l)
    e_far, mt_far, m, l, wq, wdo = prompt_scores(norm, query, opposite, m, l, d_out)

    back = functools.partial(prompt_back, d_out, wq, wdo, ((1, [slice(TILE, 2 * TILE)]), (0, [slice(0, TILE)])))
    mine, theirs, dq = back(opposite, e_far, mt_far, m)
    pair = send(theirs, dc=1)
    mine_left, theirs, dq = back(on_left, e_left, mt_left, m, dq=dq)
    pair_left = send(theirs, dc=1)
    from_far = send((mine + pair.astype(F32)).astype(BF16), dx=1)
    from_right = send((mine_left + pair_left.astype(F32)).astype(BF16), dx=-1)
    mine_right, theirs, dq = back(on_right, e_right, mt_right, m, dq=dq, after=(pair, pair_left))
    pair_right = send(theirs, dc=1)
    from_left = send((mine_right + pair_right.astype(F32) + from_far.astype(F32)).astype(BF16), dx=1)
    mine, theirs, dq = back(near, e_near, mt_near, m, dq=dq, after=(from_far, pair_right))
    pair = send(theirs, dc=1)
    total = mine + pair.astype(F32) + from_left.astype(F32) + from_right.astype(F32)

    y_high = lax.axis_index("req")
    y_low = (lax.axis_index("blk") // CORES) % 2
    up = y_high ^ y_low
    half = lambda at: lax.dynamic_slice_in_dim(total, at * (ROWS // 2), ROWS // 2)
    across = send(half(1 - y_high).astype(BF16), dy=2)
    above = send(half(2 + up).astype(BF16), dy=1)
    below = send(half(3 - up).astype(BF16), dy=-1)
    grad_key_comp, grad_value_comp, grad_query = self_back(
        d_out, wq, wdo, key_comp, value_comp, e_self, mt_self, m, l, dq
    )
    total = half(y_high) + above.astype(F32) + below.astype(F32) + across.astype(F32)
    return (
        grad_query,
        grad_key_comp,
        grad_value_comp,
        total[:, :HD].astype(BF16),
        total[:, HD:].astype(BF16),
    )


def solution(mesh):
    rows = P(("blk", "req"), "head")
    return jax.shard_map(
        shards,
        mesh=mesh,
        in_specs=(rows, rows, rows, P("blk", "head"), P("blk", "head"), rows, rows, P(("blk", "req"))),
        out_specs=(rows,) * 5,
        check_vma=False,
    )
```

```python
import functools

import jax
import jax.numpy as jnp
from jax import lax
from jax.experimental import pallas as pl
from jax.experimental.pallas import tpu as pltpu
from jax.sharding import PartitionSpec as P

HD = 128
GROUP = 8
CTOK = 256
ROWS = 384
TILE = 2 * ROWS
HALF = ROWS // 2
X, Y, CORES = 4, 4, 2
SCALE = HD ** (-0.5)
EXP2_SCALE = SCALE * 1.4426950408889634
PLAIN = 60.0
STAT = (GROUP, CTOK)
WIDE = GROUP * CTOK
DQ = (HD, WIDE)
HEADS = 4
F32 = jnp.float32
BF16 = jnp.bfloat16


def place(x, y, core):
    return ((x * 2 + y % 2) * CORES + core) * 2 + y // 2


def send(block, dx=0, dy=0, dc=0):
    route = []
    for x in range(X):
        for y in range(Y):
            for core in range(CORES):
                there = place((x + dx) % X, (y + dy) % Y, core ^ dc)
                route.append((place(x, y, core), there))
    return lax.ppermute(block, ("blk", "req"), route)


def part(ref, n, width):
    return ref[:, n * width : (n + 1) * width]


def dot(a, b, contract):
    return lax.dot_general(a, b, (contract, ((), ())), preferred_element_type=F32)


def largest_norm(rows):
    wide = rows.astype(F32)
    return jnp.max(jnp.sum(wide * wide, axis=1, keepdims=True))


def within(query_norm, key_norm):
    return query_norm * key_norm * (EXP2_SCALE * EXP2_SCALE) <= PLAIN * PLAIN


def put(e, n, parts):
    low = e.astype(BF16)
    start = 0
    for ref in parts:
        ref[:, n * CTOK : (n + 1) * CTOK] = low[start : start + ref.shape[0]]
        start += ref.shape[0]


def plain_tile(keys, q_ref, visible, l_ref, parts, mt_ref, tile):
    mt_ref[tile] = jnp.zeros(STAT, F32)
    keys = jnp.concatenate([keys, keys], axis=1)
    for n in range(GROUP):
        e = jnp.exp2(dot(keys, q_ref[n * CTOK : (n + 1) * CTOK, :], ((1,), (1,))))
        if visible is not None:
            e = jnp.where(visible, e, 0.0)
        l_ref[n : n + 1, :] += jnp.sum(e, axis=0, keepdims=True)
        put(e, n, parts)


def general_tile(keys, q_ref, visible, m_ref, l_ref, parts, mt_ref, tile):
    keys = jnp.concatenate([keys, keys], axis=1)
    for n in range(GROUP):
        scores = dot(keys, q_ref[n * CTOK : (n + 1) * CTOK, :], ((1,), (1,)))
        if visible is not None:
            scores = jnp.where(visible, scores, -jnp.inf)
        m_old = m_ref[n : n + 1, :]
        m_new = jnp.maximum(m_old, jnp.max(scores, axis=0, keepdims=True))
        e = jnp.exp2(scores - m_new)
        total = jnp.sum(e, axis=0, keepdims=True)
        l_ref[n : n + 1, :] = l_ref[n : n + 1, :] * jnp.exp2(m_old - m_new) + total
        m_ref[n : n + 1, :] = m_new
        mt_ref[tile, n : n + 1, :] = m_new
        put(e, n, parts)


def y_place():
    y_high = lax.axis_index("req")
    y_low = lax.rem(lax.div(lax.axis_index("blk"), CORES), 2)
    return y_high, jnp.where(y_low == 0, y_high, 1 - y_high)


def half_rows(at):
    return pl.ds(pl.multiple_of(at * HALF, HALF), HALF)


def fetch(pairs, sems):
    copies = [pltpu.make_async_copy(far, near, sems.at[at]) for at, (far, near) in enumerate(pairs)]
    for copy in copies:
        copy.start()
    for copy in copies:
        copy.wait()


def pack_kernel(k_hbm, v_hbm, kv_ref, turned_ref, sems):
    y_high, _ = y_place()
    pairs = []
    for far, columns in ((k_hbm, slice(0, HD)), (v_hbm, slice(HD, 2 * HD))):
        pairs.append((far, kv_ref.at[:, columns]))
        pairs.append((far.at[half_rows(1 - y_high), :], turned_ref.at[:HALF, columns]))
        pairs.append((far.at[half_rows(y_high), :], turned_ref.at[HALF:, columns]))
    fetch(pairs, sems)


def self_scores_kernel(
    q_hbm, k_hbm, out_hbm, do_hbm, step_hbm, *refs
):
    e_ref, mt_ref, m_ref, l_ref, q_out, do_out, norm_ref, q_ref, k_ref, out_ref, do_ref, step_ref, sems = refs
    fetch(
        [(k_hbm, k_ref), (step_hbm, step_ref), (q_hbm, q_ref), (do_hbm, do_ref), (out_hbm, out_ref)], sems
    )
    keys = k_ref[...]
    step = jnp.broadcast_to(step_ref[...].astype(F32), (CTOK, CTOK))
    visible = step.T <= step
    lane = lax.broadcasted_iota(jnp.int32, (CTOK, HD), 1)
    norm = None
    for n in range(GROUP):
        do_n = part(do_ref, n, HD)
        left = jnp.sum(do_n.astype(F32) * part(out_ref, n, HD).astype(F32), axis=1, keepdims=True)
        terms = jnp.zeros((CTOK, HD), F32)
        for place_at in range(3):
            term = left.astype(BF16).astype(F32)
            terms = jnp.where(lane == place_at, -term, terms)
            left = left - term
        do_out[n * CTOK : (n + 1) * CTOK, :HD] = do_n
        do_out[n * CTOK : (n + 1) * CTOK, HD:] = terms.astype(BF16)
        scaled = part(q_ref, n, HD).astype(F32) * EXP2_SCALE
        high = scaled.astype(BF16)
        q_out[n * CTOK : (n + 1) * CTOK, :HD] = high
        q_out[n * CTOK : (n + 1) * CTOK, HD:] = (scaled - high.astype(F32)).astype(BF16)
        rows = largest_norm(part(q_ref, n, HD))
        norm = rows if norm is None else jnp.maximum(norm, rows)
    norm_ref[0] = norm
    l_ref[...] = jnp.zeros(STAT, F32)
    m_ref[...] = jnp.zeros(STAT, F32)
    plain_tile(keys, q_out, visible, l_ref, [e_ref], mt_ref, 0)

    @pl.when(jnp.logical_not(within(norm, largest_norm(keys))))
    def _():
        l_ref[...] = jnp.zeros(STAT, F32)
        m_ref[...] = jnp.full(STAT, -1e30, F32)
        general_tile(keys, q_out, visible, m_ref, l_ref, [e_ref], mt_ref, 0)


def prompt_scores_kernel(last, pieces, *refs):
    norm_ref, q_ref, kv_ref, m_in, l_in, *refs = refs
    if last:
        do_ref, *refs = refs
    e_refs, refs = refs[: 2 * pieces], refs[2 * pieces :]
    mt_ref, m_ref, l_ref, *refs = refs
    m_ref[...] = m_in[...]
    l_ref[...] = l_in[...]
    for tile in range(2):
        keys = kv_ref[tile * TILE : (tile + 1) * TILE, :HD]
        parts = e_refs[tile * pieces : (tile + 1) * pieces]
        l_old = l_ref[...]
        plain = within(norm_ref[0], largest_norm(keys)) & (jnp.max(jnp.abs(m_ref[...])) == 0.0)
        plain_tile(keys, q_ref, None, l_ref, parts, mt_ref, tile)

        @pl.when(jnp.logical_not(plain))
        def _():
            l_ref[...] = l_old
            general_tile(keys, q_ref, None, m_ref, l_ref, parts, mt_ref, tile)

    if last:
        wq_ref, wdo_ref = refs
        for n in range(GROUP):
            weight = jnp.broadcast_to(1.0 / l_ref[n : n + 1, :], (HD, CTOK)).T
            heads = slice(n * CTOK, (n + 1) * CTOK)
            q_n = (q_ref[heads, :HD].astype(F32) + q_ref[heads, HD:].astype(F32)) * (1.0 / EXP2_SCALE)
            wq_ref[heads, :] = (q_n * weight).astype(BF16)
            wdo_ref[heads, :] = (do_ref[heads, :HD].astype(F32) * weight).astype(BF16)


def stack(parts):
    return parts[0] if len(parts) == 1 else jnp.concatenate(parts, axis=0)


def back_rows(pieces, do_ref, wq_ref, wdo_ref, m_ref, dq_ref, changed):
    keys = stack([keys for keys, _, _, _ in pieces])
    values = stack([values for _, values, _, _ in pieces])
    lane = lax.broadcasted_iota(jnp.int32, values.shape, 1)
    ones = jnp.where(lane < 3, 1.0, 0.0).astype(BF16)
    values = jnp.concatenate([values, ones], axis=1)
    keys_t = keys.T
    grad_keys = grad_values = None
    for n in range(0, GROUP, HEADS):
        columns = slice(n * CTOK, (n + HEADS) * CTOK)
        parts = []
        for _, _, e_ref, top in pieces:
            e = e_ref[:, columns]
            if changed:
                log_change = [top[h : h + 1, :] - m_ref[h : h + 1, :] for h in range(n, n + HEADS)]
                e = (e.astype(F32) * jnp.exp2(jnp.concatenate(log_change, axis=1))).astype(BF16)
            parts.append(e)
        e = stack(parts)
        grad_prob = dot(values, do_ref[columns, :], ((1,), (1,)))
        part_value = dot(e, wdo_ref[columns, :], ((1,), (0,)))
        grad_score = e * grad_prob.astype(BF16)
        part_key = dot(grad_score, wq_ref[columns, :], ((1,), (0,)))
        dq_ref[:, columns] += dot(keys_t, grad_score, ((1,), (0,)))
        grad_keys = part_key if n == 0 else grad_keys + part_key
        grad_values = part_value if n == 0 else grad_values + part_value
    return grad_keys * SCALE, grad_values


def either_way(m_ref, mt_refs, work):
    tops = [mt_ref[t] for mt_ref in mt_refs for t in range(mt_ref.shape[0])]
    change = functools.reduce(jnp.maximum, [jnp.abs(top - m_ref[...]) for top in tops])
    plain = jnp.max(change) == 0.0
    pl.when(plain)(lambda: work(False))
    pl.when(jnp.logical_not(plain))(lambda: work(True))


def prompt_back_kernel(first, tiles, sources, blocks, unread, *refs):
    do_ref, wq_ref, wdo_ref, m_ref, *refs = refs
    if not first:
        dq_in, *refs = refs
    kv_refs, refs = refs[:sources], refs[sources:]
    mt_refs, refs = refs[:sources], refs[sources:]
    e_refs, refs = refs[:blocks], refs[blocks + unread :]
    *out_refs, dq_ref = refs
    dq_ref[...] = jnp.zeros_like(dq_ref) if first else dq_in[...]

    def work(changed):
        for members, outs in tiles:
            pieces = []
            for source, row, block in members:
                e_ref = e_refs[block]
                rows = slice(row, row + e_ref.shape[0])
                kv_ref = kv_refs[source]
                pieces.append((kv_ref[rows, :HD], kv_ref[rows, HD:], e_ref, mt_refs[source][row // TILE]))
            grad_keys, grad_values = back_rows(pieces, do_ref, wq_ref, wdo_ref, m_ref, dq_ref, changed)
            start = 0
            for at in outs:
                ref = out_refs[at]
                rows = slice(start, start + ref.shape[0])
                ref[:, :HD] = grad_keys[rows].astype(ref.dtype)
                ref[:, HD:] = grad_values[rows].astype(ref.dtype)
                start += ref.shape[0]

    either_way(m_ref, mt_refs, work)


def self_back_kernel(do_ref, wq_ref, wdo_ref, m_ref, l_ref, dq_in, k_ref, v_ref, e_ref, mt_ref, *refs):
    dk_ref, dv_ref, out_ref, dq_ref = refs[-4:]
    dq_ref[...] = dq_in[...]

    def work(changed):
        pieces = [(k_ref[...], v_ref[...], e_ref, mt_ref[0])]
        grad_keys, grad_values = back_rows(pieces, do_ref, wq_ref, wdo_ref, m_ref, dq_ref, changed)
        dk_ref[...] = grad_keys.astype(BF16)
        dv_ref[...] = grad_values.astype(BF16)

    either_way(m_ref, [mt_ref], work)
    for n in range(GROUP):
        weight = SCALE / l_ref[n : n + 1, :]
        out_ref[:, n * HD : (n + 1) * HD] = (part(dq_ref, n, CTOK) * weight).T.astype(BF16)


def combine_kernel(mine_ref, pair_ref, left_ref, right_ref, across_ref, above_ref, below_ref, own_ref):
    y_high, up = y_place()

    def arrived(at):
        rows = half_rows(at)
        return left_ref[rows, :].astype(F32) + right_ref[rows, :].astype(F32)

    def leaving(at, beside):
        rows = half_rows(at)
        return (mine_ref[rows, :] + pair_ref[rows, :].astype(F32) + arrived(beside)).astype(BF16)

    across_ref[...] = leaving(0, 1 - y_high)
    above_ref[...] = leaving(1 + up, 2 + up)
    below_ref[...] = leaving(2 - up, 3 - up)
    own_ref[...] = arrived(y_high)


def finish_kernel(own_ref, mine_ref, pair_ref, across_ref, above_ref, below_ref, dk_ref, dv_ref):
    total = own_ref[...] + mine_ref[...]
    for ref in (pair_ref, across_ref, above_ref, below_ref):
        total = total + ref[...].astype(F32)
    dk_ref[...] = total[:, :HD].astype(BF16)
    dv_ref[...] = total[:, HD:].astype(BF16)


def params(mib):
    return pltpu.CompilerParams(vmem_limit_bytes=mib * 1024 * 1024)


VMEM = pl.BlockSpec(memory_space=pltpu.VMEM)
HBM = pl.BlockSpec(memory_space=pltpu.HBM)
SMEM = pl.BlockSpec(memory_space=pltpu.SMEM)
UNREAD = pl.BlockSpec(memory_space=pl.ANY)


def whole(dims):
    return pl.BlockSpec(dims, lambda *_: (0,) * len(dims))


def cost(rows, matmuls, exps, stored):
    return pl.CostEstimate(
        flops=2 * rows * WIDE * HD * matmuls,
        bytes_accessed=rows * WIDE * 2 * stored,
        transcendentals=rows * WIDE * exps,
    )


def shape(dims, dtype=F32):
    return jax.ShapeDtypeStruct(dims, dtype)


def pack(keys, values):
    return pl.pallas_call(
        pack_kernel,
        in_specs=[HBM] * 2,
        out_specs=(VMEM,) * 2,
        out_shape=(shape((ROWS, 2 * HD), BF16),) * 2,
        scratch_shapes=[pltpu.SemaphoreType.DMA((6,))],
        compiler_params=params(60),
        name="pack",
    )(keys, values)


def self_scores(query, key_comp, out, d_out, steps):
    return pl.pallas_call(
        self_scores_kernel,
        in_specs=[HBM] * 5,
        out_specs=(VMEM,) * 6 + (SMEM,),
        scratch_shapes=[
            pltpu.VMEM((CTOK, GROUP * HD), BF16),
            pltpu.VMEM((CTOK, HD), BF16),
            pltpu.VMEM((CTOK, GROUP * HD), BF16),
            pltpu.VMEM((CTOK, GROUP * HD), BF16),
            pltpu.VMEM((1, CTOK), jnp.int32),
            pltpu.SemaphoreType.DMA((5,)),
        ],
        out_shape=(
            shape((CTOK, WIDE), BF16),
            shape((1,) + STAT),
            shape(STAT),
            shape(STAT),
            shape((WIDE, 2 * HD), BF16),
            shape((WIDE, 2 * HD), BF16),
            shape((1,)),
        ),
        compiler_params=params(57),
        cost_estimate=cost(CTOK, 1, 1, 1),
        name="self_scores",
    )(query, key_comp, out, d_out, steps)


def prompt_scores(norm, query, kv, m, l, split=(ROWS, ROWS), d_out=None):
    last = d_out is not None
    blocks = 2 * len(split)
    results = pl.pallas_call(
        functools.partial(prompt_scores_kernel, last, len(split)),
        in_specs=[SMEM] + [VMEM] * (5 if last else 4),
        out_specs=(VMEM,) * (blocks + (5 if last else 3)),
        out_shape=tuple(shape((rows, WIDE), BF16) for rows in split) * 2
        + (shape((2,) + STAT), shape(STAT), shape(STAT))
        + ((shape((WIDE, HD), BF16),) * 2 if last else ()),
        compiler_params=params(16),
        cost_estimate=cost(2 * TILE, 1, 1, 1),
        name="prompt_scores",
    )(norm, query, kv, m, l, *([d_out] if last else []))
    return results[:blocks], *results[blocks:]


def prompt_back(shared, dq, sources, tiles, es, outs, after=(), matmuls=4):
    kvs, mts = zip(*sources)
    operands = [*shared] + ([] if dq is None else [dq]) + [*kvs, *mts, *es]
    return pl.pallas_call(
        functools.partial(prompt_back_kernel, dq is None, tiles, len(kvs), len(es), len(after)),
        in_specs=[VMEM] * len(operands) + [UNREAD] * len(after),
        out_specs=(VMEM,) * (len(outs) + 1),
        out_shape=tuple(shape((rows, 2 * HD), dtype) for rows, dtype in outs) + (shape(DQ),),
        compiler_params=params(20),
        cost_estimate=cost(sum(e.shape[0] for e in es), matmuls, 0, min(matmuls, 1)),
        name="prompt_back",
    )(*operands, *after)


def self_back(shared, l, dq, key_comp, value_comp, e, mt, after=()):
    operands = [*shared, l, dq, key_comp, value_comp, e, mt]
    return pl.pallas_call(
        self_back_kernel,
        in_specs=[VMEM] * len(operands) + [UNREAD] * len(after),
        out_specs=(VMEM,) * 3,
        out_shape=(
            shape((CTOK, HD), BF16),
            shape((CTOK, HD), BF16),
            shape((CTOK, GROUP * HD), BF16),
        ),
        scratch_shapes=[pltpu.VMEM(DQ, F32)],
        compiler_params=params(20),
        cost_estimate=cost(CTOK, 4, 0, 1),
        name="self_back",
    )(*operands, *after)


def combine(*arrays):
    return pl.pallas_call(
        combine_kernel,
        in_specs=[VMEM] * 4,
        out_specs=(VMEM,) * 4,
        out_shape=(shape((HALF, 2 * HD), BF16),) * 3 + (shape((HALF, 2 * HD)),),
        compiler_params=params(6),
        name="combine",
    )(*arrays)


def finish(*arrays):
    return pl.pallas_call(
        finish_kernel,
        in_specs=[VMEM] * 6,
        out_specs=(VMEM,) * 2,
        out_shape=(shape((HALF, HD), BF16),) * 2,
        compiler_params=params(6),
        name="finish",
    )(*arrays)


def behind(result, *blocks):
    return lax.optimization_barrier(blocks + (result,))[:-1]


def shards(query, key_comp, value_comp, key_prompt, value_prompt, out, d_out, steps):
    here, turned = pack(key_prompt, value_prompt)

    here_y = send(here, dy=1)
    left = send(here, dx=1)
    right = send(here, dx=-1)
    e_self, mt_self, m, l, query, d_out, norm = self_scores(query, key_comp, out, d_out, steps.reshape(1, CTOK))
    here_y, left, right = behind(m, here_y, left, right)
    near = stack([turned, here_y])
    beside = stack([left, right])
    near = stack([near, send(near, dc=1)])
    beside_pair = send(beside, dc=1)
    far = send(left, dx=1)
    left_y = send(left, dy=1)
    right_y = send(right, dy=-1)
    e_near, mt_near, m, l = prompt_scores(norm, query, near, m, l, split=(HALF, HALF, ROWS))
    far, left_y, right_y, beside_pair = behind(m, far, left_y, right_y, beside_pair)
    beside = stack([beside, beside_pair])
    corners = stack([left_y, right_y])
    corners_pair = send(corners, dc=1)
    far_y = send(far, dy=-1)
    e_beside, mt_beside, m, l = prompt_scores(norm, query, beside, m, l)
    far_y, corners_pair = behind(m, far_y, corners_pair)
    corners = stack([corners, corners_pair])
    opposite = stack([far, far_y])
    opposite_pair = send(opposite, dc=1)
    e_corners, mt_corners, m, l = prompt_scores(norm, query, corners, m, l)
    (opposite_pair,) = behind(m, opposite_pair)
    opposite = stack([opposite, opposite_pair])
    e_far, mt_far, m, l, wq, wdo = prompt_scores(norm, query, opposite, m, l, d_out=d_out)

    shared = d_out, wq, wdo, m
    add = lambda *parts: sum(rows.astype(F32) for rows in parts)
    far_source = [(opposite, mt_far)]
    theirs, dq = prompt_back(
        shared, None, far_source, [([(0, TILE, 0), (0, TILE + ROWS, 1)], [0])], e_far[2:], [(TILE, BF16)]
    )
    pair_far = send(theirs, dc=1)
    mine_far, dq = prompt_back(shared, dq, far_source, [([(0, 0, 0), (0, ROWS, 1)], [0])], e_far[:2], [(TILE, F32)])
    (pair_far,) = behind(mine_far, pair_far)
    from_far = send(add(mine_far, pair_far).astype(BF16), dx=1)

    sources = [(beside, mt_beside), (corners, mt_corners)]
    outs = [(TILE, F32), (TILE, BF16)]

    def side(at, dq, after, matmuls):
        row = at * ROWS
        tiles = [
            ([(0, TILE + row, 1), (1, TILE + row, 3)], [1]),
            ([(0, row, 0), (1, row, 2)], [0]),
        ]
        es = [e_beside[at], e_beside[2 + at], e_corners[at], e_corners[2 + at]]
        return prompt_back(shared, dq, sources, tiles, es, outs, after, matmuls)

    mine_left, theirs, dq = side(0, dq, (), 4)
    pair_left = send(theirs, dc=1)
    mine_right, theirs, dq = side(1, dq, (from_far,), 4)
    from_far, pair_left = behind(theirs, from_far, pair_left)
    pair_right = send(theirs, dc=1)
    from_right = send(add(mine_left, pair_left).astype(BF16), dx=-1)
    from_left = send(add(mine_right, pair_right, from_far).astype(BF16), dx=1)

    near_source = [(near, mt_near)]
    tiles = [([(0, TILE, 1), (0, TILE + ROWS, 3)], [1]), ([(0, 0, 0), (0, ROWS, 2)], [0])]
    es = [e_near[0], e_near[3], e_near[2], e_near[5]]
    outs = [(HALF + ROWS, F32), (HALF + ROWS, BF16)]
    mine, theirs, dq = prompt_back(shared, dq, near_source, tiles, es, outs, (from_far, pair_right))
    theirs, from_left, from_right = behind(mine, theirs, from_left, from_right)
    across, above, below, own = combine(mine, send(theirs, dc=1), from_left, from_right)
    across = send(across, dy=2)
    above = send(above, dy=1)
    below = send(below, dy=-1)
    tiles = [([(0, HALF, 0), (0, TILE + HALF, 1)], [0, 1])]
    es = [e_near[1], e_near[4]]
    mine, theirs, dq = prompt_back(shared, dq, near_source, tiles, es, [(HALF, F32), (HALF, BF16)], (own,))
    pair = send(theirs, dc=1)
    grad_key_comp, grad_value_comp, grad_query = self_back(shared, l, dq, key_comp, value_comp, e_self, mt_self)
    pair, across, above, below = behind(grad_key_comp, pair, across, above, below)
    grad_key_prompt, grad_value_prompt = finish(own, mine, pair, across, above, below)
    return (grad_query, grad_key_comp, grad_value_comp, grad_key_prompt, grad_value_prompt)


def solution(mesh):
    rows = P(("blk", "req"), "head")
    return jax.shard_map(
        shards,
        mesh=mesh,
        in_specs=(rows, rows, rows, P("blk", "head"), P("blk", "head"), rows, rows, P(("blk", "req"))),
        out_specs=(rows,) * 5,
        check_vma=False,
    )
```

```python
import functools

import jax
import jax.numpy as jnp
from jax import lax
from jax.experimental import pallas as pl
from jax.experimental.pallas import tpu as pltpu
from jax.sharding import PartitionSpec as P

HD = 128
GROUP = 8
CTOK = 256
ROWS = 384
TILE = 2 * ROWS
HALF = ROWS // 2
X, Y, CORES = 4, 4, 2
SCALE = HD ** (-0.5)
EXP2_SCALE = SCALE * 1.4426950408889634
PLAIN = 60.0
STAT = (GROUP, CTOK)
WIDE = GROUP * CTOK
DQ = (HD, WIDE)
HEADS = 4
CHUNK = 256
F32 = jnp.float32
BF16 = jnp.bfloat16


def place(x, y, core):
    return ((x * 2 + y % 2) * CORES + core) * 2 + y // 2


def send(block, dx=0, dy=0, dc=0):
    route = []
    for x in range(X):
        for y in range(Y):
            for core in range(CORES):
                there = place((x + dx) % X, (y + dy) % Y, core ^ dc)
                route.append((place(x, y, core), there))
    return lax.ppermute(block, ("blk", "req"), route)


def part(ref, n, width):
    return ref[:, n * width : (n + 1) * width]


def dot(a, b, contract):
    return lax.dot_general(a, b, (contract, ((), ())), preferred_element_type=F32)


def largest_norm(rows):
    wide = rows.astype(F32)
    return jnp.max(jnp.sum(wide * wide, axis=1, keepdims=True))


def within(query_norm, key_norm):
    return query_norm * key_norm * (EXP2_SCALE * EXP2_SCALE) <= PLAIN * PLAIN


def put(e, n, parts, first=0):
    low = e.astype(BF16)
    start = 0
    for ref in parts:
        begin, end = max(start, first), min(start + ref.shape[0], first + e.shape[0])
        if begin < end:
            ref[begin - start : end - start, n * CTOK : (n + 1) * CTOK] = low[begin - first : end - first]
        start += ref.shape[0]


def plain_tile(keys, q_ref, visible, l_ref, parts, mt_ref, tile):
    mt_ref[tile] = jnp.zeros(STAT, F32)
    keys = jnp.concatenate([keys, keys], axis=1)
    for n in range(GROUP):
        total = l_ref[n : n + 1, :]
        for first in range(0, keys.shape[0], CHUNK):
            e = jnp.exp2(dot(keys[first : first + CHUNK], q_ref[n * CTOK : (n + 1) * CTOK, :], ((1,), (1,))))
            if visible is not None:
                e = jnp.where(visible, e, 0.0)
            total = total + jnp.sum(e, axis=0, keepdims=True)
            put(e, n, parts, first)
        l_ref[n : n + 1, :] = total


def general_tile(keys, q_ref, visible, m_ref, l_ref, parts, mt_ref, tile):
    keys = jnp.concatenate([keys, keys], axis=1)
    for n in range(GROUP):
        scores = dot(keys, q_ref[n * CTOK : (n + 1) * CTOK, :], ((1,), (1,)))
        if visible is not None:
            scores = jnp.where(visible, scores, -jnp.inf)
        m_old = m_ref[n : n + 1, :]
        m_new = jnp.maximum(m_old, jnp.max(scores, axis=0, keepdims=True))
        e = jnp.exp2(scores - m_new)
        total = jnp.sum(e, axis=0, keepdims=True)
        l_ref[n : n + 1, :] = l_ref[n : n + 1, :] * jnp.exp2(m_old - m_new) + total
        m_ref[n : n + 1, :] = m_new
        mt_ref[tile, n : n + 1, :] = m_new
        put(e, n, parts)


def y_place():
    y_high = lax.axis_index("req")
    y_low = lax.rem(lax.div(lax.axis_index("blk"), CORES), 2)
    return y_high, jnp.where(y_low == 0, y_high, 1 - y_high)


def half_rows(at):
    return pl.ds(pl.multiple_of(at * HALF, HALF), HALF)


def fetch(pairs, sems):
    copies = [pltpu.make_async_copy(far, near, sems.at[at]) for at, (far, near) in enumerate(pairs)]
    for copy in copies:
        copy.start()
    for copy in copies:
        copy.wait()


def pack_kernel(k_hbm, v_hbm, kv_ref, turned_ref, sems):
    y_high, _ = y_place()
    pairs = []
    for far, columns in ((k_hbm, slice(0, HD)), (v_hbm, slice(HD, 2 * HD))):
        pairs.append((far, kv_ref.at[:, columns]))
        pairs.append((far.at[half_rows(1 - y_high), :], turned_ref.at[:HALF, columns]))
        pairs.append((far.at[half_rows(y_high), :], turned_ref.at[HALF:, columns]))
    fetch(pairs, sems)


def self_scores_kernel(
    q_hbm, k_hbm, out_hbm, do_hbm, step_hbm, *refs
):
    e_ref, mt_ref, m_ref, l_ref, q_out, do_out, norm_ref, q_ref, k_ref, out_ref, do_ref, step_ref, sems = refs
    fetch(
        [(k_hbm, k_ref), (step_hbm, step_ref), (q_hbm, q_ref), (do_hbm, do_ref), (out_hbm, out_ref)], sems
    )
    keys = k_ref[...]
    step = jnp.broadcast_to(step_ref[...].astype(F32), (CTOK, CTOK))
    visible = step.T <= step
    lane = lax.broadcasted_iota(jnp.int32, (CTOK, HD), 1)
    norm = None
    for n in range(GROUP):
        do_n = part(do_ref, n, HD)
        left = jnp.sum(do_n.astype(F32) * part(out_ref, n, HD).astype(F32), axis=1, keepdims=True)
        terms = jnp.zeros((CTOK, HD), F32)
        for place_at in range(3):
            term = left.astype(BF16).astype(F32)
            terms = jnp.where(lane == place_at, -term, terms)
            left = left - term
        do_out[n * CTOK : (n + 1) * CTOK, :HD] = do_n
        do_out[n * CTOK : (n + 1) * CTOK, HD:] = terms.astype(BF16)
        scaled = part(q_ref, n, HD).astype(F32) * EXP2_SCALE
        high = scaled.astype(BF16)
        q_out[n * CTOK : (n + 1) * CTOK, :HD] = high
        q_out[n * CTOK : (n + 1) * CTOK, HD:] = (scaled - high.astype(F32)).astype(BF16)
        rows = largest_norm(part(q_ref, n, HD))
        norm = rows if norm is None else jnp.maximum(norm, rows)
    norm_ref[0] = norm
    l_ref[...] = jnp.zeros(STAT, F32)
    m_ref[...] = jnp.zeros(STAT, F32)
    plain_tile(keys, q_out, visible, l_ref, [e_ref], mt_ref, 0)

    @pl.when(jnp.logical_not(within(norm, largest_norm(keys))))
    def _():
        l_ref[...] = jnp.zeros(STAT, F32)
        m_ref[...] = jnp.full(STAT, -1e30, F32)
        general_tile(keys, q_out, visible, m_ref, l_ref, [e_ref], mt_ref, 0)


def prompt_scores_kernel(last, pieces, *refs):
    norm_ref, q_ref, kv_ref, m_in, l_in, *refs = refs
    if last:
        do_ref, *refs = refs
    e_refs, refs = refs[: 2 * pieces], refs[2 * pieces :]
    mt_ref, m_ref, l_ref, *refs = refs
    m_ref[...] = m_in[...]
    l_ref[...] = l_in[...]
    for tile in range(2):
        keys = kv_ref[tile * TILE : (tile + 1) * TILE, :HD]
        parts = e_refs[tile * pieces : (tile + 1) * pieces]
        l_old = l_ref[...]
        plain = within(norm_ref[0], largest_norm(keys)) & (jnp.max(jnp.abs(m_ref[...])) == 0.0)
        plain_tile(keys, q_ref, None, l_ref, parts, mt_ref, tile)

        @pl.when(jnp.logical_not(plain))
        def _():
            l_ref[...] = l_old
            general_tile(keys, q_ref, None, m_ref, l_ref, parts, mt_ref, tile)

    if last:
        wq_ref, wdo_ref = refs
        for n in range(GROUP):
            weight = jnp.broadcast_to(1.0 / l_ref[n : n + 1, :], (HD, CTOK)).T
            heads = slice(n * CTOK, (n + 1) * CTOK)
            q_n = (q_ref[heads, :HD].astype(F32) + q_ref[heads, HD:].astype(F32)) * (1.0 / EXP2_SCALE)
            wq_ref[heads, :] = (q_n * weight).astype(BF16)
            wdo_ref[heads, :] = (do_ref[heads, :HD].astype(F32) * weight).astype(BF16)


def stack(parts):
    return parts[0] if len(parts) == 1 else jnp.concatenate(parts, axis=0)


def back_rows(pieces, do_ref, wq_ref, wdo_ref, m_ref, dq_ref, changed):
    keys = stack([keys for keys, _, _, _ in pieces])
    values = stack([values for _, values, _, _ in pieces])
    lane = lax.broadcasted_iota(jnp.int32, values.shape, 1)
    ones = jnp.where(lane < 3, 1.0, 0.0).astype(BF16)
    values = jnp.concatenate([values, ones], axis=1)
    keys_t = keys.T
    grad_keys = grad_values = None
    for n in range(0, GROUP, HEADS):
        columns = slice(n * CTOK, (n + HEADS) * CTOK)
        parts = []
        for _, _, e_ref, top in pieces:
            e = e_ref[:, columns]
            if changed:
                log_change = [top[h : h + 1, :] - m_ref[h : h + 1, :] for h in range(n, n + HEADS)]
                e = (e.astype(F32) * jnp.exp2(jnp.concatenate(log_change, axis=1))).astype(BF16)
            parts.append(e)
        e = stack(parts)
        grad_prob = dot(values, do_ref[columns, :], ((1,), (1,)))
        part_value = dot(e, wdo_ref[columns, :], ((1,), (0,)))
        grad_score = e * grad_prob.astype(BF16)
        part_key = dot(grad_score, wq_ref[columns, :], ((1,), (0,)))
        dq_ref[:, columns] += dot(keys_t, grad_score, ((1,), (0,)))
        grad_keys = part_key if n == 0 else grad_keys + part_key
        grad_values = part_value if n == 0 else grad_values + part_value
    return grad_keys * SCALE, grad_values


def either_way(m_ref, mt_refs, work):
    tops = [mt_ref[t] for mt_ref in mt_refs for t in range(mt_ref.shape[0])]
    change = functools.reduce(jnp.maximum, [jnp.abs(top - m_ref[...]) for top in tops])
    plain = jnp.max(change) == 0.0
    pl.when(plain)(lambda: work(False))
    pl.when(jnp.logical_not(plain))(lambda: work(True))


def prompt_back_kernel(first, last, tiles, sources, blocks, unread, *refs):
    do_ref, wq_ref, wdo_ref, m_ref, *refs = refs
    if not first:
        dq_in, *refs = refs
    if last:
        l_ref, *refs = refs
    kv_refs, refs = refs[:sources], refs[sources:]
    mt_refs, refs = refs[:sources], refs[sources:]
    e_refs, refs = refs[:blocks], refs[blocks + unread :]
    *out_refs, dq_ref = refs
    if last:
        *out_refs, query_ref = out_refs
    dq_ref[...] = jnp.zeros_like(dq_ref) if first else dq_in[...]

    def work(changed):
        for members, outs in tiles:
            pieces = []
            for source, row, block in members:
                e_ref = e_refs[block]
                rows = slice(row, row + e_ref.shape[0])
                kv_ref = kv_refs[source]
                pieces.append((kv_ref[rows, :HD], kv_ref[rows, HD:], e_ref, mt_refs[source][row // TILE]))
            grad_keys, grad_values = back_rows(pieces, do_ref, wq_ref, wdo_ref, m_ref, dq_ref, changed)
            start = 0
            for at in outs:
                ref = out_refs[at]
                rows = slice(start, start + ref.shape[0])
                ref[:, :HD] = grad_keys[rows].astype(ref.dtype)
                ref[:, HD:] = grad_values[rows].astype(ref.dtype)
                start += ref.shape[0]

    either_way(m_ref, mt_refs, work)
    if last:
        for n in range(GROUP):
            weight = SCALE / l_ref[n : n + 1, :]
            query_ref[:, n * HD : (n + 1) * HD] = (part(dq_ref, n, CTOK) * weight).T.astype(BF16)


def self_back_kernel(do_ref, wq_ref, wdo_ref, m_ref, dq_in, k_ref, v_ref, e_ref, mt_ref, dk_ref, dv_ref, dq_ref):
    dq_ref[...] = dq_in[...]

    def work(changed):
        pieces = [(k_ref[...], v_ref[...], e_ref, mt_ref[0])]
        grad_keys, grad_values = back_rows(pieces, do_ref, wq_ref, wdo_ref, m_ref, dq_ref, changed)
        dk_ref[...] = grad_keys.astype(BF16)
        dv_ref[...] = grad_values.astype(BF16)

    either_way(m_ref, [mt_ref], work)


def combine_kernel(mine_ref, pair_ref, left_ref, right_ref, across_ref, above_ref, below_ref, own_ref):
    y_high, up = y_place()

    def arrived(at):
        rows = half_rows(at)
        return left_ref[rows, :].astype(F32) + right_ref[rows, :].astype(F32)

    def leaving(at, beside):
        rows = half_rows(at)
        return (mine_ref[rows, :] + pair_ref[rows, :].astype(F32) + arrived(beside)).astype(BF16)

    across_ref[...] = leaving(0, 1 - y_high)
    above_ref[...] = leaving(1 + up, 2 + up)
    below_ref[...] = leaving(2 - up, 3 - up)
    own_ref[...] = arrived(y_high)


def finish_kernel(own_ref, mine_ref, pair_ref, across_ref, above_ref, below_ref, dk_ref, dv_ref):
    total = own_ref[...] + mine_ref[...]
    for ref in (pair_ref, across_ref, above_ref, below_ref):
        total = total + ref[...].astype(F32)
    dk_ref[...] = total[:, :HD].astype(BF16)
    dv_ref[...] = total[:, HD:].astype(BF16)


def params(mib):
    return pltpu.CompilerParams(vmem_limit_bytes=mib * 1024 * 1024)


VMEM = pl.BlockSpec(memory_space=pltpu.VMEM)
HBM = pl.BlockSpec(memory_space=pltpu.HBM)
SMEM = pl.BlockSpec(memory_space=pltpu.SMEM)
UNREAD = pl.BlockSpec(memory_space=pl.ANY)


def whole(dims):
    return pl.BlockSpec(dims, lambda *_: (0,) * len(dims))


def cost(rows, matmuls, exps, stored):
    return pl.CostEstimate(
        flops=2 * rows * WIDE * HD * matmuls,
        bytes_accessed=rows * WIDE * 2 * stored,
        transcendentals=rows * WIDE * exps,
    )


def shape(dims, dtype=F32):
    return jax.ShapeDtypeStruct(dims, dtype)


def pack(keys, values):
    return pl.pallas_call(
        pack_kernel,
        in_specs=[HBM] * 2,
        out_specs=(VMEM,) * 2,
        out_shape=(shape((ROWS, 2 * HD), BF16),) * 2,
        scratch_shapes=[pltpu.SemaphoreType.DMA((6,))],
        compiler_params=params(60),
        name="pack",
    )(keys, values)


def self_scores(query, key_comp, out, d_out, steps):
    return pl.pallas_call(
        self_scores_kernel,
        in_specs=[HBM] * 5,
        out_specs=(VMEM,) * 6 + (SMEM,),
        scratch_shapes=[
            pltpu.VMEM((CTOK, GROUP * HD), BF16),
            pltpu.VMEM((CTOK, HD), BF16),
            pltpu.VMEM((CTOK, GROUP * HD), BF16),
            pltpu.VMEM((CTOK, GROUP * HD), BF16),
            pltpu.VMEM((1, CTOK), jnp.int32),
            pltpu.SemaphoreType.DMA((5,)),
        ],
        out_shape=(
            shape((CTOK, WIDE), BF16),
            shape((1,) + STAT),
            shape(STAT),
            shape(STAT),
            shape((WIDE, 2 * HD), BF16),
            shape((WIDE, 2 * HD), BF16),
            shape((1,)),
        ),
        compiler_params=params(57),
        cost_estimate=cost(CTOK, 1, 1, 1),
        name="self_scores",
    )(query, key_comp, out, d_out, steps)


def prompt_scores(norm, query, kv, m, l, split=(ROWS, ROWS), d_out=None):
    last = d_out is not None
    blocks = 2 * len(split)
    results = pl.pallas_call(
        functools.partial(prompt_scores_kernel, last, len(split)),
        in_specs=[SMEM] + [VMEM] * (5 if last else 4),
        out_specs=(VMEM,) * (blocks + (5 if last else 3)),
        out_shape=tuple(shape((rows, WIDE), BF16) for rows in split) * 2
        + (shape((2,) + STAT), shape(STAT), shape(STAT))
        + ((shape((WIDE, HD), BF16),) * 2 if last else ()),
        compiler_params=params(16),
        cost_estimate=cost(2 * TILE, 1, 1, 1),
        name="prompt_scores",
    )(norm, query, kv, m, l, *([d_out] if last else []))
    return results[:blocks], *results[blocks:]


def prompt_back(shared, dq, sources, tiles, es, outs, after=(), matmuls=4, l=None):
    kvs, mts = zip(*sources)
    first, last = dq is None, l is not None
    operands = [*shared] + ([] if first else [dq]) + ([l] if last else []) + [*kvs, *mts, *es]
    out_shape = tuple(shape((rows, 2 * HD), dtype) for rows, dtype in outs)
    out_shape += (shape((CTOK, GROUP * HD), BF16) if last else shape(DQ),)
    return pl.pallas_call(
        functools.partial(prompt_back_kernel, first, last, tiles, len(kvs), len(es), len(after)),
        in_specs=[VMEM] * len(operands) + [UNREAD] * len(after),
        out_specs=(VMEM,) * len(out_shape),
        out_shape=out_shape,
        scratch_shapes=[pltpu.VMEM(DQ, F32)] if last else [],
        compiler_params=params(20),
        cost_estimate=cost(sum(e.shape[0] for e in es), matmuls, 0, min(matmuls, 1)),
        name="prompt_back",
    )(*operands, *after)


def self_back(shared, dq, key_comp, value_comp, e, mt):
    return pl.pallas_call(
        self_back_kernel,
        in_specs=[VMEM] * 9,
        out_specs=(VMEM,) * 3,
        out_shape=(shape((CTOK, HD), BF16), shape((CTOK, HD), BF16), shape(DQ)),
        compiler_params=params(20),
        cost_estimate=cost(CTOK, 4, 0, 1),
        name="self_back",
    )(*shared, dq, key_comp, value_comp, e, mt)


def combine(*arrays):
    return pl.pallas_call(
        combine_kernel,
        in_specs=[VMEM] * 4,
        out_specs=(VMEM,) * 4,
        out_shape=(shape((HALF, 2 * HD), BF16),) * 3 + (shape((HALF, 2 * HD)),),
        compiler_params=params(6),
        name="combine",
    )(*arrays)


def finish(*arrays):
    return pl.pallas_call(
        finish_kernel,
        in_specs=[VMEM] * 6,
        out_specs=(VMEM,) * 2,
        out_shape=(shape((HALF, HD), BF16),) * 2,
        compiler_params=params(6),
        name="finish",
    )(*arrays)


def behind(result, *blocks):
    return lax.optimization_barrier(blocks + (result,))[:-1]


def shards(query, key_comp, value_comp, key_prompt, value_prompt, out, d_out, steps):
    here, turned = pack(key_prompt, value_prompt)

    here_y = send(here, dy=1)
    left = send(here, dx=1)
    right = send(here, dx=-1)
    e_self, mt_self, m, l, query, d_out, norm = self_scores(query, key_comp, out, d_out, steps.reshape(1, CTOK))
    here_y, left, right = behind(m, here_y, left, right)
    near = stack([turned, here_y])
    beside = stack([left, right])
    near = stack([near, send(near, dc=1)])
    beside_pair = send(beside, dc=1)
    far = send(left, dx=1)
    left_y = send(left, dy=1)
    right_y = send(right, dy=-1)
    e_near, mt_near, m, l = prompt_scores(norm, query, near, m, l, split=(HALF, HALF, ROWS))
    far, beside_pair = behind(m, far, beside_pair)
    beside = stack([beside, beside_pair])
    far_y = send(far, dy=-1)
    e_beside, mt_beside, m, l = prompt_scores(norm, query, beside, m, l)
    left_y, right_y, far_y = behind(m, left_y, right_y, far_y)
    corners = stack([left_y, right_y])
    corners = stack([corners, send(corners, dc=1)])
    opposite = stack([far, far_y])
    opposite_pair = send(opposite, dc=1)
    e_corners, mt_corners, m, l = prompt_scores(norm, query, corners, m, l)
    (opposite_pair,) = behind(m, opposite_pair)
    opposite = stack([opposite, opposite_pair])
    e_far, mt_far, m, l, wq, wdo = prompt_scores(norm, query, opposite, m, l, d_out=d_out)

    shared = d_out, wq, wdo, m
    add = lambda *parts: sum(rows.astype(F32) for rows in parts)
    far_source = [(opposite, mt_far)]
    theirs, dq = prompt_back(
        shared, None, far_source, [([(0, TILE, 0), (0, TILE + ROWS, 1)], [0])], e_far[2:], [(TILE, BF16)]
    )
    pair_far = send(theirs, dc=1)
    mine_far, dq = prompt_back(shared, dq, far_source, [([(0, 0, 0), (0, ROWS, 1)], [0])], e_far[:2], [(TILE, F32)])
    (pair_far,) = behind(mine_far, pair_far)
    total = add(mine_far, pair_far).astype(BF16)
    far_right = send(total[:ROWS], dx=1)
    far_left = send(total[ROWS:], dx=-1)

    sources = [(beside, mt_beside), (corners, mt_corners)]
    outs = [(TILE, F32), (TILE, BF16)]

    def side(at, dq, after, matmuls):
        row = at * ROWS
        tiles = [
            ([(0, TILE + row, 1), (1, TILE + row, 3)], [1]),
            ([(0, row, 0), (1, row, 2)], [0]),
        ]
        es = [e_beside[at], e_beside[2 + at], e_corners[at], e_corners[2 + at]]
        return prompt_back(shared, dq, sources, tiles, es, outs, after, matmuls)

    mine_left, theirs, dq = side(0, dq, (), 4)
    pair_left = send(theirs, dc=1)
    mine_right, theirs, dq = side(1, dq, (far_left, far_right), 4)
    pair_right = send(theirs, dc=1)
    (pair_left,) = behind(theirs, pair_left)
    total = stack([add(mine_left[:ROWS], pair_left[:ROWS]), add(mine_left[ROWS:], pair_left[ROWS:], far_left)])
    from_right = send(total.astype(BF16), dx=-1)
    total = stack([add(mine_right[:ROWS], pair_right[:ROWS], far_right), add(mine_right[ROWS:], pair_right[ROWS:])])
    from_left = send(total.astype(BF16), dx=1)

    near_source = [(near, mt_near)]
    tiles = [([(0, TILE, 1), (0, TILE + ROWS, 3)], [1]), ([(0, 0, 0), (0, ROWS, 2)], [0])]
    es = [e_near[0], e_near[3], e_near[2], e_near[5]]
    outs = [(HALF + ROWS, F32), (HALF + ROWS, BF16)]
    mine, theirs, dq = prompt_back(shared, dq, near_source, tiles, es, outs, (pair_right,))
    pair = send(theirs, dc=1)
    grad_key_comp, grad_value_comp, dq = self_back(shared, dq, key_comp, value_comp, e_self, mt_self)
    pair, from_left, from_right = behind(grad_key_comp, pair, from_left, from_right)
    across, above, below, own = combine(mine, pair, from_left, from_right)
    across = send(across, dy=2)
    above = send(above, dy=1)
    below = send(below, dy=-1)
    tiles = [([(0, HALF, 0), (0, TILE + HALF, 1)], [0, 1])]
    es = [e_near[1], e_near[4]]
    outs = [(HALF, F32), (HALF, BF16)]
    mine, theirs, grad_query = prompt_back(shared, dq, near_source, tiles, es, outs, (own,), l=l)
    pair = send(theirs, dc=1)
    across, above, below = behind(mine, across, above, below)
    grad_key_prompt, grad_value_prompt = finish(own, mine, pair, across, above, below)
    return (grad_query, grad_key_comp, grad_value_comp, grad_key_prompt, grad_value_prompt)


def solution(mesh):
    rows = P(("blk", "req"), "head")
    return jax.shard_map(
        shards,
        mesh=mesh,
        in_specs=(rows, rows, rows, P("blk", "head"), P("blk", "head"), rows, rows, P(("blk", "req"))),
        out_specs=(rows,) * 5,
        check_vma=False,
    )
```

```python
import functools

import jax
import jax.numpy as jnp
from jax import lax
from jax.experimental import pallas as pl
from jax.experimental.pallas import tpu as pltpu
from jax.sharding import PartitionSpec as P

HD = 128
GROUP = 8
CTOK = 256
ROWS = 384
TILE = 2 * ROWS
HALF = ROWS // 2
X, Y, CORES = 4, 4, 2
SCALE = HD ** (-0.5)
EXP2_SCALE = SCALE * 1.4426950408889634
PLAIN = 60.0
STAT = (GROUP, CTOK)
WIDE = GROUP * CTOK
DQ = (HD, WIDE)
HEADS = 4
CHUNK = 256
F32 = jnp.float32
BF16 = jnp.bfloat16


def place(x, y, core):
    return ((x * 2 + y % 2) * CORES + core) * 2 + y // 2


def send(block, dx=0, dy=0, dc=0):
    route = []
    for x in range(X):
        for y in range(Y):
            for core in range(CORES):
                there = place((x + dx) % X, (y + dy) % Y, core ^ dc)
                route.append((place(x, y, core), there))
    return lax.ppermute(block, ("blk", "req"), route)


def part(ref, n, width):
    return ref[:, n * width : (n + 1) * width]


def dot(a, b, contract):
    return lax.dot_general(a, b, (contract, ((), ())), preferred_element_type=F32)


def largest_norm(rows):
    wide = rows.astype(F32)
    return jnp.max(jnp.sum(wide * wide, axis=1, keepdims=True))


def within(query_norm, key_norm):
    return query_norm * key_norm * (EXP2_SCALE * EXP2_SCALE) <= PLAIN * PLAIN


def put(e, n, parts, first=0):
    low = e.astype(BF16)
    start = 0
    for ref in parts:
        begin, end = max(start, first), min(start + ref.shape[0], first + e.shape[0])
        if begin < end:
            ref[begin - start : end - start, n * CTOK : (n + 1) * CTOK] = low[begin - first : end - first]
        start += ref.shape[0]


def plain_tile(keys, q_ref, visible, l_ref, parts, mt_ref, tile):
    mt_ref[tile] = jnp.zeros(STAT, F32)
    keys = jnp.concatenate([keys, keys], axis=1)
    for n in range(GROUP):
        total = l_ref[n : n + 1, :]
        for first in range(0, keys.shape[0], CHUNK):
            e = jnp.exp2(dot(keys[first : first + CHUNK], q_ref[n * CTOK : (n + 1) * CTOK, :], ((1,), (1,))))
            if visible is not None:
                e = jnp.where(visible, e, 0.0)
            total = total + jnp.sum(e, axis=0, keepdims=True)
            put(e, n, parts, first)
        l_ref[n : n + 1, :] = total


def general_tile(keys, q_ref, visible, m_ref, l_ref, parts, mt_ref, tile):
    keys = jnp.concatenate([keys, keys], axis=1)
    for n in range(GROUP):
        scores = dot(keys, q_ref[n * CTOK : (n + 1) * CTOK, :], ((1,), (1,)))
        if visible is not None:
            scores = jnp.where(visible, scores, -jnp.inf)
        m_old = m_ref[n : n + 1, :]
        m_new = jnp.maximum(m_old, jnp.max(scores, axis=0, keepdims=True))
        e = jnp.exp2(scores - m_new)
        total = jnp.sum(e, axis=0, keepdims=True)
        l_ref[n : n + 1, :] = l_ref[n : n + 1, :] * jnp.exp2(m_old - m_new) + total
        m_ref[n : n + 1, :] = m_new
        mt_ref[tile, n : n + 1, :] = m_new
        put(e, n, parts)


def y_place():
    y_high = lax.axis_index("req")
    y_low = lax.rem(lax.div(lax.axis_index("blk"), CORES), 2)
    return y_high, jnp.where(y_low == 0, y_high, 1 - y_high)


def half_rows(at):
    return pl.ds(pl.multiple_of(at * HALF, HALF), HALF)


def fetch(pairs, sems):
    copies = [pltpu.make_async_copy(far, near, sems.at[at]) for at, (far, near) in enumerate(pairs)]
    for copy in copies:
        copy.start()
    for copy in copies:
        copy.wait()


def pack_kernel(k_hbm, v_hbm, kv_ref, turned_ref, sems):
    y_high, _ = y_place()
    pairs = []
    for far, columns in ((k_hbm, slice(0, HD)), (v_hbm, slice(HD, 2 * HD))):
        pairs.append((far, kv_ref.at[:, columns]))
        pairs.append((far.at[half_rows(1 - y_high), :], turned_ref.at[:HALF, columns]))
        pairs.append((far.at[half_rows(y_high), :], turned_ref.at[HALF:, columns]))
    fetch(pairs, sems)


def self_scores_kernel(
    q_hbm, k_hbm, out_hbm, do_hbm, step_hbm, *refs
):
    e_ref, mt_ref, m_ref, l_ref, q_out, do_out, norm_ref, q_ref, k_ref, out_ref, do_ref, step_ref, sems = refs
    fetch(
        [(k_hbm, k_ref), (step_hbm, step_ref), (q_hbm, q_ref), (do_hbm, do_ref), (out_hbm, out_ref)], sems
    )
    keys = k_ref[...]
    step = jnp.broadcast_to(step_ref[...].astype(F32), (CTOK, CTOK))
    visible = step.T <= step
    lane = lax.broadcasted_iota(jnp.int32, (CTOK, HD), 1)
    norm = None
    for n in range(GROUP):
        do_n = part(do_ref, n, HD)
        left = jnp.sum(do_n.astype(F32) * part(out_ref, n, HD).astype(F32), axis=1, keepdims=True)
        terms = jnp.zeros((CTOK, HD), F32)
        for place_at in range(3):
            term = left.astype(BF16).astype(F32)
            terms = jnp.where(lane == place_at, -term, terms)
            left = left - term
        do_out[n * CTOK : (n + 1) * CTOK, :HD] = do_n
        do_out[n * CTOK : (n + 1) * CTOK, HD:] = terms.astype(BF16)
        scaled = part(q_ref, n, HD).astype(F32) * EXP2_SCALE
        high = scaled.astype(BF16)
        q_out[n * CTOK : (n + 1) * CTOK, :HD] = high
        q_out[n * CTOK : (n + 1) * CTOK, HD:] = (scaled - high.astype(F32)).astype(BF16)
        rows = largest_norm(part(q_ref, n, HD))
        norm = rows if norm is None else jnp.maximum(norm, rows)
    norm_ref[0] = norm
    l_ref[...] = jnp.zeros(STAT, F32)
    m_ref[...] = jnp.zeros(STAT, F32)
    plain_tile(keys, q_out, visible, l_ref, [e_ref], mt_ref, 0)

    @pl.when(jnp.logical_not(within(norm, largest_norm(keys))))
    def _():
        l_ref[...] = jnp.zeros(STAT, F32)
        m_ref[...] = jnp.full(STAT, -1e30, F32)
        general_tile(keys, q_out, visible, m_ref, l_ref, [e_ref], mt_ref, 0)


def prompt_scores_kernel(last, pieces, row, unread, *refs):
    norm_ref, q_ref, own_ref, pair_ref, m_in, l_in, *refs = refs
    if last:
        do_ref, *refs = refs
    refs = refs[unread:]
    e_refs, refs = refs[: 2 * pieces], refs[2 * pieces :]
    mt_ref, m_ref, l_ref, *refs = refs
    m_ref[...] = m_in[...]
    l_ref[...] = l_in[...]
    for tile, kv_ref in enumerate((own_ref, pair_ref)):
        keys = kv_ref[row : row + TILE, :HD]
        parts = e_refs[tile * pieces : (tile + 1) * pieces]
        l_old = l_ref[...]
        plain = within(norm_ref[0], largest_norm(keys)) & (jnp.max(jnp.abs(m_ref[...])) == 0.0)
        plain_tile(keys, q_ref, None, l_ref, parts, mt_ref, tile)

        @pl.when(jnp.logical_not(plain))
        def _():
            l_ref[...] = l_old
            general_tile(keys, q_ref, None, m_ref, l_ref, parts, mt_ref, tile)

    if last:
        wq_ref, wdo_ref = refs
        for n in range(GROUP):
            weight = jnp.broadcast_to(1.0 / l_ref[n : n + 1, :], (HD, CTOK)).T
            heads = slice(n * CTOK, (n + 1) * CTOK)
            q_n = (q_ref[heads, :HD].astype(F32) + q_ref[heads, HD:].astype(F32)) * (1.0 / EXP2_SCALE)
            wq_ref[heads, :] = (q_n * weight).astype(BF16)
            wdo_ref[heads, :] = (do_ref[heads, :HD].astype(F32) * weight).astype(BF16)


def stack(parts):
    return parts[0] if len(parts) == 1 else jnp.concatenate(parts, axis=0)


def back_rows(pieces, do_ref, wq_ref, wdo_ref, m_ref, dq_ref, changed):
    keys = stack([keys for keys, _, _, _ in pieces])
    values = stack([values for _, values, _, _ in pieces])
    lane = lax.broadcasted_iota(jnp.int32, values.shape, 1)
    ones = jnp.where(lane < 3, 1.0, 0.0).astype(BF16)
    values = jnp.concatenate([values, ones], axis=1)
    keys_t = keys.T
    grad_keys = grad_values = None
    for n in range(0, GROUP, HEADS):
        columns = slice(n * CTOK, (n + HEADS) * CTOK)
        parts = []
        for _, _, e_ref, top in pieces:
            e = e_ref[:, columns]
            if changed:
                log_change = [top[h : h + 1, :] - m_ref[h : h + 1, :] for h in range(n, n + HEADS)]
                e = (e.astype(F32) * jnp.exp2(jnp.concatenate(log_change, axis=1))).astype(BF16)
            parts.append(e)
        e = stack(parts)
        grad_prob = dot(values, do_ref[columns, :], ((1,), (1,)))
        part_value = dot(e, wdo_ref[columns, :], ((1,), (0,)))
        grad_score = e * grad_prob.astype(BF16)
        part_key = dot(grad_score, wq_ref[columns, :], ((1,), (0,)))
        dq_ref[:, columns] += dot(keys_t, grad_score, ((1,), (0,)))
        grad_keys = part_key if n == 0 else grad_keys + part_key
        grad_values = part_value if n == 0 else grad_values + part_value
    return grad_keys * SCALE, grad_values


def either_way(m_ref, mt_refs, work):
    tops = [mt_ref[t] for mt_ref in mt_refs for t in range(mt_ref.shape[0])]
    change = functools.reduce(jnp.maximum, [jnp.abs(top - m_ref[...]) for top in tops])
    plain = jnp.max(change) == 0.0
    pl.when(plain)(lambda: work(False))
    pl.when(jnp.logical_not(plain))(lambda: work(True))


def prompt_back_kernel(first, last, tiles, sources, tops, blocks, unread, *refs):
    do_ref, wq_ref, wdo_ref, m_ref, *refs = refs
    if not first:
        dq_in, *refs = refs
    if last:
        l_ref, *refs = refs
    kv_refs, refs = refs[:sources], refs[sources:]
    mt_refs, refs = refs[:tops], refs[tops:]
    e_refs, refs = refs[:blocks], refs[blocks + unread :]
    *out_refs, dq_ref = refs
    if last:
        *out_refs, query_ref = out_refs
    dq_ref[...] = jnp.zeros_like(dq_ref) if first else dq_in[...]

    def work(changed):
        for members, outs in tiles:
            pieces = []
            for source, row, block, top, tile in members:
                e_ref = e_refs[block]
                rows = slice(row, row + e_ref.shape[0])
                kv_ref = kv_refs[source]
                pieces.append((kv_ref[rows, :HD], kv_ref[rows, HD:], e_ref, mt_refs[top][tile]))
            grad_keys, grad_values = back_rows(pieces, do_ref, wq_ref, wdo_ref, m_ref, dq_ref, changed)
            start = 0
            for at in outs:
                ref = out_refs[at]
                rows = slice(start, start + ref.shape[0])
                ref[:, :HD] = grad_keys[rows].astype(ref.dtype)
                ref[:, HD:] = grad_values[rows].astype(ref.dtype)
                start += ref.shape[0]

    either_way(m_ref, mt_refs, work)
    if last:
        for n in range(GROUP):
            weight = SCALE / l_ref[n : n + 1, :]
            query_ref[:, n * HD : (n + 1) * HD] = (part(dq_ref, n, CTOK) * weight).T.astype(BF16)


def self_back_kernel(do_ref, wq_ref, wdo_ref, m_ref, dq_in, k_ref, v_ref, e_ref, mt_ref, dk_ref, dv_ref, dq_ref):
    dq_ref[...] = dq_in[...]

    def work(changed):
        pieces = [(k_ref[...], v_ref[...], e_ref, mt_ref[0])]
        grad_keys, grad_values = back_rows(pieces, do_ref, wq_ref, wdo_ref, m_ref, dq_ref, changed)
        dk_ref[...] = grad_keys.astype(BF16)
        dv_ref[...] = grad_values.astype(BF16)

    either_way(m_ref, [mt_ref], work)


def combine_kernel(mine_ref, pair_ref, left_ref, right_ref, across_ref, above_ref, below_ref, own_ref):
    y_high, up = y_place()

    def arrived(at):
        rows = half_rows(at)
        return left_ref[rows, :].astype(F32) + right_ref[rows, :].astype(F32)

    def leaving(at, beside):
        rows = half_rows(at)
        return (mine_ref[rows, :] + pair_ref[rows, :].astype(F32) + arrived(beside)).astype(BF16)

    across_ref[...] = leaving(0, 1 - y_high)
    above_ref[...] = leaving(1 + up, 2 + up)
    below_ref[...] = leaving(2 - up, 3 - up)
    own_ref[...] = arrived(y_high)


def finish_kernel(own_ref, mine_ref, pair_ref, across_ref, above_ref, below_ref, dk_ref, dv_ref):
    total = own_ref[...] + mine_ref[...]
    for ref in (pair_ref, across_ref, above_ref, below_ref):
        total = total + ref[...].astype(F32)
    dk_ref[...] = total[:, :HD].astype(BF16)
    dv_ref[...] = total[:, HD:].astype(BF16)


def params(mib):
    return pltpu.CompilerParams(vmem_limit_bytes=mib * 1024 * 1024)


VMEM = pl.BlockSpec(memory_space=pltpu.VMEM)
HBM = pl.BlockSpec(memory_space=pltpu.HBM)
SMEM = pl.BlockSpec(memory_space=pltpu.SMEM)
UNREAD = pl.BlockSpec(memory_space=pl.ANY)


def whole(dims):
    return pl.BlockSpec(dims, lambda *_: (0,) * len(dims))


def cost(rows, matmuls, exps, stored):
    return pl.CostEstimate(
        flops=2 * rows * WIDE * HD * matmuls,
        bytes_accessed=rows * WIDE * 2 * stored,
        transcendentals=rows * WIDE * exps,
    )


def shape(dims, dtype=F32):
    return jax.ShapeDtypeStruct(dims, dtype)


def pack(keys, values):
    return pl.pallas_call(
        pack_kernel,
        in_specs=[HBM] * 2,
        out_specs=(VMEM,) * 2,
        out_shape=(shape((ROWS, 2 * HD), BF16),) * 2,
        scratch_shapes=[pltpu.SemaphoreType.DMA((6,))],
        compiler_params=params(60),
        name="pack",
    )(keys, values)


def self_scores(query, key_comp, out, d_out, steps):
    return pl.pallas_call(
        self_scores_kernel,
        in_specs=[HBM] * 5,
        out_specs=(VMEM,) * 6 + (SMEM,),
        scratch_shapes=[
            pltpu.VMEM((CTOK, GROUP * HD), BF16),
            pltpu.VMEM((CTOK, HD), BF16),
            pltpu.VMEM((CTOK, GROUP * HD), BF16),
            pltpu.VMEM((CTOK, GROUP * HD), BF16),
            pltpu.VMEM((1, CTOK), jnp.int32),
            pltpu.SemaphoreType.DMA((5,)),
        ],
        out_shape=(
            shape((CTOK, WIDE), BF16),
            shape((1,) + STAT),
            shape(STAT),
            shape(STAT),
            shape((WIDE, 2 * HD), BF16),
            shape((WIDE, 2 * HD), BF16),
            shape((1,)),
        ),
        compiler_params=params(57),
        cost_estimate=cost(CTOK, 1, 1, 1),
        name="self_scores",
    )(query, key_comp, out, d_out, steps)


def prompt_scores(norm, query, own, pair, row, m, l, split=(ROWS, ROWS), d_out=None, after=()):
    last = d_out is not None
    blocks = 2 * len(split)
    results = pl.pallas_call(
        functools.partial(prompt_scores_kernel, last, len(split), row, len(after)),
        in_specs=[SMEM] + [VMEM] * (6 if last else 5) + [UNREAD] * len(after),
        out_specs=(VMEM,) * (blocks + (5 if last else 3)),
        out_shape=tuple(shape((rows, WIDE), BF16) for rows in split) * 2
        + (shape((2,) + STAT), shape(STAT), shape(STAT))
        + ((shape((WIDE, HD), BF16),) * 2 if last else ()),
        compiler_params=params(16),
        cost_estimate=cost(2 * TILE, 1, 1, 1),
        name="prompt_scores",
    )(norm, query, own, pair, m, l, *([d_out] if last else []), *after)
    return results[:blocks], *results[blocks:]


def prompt_back(shared, dq, kvs, mts, tiles, es, outs, after=(), l=None):
    first, last = dq is None, l is not None
    operands = [*shared] + ([] if first else [dq]) + ([l] if last else []) + [*kvs, *mts, *es]
    out_shape = tuple(shape((rows, 2 * HD), dtype) for rows, dtype in outs)
    out_shape += (shape((CTOK, GROUP * HD), BF16) if last else shape(DQ),)
    return pl.pallas_call(
        functools.partial(prompt_back_kernel, first, last, tiles, len(kvs), len(mts), len(es), len(after)),
        in_specs=[VMEM] * len(operands) + [UNREAD] * len(after),
        out_specs=(VMEM,) * len(out_shape),
        out_shape=out_shape,
        scratch_shapes=[pltpu.VMEM(DQ, F32)] if last else [],
        compiler_params=params(20),
        cost_estimate=cost(sum(e.shape[0] for e in es), 4, 0, 1),
        name="prompt_back",
    )(*operands, *after)


def self_back(shared, dq, key_comp, value_comp, e, mt):
    return pl.pallas_call(
        self_back_kernel,
        in_specs=[VMEM] * 9,
        out_specs=(VMEM,) * 3,
        out_shape=(shape((CTOK, HD), BF16), shape((CTOK, HD), BF16), shape(DQ)),
        compiler_params=params(20),
        cost_estimate=cost(CTOK, 4, 0, 1),
        name="self_back",
    )(*shared, dq, key_comp, value_comp, e, mt)


def combine(*arrays):
    return pl.pallas_call(
        combine_kernel,
        in_specs=[VMEM] * 4,
        out_specs=(VMEM,) * 4,
        out_shape=(shape((HALF, 2 * HD), BF16),) * 3 + (shape((HALF, 2 * HD)),),
        compiler_params=params(6),
        name="combine",
    )(*arrays)


def finish(*arrays):
    return pl.pallas_call(
        finish_kernel,
        in_specs=[VMEM] * 6,
        out_specs=(VMEM,) * 2,
        out_shape=(shape((HALF, HD), BF16),) * 2,
        compiler_params=params(6),
        name="finish",
    )(*arrays)


def behind(result, *blocks):
    return lax.optimization_barrier(blocks + (result,))[:-1]


def shards(query, key_comp, value_comp, key_prompt, value_prompt, out, d_out, steps):
    here, turned = pack(key_prompt, value_prompt)

    here_y = send(here, dy=1)
    left = send(here, dx=1)
    right = send(here, dx=-1)
    e_self, mt_self, m, l, query, d_out, norm = self_scores(query, key_comp, out, d_out, steps.reshape(1, CTOK))
    here_y, left, right = behind(m, here_y, left, right)
    far = send(left, dx=1)
    near = stack([turned, here_y, left, right])
    near_pair = send(near, dc=1)
    left_y = send(left, dy=1)
    right_y = send(right, dy=-1)
    split = (HALF, HALF, ROWS)
    e_near, mt_near, m, l = prompt_scores(norm, query, near, near_pair, 0, m, l, split, after=(far,))
    far_y = send(far, dy=-1)
    e_beside, mt_beside, m, l = prompt_scores(norm, query, near, near_pair, TILE, m, l)
    left_y, right_y, far_y = behind(m, left_y, right_y, far_y)
    corners = stack([left_y, right_y])
    corners_pair = send(corners, dc=1)
    opposite = stack([far, far_y])
    opposite_pair = send(opposite, dc=1)
    e_corners, mt_corners, m, l = prompt_scores(norm, query, corners, corners_pair, 0, m, l)
    (opposite_pair,) = behind(m, opposite_pair)
    e_far, mt_far, m, l, wq, wdo = prompt_scores(norm, query, opposite, opposite_pair, 0, m, l, d_out=d_out)

    shared = d_out, wq, wdo, m
    add = lambda *parts: sum(rows.astype(F32) for rows in parts)
    both = [(TILE, F32), (TILE, BF16)]
    tiles = [([(1, 0, 2, 0, 1), (1, ROWS, 3, 0, 1)], [1]), ([(0, 0, 0, 0, 0), (0, ROWS, 1, 0, 0)], [0])]
    mine, theirs, dq = prompt_back(shared, None, [opposite, opposite_pair], [mt_far], tiles, e_far, both)
    pair_far = send(theirs, dc=1)
    total = add(mine, pair_far).astype(BF16)
    far_right = send(total[:ROWS], dx=1)
    far_left = send(total[ROWS:], dx=-1)

    def side(at, dq, after):
        row = at * ROWS
        beside = TILE + row
        tiles = [
            ([(1, beside, 1, 0, 1), (3, row, 3, 1, 1)], [1]),
            ([(0, beside, 0, 0, 0), (2, row, 2, 1, 0)], [0]),
        ]
        es = [e_beside[at], e_beside[2 + at], e_corners[at], e_corners[2 + at]]
        kvs = [near, near_pair, corners, corners_pair]
        return prompt_back(shared, dq, kvs, [mt_beside, mt_corners], tiles, es, both, after)

    mine_left, theirs, dq = side(0, dq, ())
    pair_left = send(theirs, dc=1)
    mine_right, theirs, dq = side(1, dq, (far_left, far_right))
    pair_right = send(theirs, dc=1)
    (pair_left,) = behind(theirs, pair_left)
    total = stack([add(mine_left[:ROWS], pair_left[:ROWS]), add(mine_left[ROWS:], pair_left[ROWS:], far_left)])
    from_right = send(total.astype(BF16), dx=-1)
    total = stack([add(mine_right[:ROWS], pair_right[:ROWS], far_right), add(mine_right[ROWS:], pair_right[ROWS:])])
    from_left = send(total.astype(BF16), dx=1)

    kvs = [near, near_pair]
    tiles = [([(1, 0, 1, 0, 1), (1, ROWS, 3, 0, 1)], [1]), ([(0, 0, 0, 0, 0), (0, ROWS, 2, 0, 0)], [0])]
    es = [e_near[0], e_near[3], e_near[2], e_near[5]]
    outs = [(HALF + ROWS, F32), (HALF + ROWS, BF16)]
    mine, theirs, dq = prompt_back(shared, dq, kvs, [mt_near], tiles, es, outs, (pair_right,))
    pair = send(theirs, dc=1)
    grad_key_comp, grad_value_comp, dq = self_back(shared, dq, key_comp, value_comp, e_self, mt_self)
    pair, from_left, from_right = behind(grad_key_comp, pair, from_left, from_right)
    across, above, below, own = combine(mine, pair, from_left, from_right)
    across = send(across, dy=2)
    above = send(above, dy=1)
    below = send(below, dy=-1)
    tiles = [([(0, HALF, 0, 0, 0), (1, HALF, 1, 0, 1)], [0, 1])]
    es = [e_near[1], e_near[4]]
    outs = [(HALF, F32), (HALF, BF16)]
    mine, theirs, grad_query = prompt_back(shared, dq, kvs, [mt_near], tiles, es, outs, (own,), l)
    pair = send(theirs, dc=1)
    across, above, below = behind(mine, across, above, below)
    grad_key_prompt, grad_value_prompt = finish(own, mine, pair, across, above, below)
    return (grad_query, grad_key_comp, grad_value_comp, grad_key_prompt, grad_value_prompt)


def solution(mesh):
    rows = P(("blk", "req"), "head")
    return jax.shard_map(
        shards,
        mesh=mesh,
        in_specs=(rows, rows, rows, P("blk", "head"), P("blk", "head"), rows, rows, P(("blk", "req"))),
        out_specs=(rows,) * 5,
        check_vma=False,
    )
```

```python
import functools

import jax
import jax.numpy as jnp
from jax import lax
from jax.experimental import pallas as pl
from jax.experimental.pallas import tpu as pltpu
from jax.sharding import PartitionSpec as P

HD = 128
GROUP = 8
CTOK = 256
ROWS = 384
TILE = 2 * ROWS
HALF = ROWS // 2
X, Y, CORES = 4, 4, 2
SCALE = HD ** (-0.5)
EXP2_SCALE = SCALE * 1.4426950408889634
PLAIN = 60.0
STAT = (GROUP, CTOK)
WIDE = GROUP * CTOK
DQ = (HD, WIDE)
HEADS = 4
CHUNK = 256
F32 = jnp.float32
BF16 = jnp.bfloat16


def place(x, y, core):
    return ((x * 2 + y % 2) * CORES + core) * 2 + y // 2


def send(block, dx=0, dy=0, dc=0):
    route = []
    for x in range(X):
        for y in range(Y):
            for core in range(CORES):
                there = place((x + dx) % X, (y + dy) % Y, core ^ dc)
                route.append((place(x, y, core), there))
    return lax.ppermute(block, ("blk", "req"), route)


def part(ref, n, width):
    return ref[:, n * width : (n + 1) * width]


def dot(a, b, contract):
    return lax.dot_general(a, b, (contract, ((), ())), preferred_element_type=F32)


def largest_norm(rows):
    wide = rows.astype(F32)
    return jnp.max(jnp.sum(wide * wide, axis=1, keepdims=True))


def within(query_norm, key_norm):
    return query_norm * key_norm * (EXP2_SCALE * EXP2_SCALE) <= PLAIN * PLAIN


def put(e, n, parts, first=0):
    low = e.astype(BF16)
    start = 0
    for ref in parts:
        begin, end = max(start, first), min(start + ref.shape[0], first + e.shape[0])
        if begin < end:
            ref[begin - start : end - start, n * CTOK : (n + 1) * CTOK] = low[begin - first : end - first]
        start += ref.shape[0]


def plain_tile(keys, q_ref, visible, l_ref, parts, mt_ref, tile):
    mt_ref[tile] = jnp.zeros(STAT, F32)
    keys = jnp.concatenate([keys, keys], axis=1)
    for n in range(GROUP):
        total = l_ref[n : n + 1, :]
        for first in range(0, keys.shape[0], CHUNK):
            e = jnp.exp2(dot(keys[first : first + CHUNK], q_ref[n * CTOK : (n + 1) * CTOK, :], ((1,), (1,))))
            if visible is not None:
                e = jnp.where(visible, e, 0.0)
            total = total + jnp.sum(e, axis=0, keepdims=True)
            put(e, n, parts, first)
        l_ref[n : n + 1, :] = total


def general_tile(keys, q_ref, visible, m_ref, l_ref, parts, mt_ref, tile):
    keys = jnp.concatenate([keys, keys], axis=1)
    for n in range(GROUP):
        scores = dot(keys, q_ref[n * CTOK : (n + 1) * CTOK, :], ((1,), (1,)))
        if visible is not None:
            scores = jnp.where(visible, scores, -jnp.inf)
        m_old = m_ref[n : n + 1, :]
        m_new = jnp.maximum(m_old, jnp.max(scores, axis=0, keepdims=True))
        e = jnp.exp2(scores - m_new)
        total = jnp.sum(e, axis=0, keepdims=True)
        l_ref[n : n + 1, :] = l_ref[n : n + 1, :] * jnp.exp2(m_old - m_new) + total
        m_ref[n : n + 1, :] = m_new
        mt_ref[tile, n : n + 1, :] = m_new
        put(e, n, parts)


def y_place():
    y_high = lax.axis_index("req")
    y_low = lax.rem(lax.div(lax.axis_index("blk"), CORES), 2)
    return y_high, jnp.where(y_low == 0, y_high, 1 - y_high)


def half_rows(at):
    return pl.ds(pl.multiple_of(at * HALF, HALF), HALF)


def fetch(pairs, sems):
    copies = [pltpu.make_async_copy(far, near, sems.at[at]) for at, (far, near) in enumerate(pairs)]
    for copy in copies:
        copy.start()
    for copy in copies:
        copy.wait()


def pack_kernel(k_hbm, v_hbm, kv_ref, turned_ref, sems):
    y_high, _ = y_place()
    pairs = []
    for far, columns in ((k_hbm, slice(0, HD)), (v_hbm, slice(HD, 2 * HD))):
        pairs.append((far, kv_ref.at[:, columns]))
        pairs.append((far.at[half_rows(1 - y_high), :], turned_ref.at[:HALF, columns]))
        pairs.append((far.at[half_rows(y_high), :], turned_ref.at[HALF:, columns]))
    fetch(pairs, sems)


def self_scores_kernel(
    q_hbm, k_hbm, out_hbm, do_hbm, step_hbm, *refs
):
    e_ref, mt_ref, m_ref, l_ref, q_out, do_out, norm_ref, q_ref, k_ref, out_ref, do_ref, step_ref, sems = refs
    fetch(
        [(k_hbm, k_ref), (step_hbm, step_ref), (q_hbm, q_ref), (do_hbm, do_ref), (out_hbm, out_ref)], sems
    )
    keys = k_ref[...]
    step = jnp.broadcast_to(step_ref[...].astype(F32), (CTOK, CTOK))
    visible = step.T <= step
    lane = lax.broadcasted_iota(jnp.int32, (CTOK, HD), 1)
    norm = None
    for n in range(GROUP):
        do_n = part(do_ref, n, HD)
        left = jnp.sum(do_n.astype(F32) * part(out_ref, n, HD).astype(F32), axis=1, keepdims=True)
        terms = jnp.zeros((CTOK, HD), F32)
        for place_at in range(3):
            term = left.astype(BF16).astype(F32)
            terms = jnp.where(lane == place_at, -term, terms)
            left = left - term
        do_out[n * CTOK : (n + 1) * CTOK, :HD] = do_n
        do_out[n * CTOK : (n + 1) * CTOK, HD:] = terms.astype(BF16)
        scaled = part(q_ref, n, HD).astype(F32) * EXP2_SCALE
        high = scaled.astype(BF16)
        q_out[n * CTOK : (n + 1) * CTOK, :HD] = high
        q_out[n * CTOK : (n + 1) * CTOK, HD:] = (scaled - high.astype(F32)).astype(BF16)
        rows = largest_norm(part(q_ref, n, HD))
        norm = rows if norm is None else jnp.maximum(norm, rows)
    norm_ref[0] = norm
    l_ref[...] = jnp.zeros(STAT, F32)
    m_ref[...] = jnp.zeros(STAT, F32)
    plain_tile(keys, q_out, visible, l_ref, [e_ref], mt_ref, 0)

    @pl.when(jnp.logical_not(within(norm, largest_norm(keys))))
    def _():
        l_ref[...] = jnp.zeros(STAT, F32)
        m_ref[...] = jnp.full(STAT, -1e30, F32)
        general_tile(keys, q_out, visible, m_ref, l_ref, [e_ref], mt_ref, 0)


def prompt_scores_kernel(last, pieces, row, unread, *refs):
    norm_ref, q_ref, own_ref, pair_ref, m_in, l_in, *refs = refs
    if last:
        do_ref, *refs = refs
    refs = refs[unread:]
    e_refs, refs = refs[: 2 * pieces], refs[2 * pieces :]
    mt_ref, m_ref, l_ref, *refs = refs
    m_ref[...] = m_in[...]
    l_ref[...] = l_in[...]
    for tile, kv_ref in enumerate((own_ref, pair_ref)):
        keys = kv_ref[row : row + TILE, :HD]
        parts = e_refs[tile * pieces : (tile + 1) * pieces]
        l_old = l_ref[...]
        plain = within(norm_ref[0], largest_norm(keys)) & (jnp.max(jnp.abs(m_ref[...])) == 0.0)
        plain_tile(keys, q_ref, None, l_ref, parts, mt_ref, tile)

        @pl.when(jnp.logical_not(plain))
        def _():
            l_ref[...] = l_old
            general_tile(keys, q_ref, None, m_ref, l_ref, parts, mt_ref, tile)

    if last:
        wq_ref, wdo_ref = refs
        for n in range(GROUP):
            weight = jnp.broadcast_to(1.0 / l_ref[n : n + 1, :], (HD, CTOK)).T
            heads = slice(n * CTOK, (n + 1) * CTOK)
            q_n = (q_ref[heads, :HD].astype(F32) + q_ref[heads, HD:].astype(F32)) * (1.0 / EXP2_SCALE)
            wq_ref[heads, :] = (q_n * weight).astype(BF16)
            wdo_ref[heads, :] = (do_ref[heads, :HD].astype(F32) * weight).astype(BF16)


def stack(parts):
    return parts[0] if len(parts) == 1 else jnp.concatenate(parts, axis=0)


def back_rows(pieces, do_ref, wq_ref, wdo_ref, m_ref, dq_ref, changed):
    keys = stack([keys for keys, _, _, _ in pieces])
    values = stack([values for _, values, _, _ in pieces])
    lane = lax.broadcasted_iota(jnp.int32, values.shape, 1)
    ones = jnp.where(lane < 3, 1.0, 0.0).astype(BF16)
    values = jnp.concatenate([values, ones], axis=1)
    keys_t = keys.T
    grad_keys = grad_values = None
    for n in range(0, GROUP, HEADS):
        columns = slice(n * CTOK, (n + HEADS) * CTOK)
        parts = []
        for _, _, e_ref, top in pieces:
            e = e_ref[:, columns]
            if changed:
                log_change = [top[h : h + 1, :] - m_ref[h : h + 1, :] for h in range(n, n + HEADS)]
                e = (e.astype(F32) * jnp.exp2(jnp.concatenate(log_change, axis=1))).astype(BF16)
            parts.append(e)
        e = stack(parts)
        grad_prob = dot(values, do_ref[columns, :], ((1,), (1,)))
        part_value = dot(e, wdo_ref[columns, :], ((1,), (0,)))
        grad_score = e * grad_prob.astype(BF16)
        part_key = dot(grad_score, wq_ref[columns, :], ((1,), (0,)))
        dq_ref[:, columns] += dot(keys_t, grad_score, ((1,), (0,)))
        grad_keys = part_key if n == 0 else grad_keys + part_key
        grad_values = part_value if n == 0 else grad_values + part_value
    return grad_keys * SCALE, grad_values


def either_way(m_ref, mt_refs, work):
    tops = [mt_ref[t] for mt_ref in mt_refs for t in range(mt_ref.shape[0])]
    change = functools.reduce(jnp.maximum, [jnp.abs(top - m_ref[...]) for top in tops])
    plain = jnp.max(change) == 0.0
    pl.when(plain)(lambda: work(False))
    pl.when(jnp.logical_not(plain))(lambda: work(True))


def prompt_back_kernel(first, last, tiles, sources, tops, blocks, unread, *refs):
    do_ref, wq_ref, wdo_ref, m_ref, *refs = refs
    if not first:
        dq_in, *refs = refs
    if last:
        l_ref, *refs = refs
    kv_refs, refs = refs[:sources], refs[sources:]
    mt_refs, refs = refs[:tops], refs[tops:]
    e_refs, refs = refs[:blocks], refs[blocks + unread :]
    *out_refs, dq_ref = refs
    if last:
        *out_refs, query_ref = out_refs
    dq_ref[...] = jnp.zeros_like(dq_ref) if first else dq_in[...]

    def work(changed):
        for members, outs in tiles:
            pieces = []
            for source, row, block, top, tile in members:
                e_ref = e_refs[block]
                rows = slice(row, row + e_ref.shape[0])
                kv_ref = kv_refs[source]
                pieces.append((kv_ref[rows, :HD], kv_ref[rows, HD:], e_ref, mt_refs[top][tile]))
            grad_keys, grad_values = back_rows(pieces, do_ref, wq_ref, wdo_ref, m_ref, dq_ref, changed)
            start = 0
            for at in outs:
                ref = out_refs[at]
                rows = slice(start, start + ref.shape[0])
                ref[:, :HD] = grad_keys[rows].astype(ref.dtype)
                ref[:, HD:] = grad_values[rows].astype(ref.dtype)
                start += ref.shape[0]

    either_way(m_ref, mt_refs, work)
    if last:
        for n in range(GROUP):
            weight = SCALE / l_ref[n : n + 1, :]
            query_ref[:, n * HD : (n + 1) * HD] = (part(dq_ref, n, CTOK) * weight).T.astype(BF16)


def self_back_kernel(do_ref, wq_ref, wdo_ref, m_ref, dq_in, k_ref, v_ref, e_ref, mt_ref, dk_ref, dv_ref, dq_ref):
    dq_ref[...] = dq_in[...]

    def work(changed):
        pieces = [(k_ref[...], v_ref[...], e_ref, mt_ref[0])]
        grad_keys, grad_values = back_rows(pieces, do_ref, wq_ref, wdo_ref, m_ref, dq_ref, changed)
        dk_ref[...] = grad_keys.astype(BF16)
        dv_ref[...] = grad_values.astype(BF16)

    either_way(m_ref, [mt_ref], work)


def combine_kernel(mine_ref, pair_ref, left_ref, right_ref, across_ref, above_ref, below_ref, own_ref):
    y_high, up = y_place()

    def arrived(at):
        rows = half_rows(at)
        return left_ref[rows, :].astype(F32) + right_ref[rows, :].astype(F32)

    def leaving(at, beside):
        rows = half_rows(at)
        return (mine_ref[rows, :] + pair_ref[rows, :].astype(F32) + arrived(beside)).astype(BF16)

    across_ref[...] = leaving(0, 1 - y_high)
    above_ref[...] = leaving(1 + up, 2 + up)
    below_ref[...] = leaving(2 - up, 3 - up)
    own_ref[...] = arrived(y_high)


def finish_kernel(own_ref, mine_ref, pair_ref, across_ref, above_ref, below_ref, dk_ref, dv_ref):
    total = own_ref[...] + mine_ref[...]
    for ref in (pair_ref, across_ref, above_ref, below_ref):
        total = total + ref[...].astype(F32)
    dk_ref[...] = total[:, :HD].astype(BF16)
    dv_ref[...] = total[:, HD:].astype(BF16)


def params(mib):
    return pltpu.CompilerParams(vmem_limit_bytes=mib * 1024 * 1024)


VMEM = pl.BlockSpec(memory_space=pltpu.VMEM)
HBM = pl.BlockSpec(memory_space=pltpu.HBM)
SMEM = pl.BlockSpec(memory_space=pltpu.SMEM)
UNREAD = pl.BlockSpec(memory_space=pl.ANY)


def whole(dims):
    return pl.BlockSpec(dims, lambda *_: (0,) * len(dims))


def cost(rows, matmuls, exps, stored):
    return pl.CostEstimate(
        flops=2 * rows * WIDE * HD * matmuls,
        bytes_accessed=rows * WIDE * 2 * stored,
        transcendentals=rows * WIDE * exps,
    )


def shape(dims, dtype=F32):
    return jax.ShapeDtypeStruct(dims, dtype)


def pack(keys, values):
    return pl.pallas_call(
        pack_kernel,
        in_specs=[HBM] * 2,
        out_specs=(VMEM,) * 2,
        out_shape=(shape((ROWS, 2 * HD), BF16),) * 2,
        scratch_shapes=[pltpu.SemaphoreType.DMA((6,))],
        compiler_params=params(60),
        name="pack",
    )(keys, values)


def self_scores(query, key_comp, out, d_out, steps):
    return pl.pallas_call(
        self_scores_kernel,
        in_specs=[HBM] * 5,
        out_specs=(VMEM,) * 6 + (SMEM,),
        scratch_shapes=[
            pltpu.VMEM((CTOK, GROUP * HD), BF16),
            pltpu.VMEM((CTOK, HD), BF16),
            pltpu.VMEM((CTOK, GROUP * HD), BF16),
            pltpu.VMEM((CTOK, GROUP * HD), BF16),
            pltpu.VMEM((1, CTOK), jnp.int32),
            pltpu.SemaphoreType.DMA((5,)),
        ],
        out_shape=(
            shape((CTOK, WIDE), BF16),
            shape((1,) + STAT),
            shape(STAT),
            shape(STAT),
            shape((WIDE, 2 * HD), BF16),
            shape((WIDE, 2 * HD), BF16),
            shape((1,)),
        ),
        compiler_params=params(57),
        cost_estimate=cost(CTOK, 1, 1, 1),
        name="self_scores",
    )(query, key_comp, out, d_out, steps)


def prompt_scores(norm, query, own, pair, row, m, l, split=(ROWS, ROWS), d_out=None, after=()):
    last = d_out is not None
    blocks = 2 * len(split)
    results = pl.pallas_call(
        functools.partial(prompt_scores_kernel, last, len(split), row, len(after)),
        in_specs=[SMEM] + [VMEM] * (6 if last else 5) + [UNREAD] * len(after),
        out_specs=(VMEM,) * (blocks + (5 if last else 3)),
        out_shape=tuple(shape((rows, WIDE), BF16) for rows in split) * 2
        + (shape((2,) + STAT), shape(STAT), shape(STAT))
        + ((shape((WIDE, HD), BF16),) * 2 if last else ()),
        compiler_params=params(16),
        cost_estimate=cost(2 * TILE, 1, 1, 1),
        name="prompt_scores",
    )(norm, query, own, pair, m, l, *([d_out] if last else []), *after)
    return results[:blocks], *results[blocks:]


def prompt_back(shared, dq, kvs, mts, tiles, es, outs, after=(), l=None):
    first, last = dq is None, l is not None
    operands = [*shared] + ([] if first else [dq]) + ([l] if last else []) + [*kvs, *mts, *es]
    out_shape = tuple(shape((rows, 2 * HD), dtype) for rows, dtype in outs)
    out_shape += (shape((CTOK, GROUP * HD), BF16) if last else shape(DQ),)
    return pl.pallas_call(
        functools.partial(prompt_back_kernel, first, last, tiles, len(kvs), len(mts), len(es), len(after)),
        in_specs=[VMEM] * len(operands) + [UNREAD] * len(after),
        out_specs=(VMEM,) * len(out_shape),
        out_shape=out_shape,
        scratch_shapes=[pltpu.VMEM(DQ, F32)] if last else [],
        compiler_params=params(20),
        cost_estimate=cost(sum(e.shape[0] for e in es), 4, 0, 1),
        name="prompt_back",
    )(*operands, *after)


def self_back(shared, dq, key_comp, value_comp, e, mt):
    return pl.pallas_call(
        self_back_kernel,
        in_specs=[VMEM] * 9,
        out_specs=(VMEM,) * 3,
        out_shape=(shape((CTOK, HD), BF16), shape((CTOK, HD), BF16), shape(DQ)),
        compiler_params=params(20),
        cost_estimate=cost(CTOK, 4, 0, 1),
        name="self_back",
    )(*shared, dq, key_comp, value_comp, e, mt)


def combine(*arrays):
    return pl.pallas_call(
        combine_kernel,
        in_specs=[VMEM] * 4,
        out_specs=(VMEM,) * 4,
        out_shape=(shape((HALF, 2 * HD), BF16),) * 3 + (shape((HALF, 2 * HD)),),
        compiler_params=params(6),
        name="combine",
    )(*arrays)


def finish(*arrays):
    return pl.pallas_call(
        finish_kernel,
        in_specs=[VMEM] * 6,
        out_specs=(VMEM,) * 2,
        out_shape=(shape((HALF, HD), BF16),) * 2,
        compiler_params=params(6),
        name="finish",
    )(*arrays)


def behind(result, *blocks):
    return lax.optimization_barrier(blocks + (result,))[:-1]


def shards(query, key_comp, value_comp, key_prompt, value_prompt, out, d_out, steps):
    here, turned = pack(key_prompt, value_prompt)

    here_y = send(here, dy=1)
    left = send(here, dx=1)
    right = send(here, dx=-1)
    e_self, mt_self, m, l, query, d_out, norm = self_scores(query, key_comp, out, d_out, steps.reshape(1, CTOK))
    here_y, left, right = behind(m, here_y, left, right)
    far = send(left, dx=1)
    near = stack([turned, here_y, left, right])
    near_pair = send(near, dc=1)
    left_y = send(left, dy=1)
    right_y = send(right, dy=-1)
    split = (HALF, HALF, ROWS)
    e_near, mt_near, m, l = prompt_scores(norm, query, near, near_pair, 0, m, l, split)
    (far,) = behind(m, far)
    far_y = send(far, dy=-1)
    e_beside, mt_beside, m, l = prompt_scores(norm, query, near, near_pair, TILE, m, l)
    left_y, right_y = behind(m, left_y, right_y)
    corners = stack([left_y, right_y])
    corners_pair = send(corners, dc=1)
    (far_y,) = behind(m, far_y)
    opposite = stack([far, far_y])
    opposite_pair = send(opposite, dc=1)
    e_corners, mt_corners, m, l = prompt_scores(norm, query, corners, corners_pair, 0, m, l)
    (opposite_pair,) = behind(m, opposite_pair)
    e_far, mt_far, m, l, wq, wdo = prompt_scores(norm, query, opposite, opposite_pair, 0, m, l, d_out=d_out)

    shared = d_out, wq, wdo, m
    add = lambda *parts: sum(rows.astype(F32) for rows in parts)
    both = [(TILE, F32), (TILE, BF16)]
    tiles = [([(1, 0, 2, 0, 1), (1, ROWS, 3, 0, 1)], [1]), ([(0, 0, 0, 0, 0), (0, ROWS, 1, 0, 0)], [0])]
    mine, theirs, dq = prompt_back(shared, None, [opposite, opposite_pair], [mt_far], tiles, e_far, both)
    pair_far = send(theirs, dc=1)
    total = add(mine, pair_far).astype(BF16)
    far_right = send(total[:ROWS], dx=1)
    far_left = send(total[ROWS:], dx=-1)

    def side(at, dq, after):
        row = at * ROWS
        beside = TILE + row
        tiles = [
            ([(1, beside, 1, 0, 1), (3, row, 3, 1, 1)], [1]),
            ([(0, beside, 0, 0, 0), (2, row, 2, 1, 0)], [0]),
        ]
        es = [e_beside[at], e_beside[2 + at], e_corners[at], e_corners[2 + at]]
        kvs = [near, near_pair, corners, corners_pair]
        return prompt_back(shared, dq, kvs, [mt_beside, mt_corners], tiles, es, both, after)

    mine_left, theirs, dq = side(0, dq, ())
    pair_left = send(theirs, dc=1)
    mine_right, theirs, dq = side(1, dq, (far_left, far_right))
    pair_right = send(theirs, dc=1)
    (pair_left,) = behind(theirs, pair_left)
    total = stack([add(mine_left[:ROWS], pair_left[:ROWS]), add(mine_left[ROWS:], pair_left[ROWS:], far_left)])
    from_right = send(total.astype(BF16), dx=-1)
    total = stack([add(mine_right[:ROWS], pair_right[:ROWS], far_right), add(mine_right[ROWS:], pair_right[ROWS:])])
    from_left = send(total.astype(BF16), dx=1)

    kvs = [near, near_pair]
    tiles = [([(1, 0, 1, 0, 1), (1, ROWS, 3, 0, 1)], [1]), ([(0, 0, 0, 0, 0), (0, ROWS, 2, 0, 0)], [0])]
    es = [e_near[0], e_near[3], e_near[2], e_near[5]]
    outs = [(HALF + ROWS, F32), (HALF + ROWS, BF16)]
    mine, theirs, dq = prompt_back(shared, dq, kvs, [mt_near], tiles, es, outs, (pair_right,))
    pair = send(theirs, dc=1)
    grad_key_comp, grad_value_comp, dq = self_back(shared, dq, key_comp, value_comp, e_self, mt_self)
    pair, from_left, from_right = behind(grad_key_comp, pair, from_left, from_right)
    across, above, below, own = combine(mine, pair, from_left, from_right)
    across = send(across, dy=2)
    above = send(above, dy=1)
    below = send(below, dy=-1)
    tiles = [([(0, HALF, 0, 0, 0), (1, HALF, 1, 0, 1)], [0, 1])]
    es = [e_near[1], e_near[4]]
    outs = [(HALF, F32), (HALF, BF16)]
    mine, theirs, grad_query = prompt_back(shared, dq, kvs, [mt_near], tiles, es, outs, (own,), l)
    pair = send(theirs, dc=1)
    across, above, below = behind(mine, across, above, below)
    grad_key_prompt, grad_value_prompt = finish(own, mine, pair, across, above, below)
    return (grad_query, grad_key_comp, grad_value_comp, grad_key_prompt, grad_value_prompt)


def solution(mesh):
    rows = P(("blk", "req"), "head")
    return jax.shard_map(
        shards,
        mesh=mesh,
        in_specs=(rows, rows, rows, P("blk", "head"), P("blk", "head"), rows, rows, P(("blk", "req"))),
        out_specs=(rows,) * 5,
        check_vma=False,
    )
```

```python
import functools

import jax
import jax.numpy as jnp
from jax import lax
from jax.experimental import pallas as pl
from jax.experimental.pallas import tpu as pltpu
from jax.sharding import PartitionSpec as P

HD = 128
GROUP = 8
CTOK = 256
ROWS = 384
TILE = 2 * ROWS
HALF = ROWS // 2
X, Y, CORES = 4, 4, 2
SCALE = HD ** (-0.5)
EXP2_SCALE = SCALE * 1.4426950408889634
PLAIN = 60.0
STAT = (GROUP, CTOK)
WIDE = GROUP * CTOK
DQ = (HD, WIDE)
HEADS = 4
CHUNK = 256
F32 = jnp.float32
BF16 = jnp.bfloat16


def place(x, y, core):
    return ((x * 2 + y % 2) * CORES + core) * 2 + y // 2


def send(block, dx=0, dy=0, dc=0):
    route = []
    for x in range(X):
        for y in range(Y):
            for core in range(CORES):
                there = place((x + dx) % X, (y + dy) % Y, core ^ dc)
                route.append((place(x, y, core), there))
    return lax.ppermute(block, ("blk", "req"), route)


def part(ref, n, width):
    return ref[:, n * width : (n + 1) * width]


def dot(a, b, contract):
    return lax.dot_general(a, b, (contract, ((), ())), preferred_element_type=F32)


def largest_norm(rows):
    wide = rows.astype(F32)
    return jnp.max(jnp.sum(wide * wide, axis=1, keepdims=True))


def within(query_norm, key_norm):
    return query_norm * key_norm * (EXP2_SCALE * EXP2_SCALE) <= PLAIN * PLAIN


def put(e, n, parts, first=0):
    low = e.astype(BF16)
    start = 0
    for ref in parts:
        begin, end = max(start, first), min(start + ref.shape[0], first + e.shape[0])
        if begin < end:
            ref[begin - start : end - start, n * CTOK : (n + 1) * CTOK] = low[begin - first : end - first]
        start += ref.shape[0]


def plain_tile(keys, q_ref, visible, l_ref, parts, mt_ref, tile):
    mt_ref[tile] = jnp.zeros(STAT, F32)
    keys = jnp.concatenate([keys, keys], axis=1)
    for n in range(GROUP):
        total = l_ref[n : n + 1, :]
        for first in range(0, keys.shape[0], CHUNK):
            e = jnp.exp2(dot(keys[first : first + CHUNK], q_ref[n * CTOK : (n + 1) * CTOK, :], ((1,), (1,))))
            if visible is not None:
                e = jnp.where(visible, e, 0.0)
            total = total + jnp.sum(e, axis=0, keepdims=True)
            put(e, n, parts, first)
        l_ref[n : n + 1, :] = total


def general_tile(keys, q_ref, visible, m_ref, l_ref, parts, mt_ref, tile):
    keys = jnp.concatenate([keys, keys], axis=1)

    def one_head(n, carry):
        columns = pl.ds(pl.multiple_of(n * CTOK, CTOK), CTOK)
        row = pl.ds(n, 1)
        scores = dot(keys, q_ref[columns, :], ((1,), (1,)))
        if visible is not None:
            scores = jnp.where(visible, scores, -jnp.inf)
        m_old = m_ref[row, :]
        m_new = jnp.maximum(m_old, jnp.max(scores, axis=0, keepdims=True))
        e = jnp.exp2(scores - m_new)
        total = jnp.sum(e, axis=0, keepdims=True)
        l_ref[row, :] = l_ref[row, :] * jnp.exp2(m_old - m_new) + total
        m_ref[row, :] = m_new
        mt_ref[tile, row, :] = m_new
        start = 0
        for ref in parts:
            ref[:, columns] = e[start : start + ref.shape[0]].astype(BF16)
            start += ref.shape[0]
        return carry

    lax.fori_loop(0, GROUP, one_head, 0)


def bring_to(m_ref, members):
    change = functools.reduce(jnp.maximum, [jnp.abs(mt_ref[tile] - m_ref[...]) for _, mt_ref, tile in members])

    @pl.when(jnp.max(change) != 0.0)
    def _():
        for ref, mt_ref, tile in members:
            log_change = mt_ref[tile] - m_ref[...]
            factor = jnp.exp2(jnp.concatenate([log_change[n : n + 1] for n in range(GROUP)], axis=1))

            def some_rows(step, carry, ref=ref, factor=factor):
                rows = pl.ds(pl.multiple_of(step * 16, 16), 16)
                ref[rows, :] = (ref[rows, :].astype(F32) * factor).astype(BF16)
                return carry

            lax.fori_loop(0, ref.shape[0] // 16, some_rows, 0)


def y_place():
    y_high = lax.axis_index("req")
    y_low = lax.rem(lax.div(lax.axis_index("blk"), CORES), 2)
    return y_high, jnp.where(y_low == 0, y_high, 1 - y_high)


def half_rows(at):
    return pl.ds(pl.multiple_of(at * HALF, HALF), HALF)


def fetch(pairs, sems):
    copies = [pltpu.make_async_copy(far, near, sems.at[at]) for at, (far, near) in enumerate(pairs)]
    for copy in copies:
        copy.start()
    for copy in copies:
        copy.wait()


def pack_kernel(k_hbm, v_hbm, kv_ref, turned_ref, sems):
    y_high, _ = y_place()
    pairs = []
    for far, columns in ((k_hbm, slice(0, HD)), (v_hbm, slice(HD, 2 * HD))):
        pairs.append((far, kv_ref.at[:, columns]))
        pairs.append((far.at[half_rows(1 - y_high), :], turned_ref.at[:HALF, columns]))
        pairs.append((far.at[half_rows(y_high), :], turned_ref.at[HALF:, columns]))
    fetch(pairs, sems)


def self_scores_kernel(
    q_hbm, k_hbm, out_hbm, do_hbm, step_hbm, *refs
):
    e_ref, mt_ref, m_ref, l_ref, q_out, do_out, norm_ref, q_ref, k_ref, out_ref, do_ref, step_ref, sems = refs
    fetch(
        [(k_hbm, k_ref), (step_hbm, step_ref), (q_hbm, q_ref), (do_hbm, do_ref), (out_hbm, out_ref)], sems
    )
    keys = k_ref[...]
    step = jnp.broadcast_to(step_ref[...].astype(F32), (CTOK, CTOK))
    visible = step.T <= step
    lane = lax.broadcasted_iota(jnp.int32, (CTOK, HD), 1)
    norm = None
    for n in range(GROUP):
        do_n = part(do_ref, n, HD)
        left = jnp.sum(do_n.astype(F32) * part(out_ref, n, HD).astype(F32), axis=1, keepdims=True)
        terms = jnp.zeros((CTOK, HD), F32)
        for place_at in range(3):
            term = left.astype(BF16).astype(F32)
            terms = jnp.where(lane == place_at, -term, terms)
            left = left - term
        do_out[n * CTOK : (n + 1) * CTOK, :HD] = do_n
        do_out[n * CTOK : (n + 1) * CTOK, HD:] = terms.astype(BF16)
        scaled = part(q_ref, n, HD).astype(F32) * EXP2_SCALE
        high = scaled.astype(BF16)
        q_out[n * CTOK : (n + 1) * CTOK, :HD] = high
        q_out[n * CTOK : (n + 1) * CTOK, HD:] = (scaled - high.astype(F32)).astype(BF16)
        rows = largest_norm(part(q_ref, n, HD))
        norm = rows if norm is None else jnp.maximum(norm, rows)
    norm_ref[...] = jnp.full(norm_ref.shape, norm, F32)
    l_ref[...] = jnp.zeros(STAT, F32)
    m_ref[...] = jnp.zeros(STAT, F32)
    plain_tile(keys, q_out, visible, l_ref, [e_ref], mt_ref, 0)

    @pl.when(jnp.logical_not(within(norm, largest_norm(keys))))
    def _():
        l_ref[...] = jnp.zeros(STAT, F32)
        m_ref[...] = jnp.full(STAT, -1e30, F32)
        general_tile(keys, q_out, visible, m_ref, l_ref, [e_ref], mt_ref, 0)


def prompt_scores_kernel(pieces, row, earlier, *refs):
    norm_ref, q_ref, own_ref, pair_ref, m_in, l_in, *refs = refs
    if earlier:
        do_ref, *refs = refs
        tops = max(top for top, _ in earlier) + 1
        mt_refs, refs = refs[:tops], refs[tops + len(earlier) :]
    e_refs, refs = refs[: 2 * pieces], refs[2 * pieces :]
    mt_ref, m_ref, l_ref, *refs = refs
    m_ref[...] = m_in[...]
    l_ref[...] = l_in[...]
    for tile, kv_ref in enumerate((own_ref, pair_ref)):
        keys = kv_ref[row : row + TILE, :HD]
        parts = e_refs[tile * pieces : (tile + 1) * pieces]
        l_old = l_ref[...]
        plain = within(jnp.max(norm_ref[...]), largest_norm(keys)) & (jnp.max(jnp.abs(m_ref[...])) == 0.0)
        plain_tile(keys, q_ref, None, l_ref, parts, mt_ref, tile)

        @pl.when(jnp.logical_not(plain))
        def _():
            l_ref[...] = l_old
            general_tile(keys, q_ref, None, m_ref, l_ref, parts, mt_ref, tile)

    if earlier:
        wq_ref, wdo_ref, *blocks = refs
        for n in range(GROUP):
            weight = jnp.broadcast_to(1.0 / l_ref[n : n + 1, :], (HD, CTOK)).T
            heads = slice(n * CTOK, (n + 1) * CTOK)
            q_n = (q_ref[heads, :HD].astype(F32) + q_ref[heads, HD:].astype(F32)) * (1.0 / EXP2_SCALE)
            wq_ref[heads, :] = (q_n * weight).astype(BF16)
            wdo_ref[heads, :] = (do_ref[heads, :HD].astype(F32) * weight).astype(BF16)
        members = [(ref, mt_refs[top], tile) for ref, (top, tile) in zip(blocks, earlier)]
        members += [(ref, mt_ref, at // pieces) for at, ref in enumerate(e_refs)]
        bring_to(m_ref, members)


def stack(parts):
    return parts[0] if len(parts) == 1 else jnp.concatenate(parts, axis=0)


def back_rows(pieces, do_ref, wq_ref, wdo_ref, dq_ref):
    keys = stack([keys for keys, _, _ in pieces])
    values = stack([values for _, values, _ in pieces])
    lane = lax.broadcasted_iota(jnp.int32, values.shape, 1)
    ones = jnp.where(lane < 3, 1.0, 0.0).astype(BF16)
    values = jnp.concatenate([values, ones], axis=1)
    keys_t = keys.T
    grad_keys = grad_values = None
    for n in range(0, GROUP, HEADS):
        columns = slice(n * CTOK, (n + HEADS) * CTOK)
        e = stack([e_ref[:, columns] for _, _, e_ref in pieces])
        grad_prob = dot(values, do_ref[columns, :], ((1,), (1,)))
        part_value = dot(e, wdo_ref[columns, :], ((1,), (0,)))
        grad_score = e * grad_prob.astype(BF16)
        part_key = dot(grad_score, wq_ref[columns, :], ((1,), (0,)))
        dq_ref[:, columns] += dot(keys_t, grad_score, ((1,), (0,)))
        grad_keys = part_key if n == 0 else grad_keys + part_key
        grad_values = part_value if n == 0 else grad_values + part_value
    return grad_keys * SCALE, grad_values


def prompt_back_kernel(first, last, tiles, sources, blocks, unread, *refs):
    do_ref, wq_ref, wdo_ref, *refs = refs
    if not first:
        dq_in, *refs = refs
    if last:
        l_ref, *refs = refs
    kv_refs, refs = refs[:sources], refs[sources:]
    e_refs, refs = refs[:blocks], refs[blocks + unread :]
    *out_refs, dq_ref = refs
    if last:
        *out_refs, query_ref = out_refs
    dq_ref[...] = jnp.zeros_like(dq_ref) if first else dq_in[...]
    for members, outs in tiles:
        pieces = []
        for source, row, block in members:
            e_ref = e_refs[block]
            rows = slice(row, row + e_ref.shape[0])
            kv_ref = kv_refs[source]
            pieces.append((kv_ref[rows, :HD], kv_ref[rows, HD:], e_ref))
        grad_keys, grad_values = back_rows(pieces, do_ref, wq_ref, wdo_ref, dq_ref)
        start = 0
        for at in outs:
            ref = out_refs[at]
            rows = slice(start, start + ref.shape[0])
            ref[:, :HD] = grad_keys[rows].astype(ref.dtype)
            ref[:, HD:] = grad_values[rows].astype(ref.dtype)
            start += ref.shape[0]
    if last:
        for n in range(GROUP):
            weight = SCALE / l_ref[n : n + 1, :]
            query_ref[:, n * HD : (n + 1) * HD] = (part(dq_ref, n, CTOK) * weight).T.astype(BF16)


def self_back_kernel(do_ref, wq_ref, wdo_ref, dq_in, k_ref, v_ref, e_ref, dk_ref, dv_ref, dq_ref):
    dq_ref[...] = dq_in[...]
    pieces = [(k_ref[...], v_ref[...], e_ref)]
    grad_keys, grad_values = back_rows(pieces, do_ref, wq_ref, wdo_ref, dq_ref)
    dk_ref[...] = grad_keys.astype(BF16)
    dv_ref[...] = grad_values.astype(BF16)


def combine_kernel(mine_ref, pair_ref, left_ref, right_ref, across_ref, above_ref, below_ref, own_ref):
    y_high, up = y_place()

    def arrived(at):
        rows = half_rows(at)
        return left_ref[rows, :].astype(F32) + right_ref[rows, :].astype(F32)

    def leaving(at, beside):
        rows = half_rows(at)
        return (mine_ref[rows, :] + pair_ref[rows, :].astype(F32) + arrived(beside)).astype(BF16)

    across_ref[...] = leaving(0, 1 - y_high)
    above_ref[...] = leaving(1 + up, 2 + up)
    below_ref[...] = leaving(2 - up, 3 - up)
    own_ref[...] = arrived(y_high)


def finish_kernel(own_ref, mine_ref, pair_ref, across_ref, above_ref, below_ref, dk_ref, dv_ref):
    total = own_ref[...] + mine_ref[...]
    for ref in (pair_ref, across_ref, above_ref, below_ref):
        total = total + ref[...].astype(F32)
    dk_ref[...] = total[:, :HD].astype(BF16)
    dv_ref[...] = total[:, HD:].astype(BF16)


def params(mib):
    return pltpu.CompilerParams(vmem_limit_bytes=mib * 1024 * 1024)


VMEM = pl.BlockSpec(memory_space=pltpu.VMEM)
HBM = pl.BlockSpec(memory_space=pltpu.HBM)
SMEM = pl.BlockSpec(memory_space=pltpu.SMEM)
UNREAD = pl.BlockSpec(memory_space=pl.ANY)


def whole(dims):
    return pl.BlockSpec(dims, lambda *_: (0,) * len(dims))


def cost(rows, matmuls, exps, stored):
    return pl.CostEstimate(
        flops=2 * rows * WIDE * HD * matmuls,
        bytes_accessed=rows * WIDE * 2 * stored,
        transcendentals=rows * WIDE * exps,
    )


def shape(dims, dtype=F32):
    return jax.ShapeDtypeStruct(dims, dtype)


def pack(keys, values):
    return pl.pallas_call(
        pack_kernel,
        in_specs=[HBM] * 2,
        out_specs=(VMEM,) * 2,
        out_shape=(shape((ROWS, 2 * HD), BF16),) * 2,
        scratch_shapes=[pltpu.SemaphoreType.DMA((6,))],
        compiler_params=params(60),
        name="pack",
    )(keys, values)


def self_scores(query, key_comp, out, d_out, steps):
    return pl.pallas_call(
        self_scores_kernel,
        in_specs=[HBM] * 5,
        out_specs=(VMEM,) * 7,
        scratch_shapes=[
            pltpu.VMEM((CTOK, GROUP * HD), BF16),
            pltpu.VMEM((CTOK, HD), BF16),
            pltpu.VMEM((CTOK, GROUP * HD), BF16),
            pltpu.VMEM((CTOK, GROUP * HD), BF16),
            pltpu.VMEM((1, CTOK), jnp.int32),
            pltpu.SemaphoreType.DMA((5,)),
        ],
        out_shape=(
            shape((CTOK, WIDE), BF16),
            shape((1,) + STAT),
            shape(STAT),
            shape(STAT),
            shape((WIDE, 2 * HD), BF16),
            shape((WIDE, 2 * HD), BF16),
            shape((8, HD)),
        ),
        compiler_params=params(57),
        cost_estimate=cost(CTOK, 1, 1, 1),
        name="self_scores",
    )(query, key_comp, out, d_out, steps)


def prompt_scores(norm, query, own, pair, row, m, l, split=(ROWS, ROWS), d_out=None, tops=(), blocks=(), earlier=()):
    count = 2 * len(split)
    operands = [norm, query, own, pair, m, l] + ([d_out, *tops, *blocks] if blocks else [])
    out_shape = tuple(shape((rows, WIDE), BF16) for rows in split) * 2
    out_shape += (shape((2,) + STAT), shape(STAT), shape(STAT))
    if blocks:
        out_shape += (shape((WIDE, HD), BF16),) * 2 + tuple(shape(block.shape, BF16) for block in blocks)
    first_in, first_out = len(operands) - len(blocks), len(out_shape) - len(blocks)
    results = pl.pallas_call(
        functools.partial(prompt_scores_kernel, len(split), row, earlier),
        in_specs=[VMEM] * len(operands),
        out_specs=(VMEM,) * len(out_shape),
        out_shape=out_shape,
        input_output_aliases={first_in + at: first_out + at for at in range(len(blocks))},
        compiler_params=params(16),
        cost_estimate=cost(2 * TILE, 1, 1, 1),
        name="prompt_scores",
    )(*operands)
    return results[:count], *results[count:]


def prompt_back(shared, dq, kvs, tiles, es, outs, after=(), l=None):
    first, last = dq is None, l is not None
    operands = [*shared] + ([] if first else [dq]) + ([l] if last else []) + [*kvs, *es]
    out_shape = tuple(shape((rows, 2 * HD), dtype) for rows, dtype in outs)
    out_shape += (shape((CTOK, GROUP * HD), BF16) if last else shape(DQ),)
    return pl.pallas_call(
        functools.partial(prompt_back_kernel, first, last, tiles, len(kvs), len(es), len(after)),
        in_specs=[VMEM] * len(operands) + [UNREAD] * len(after),
        out_specs=(VMEM,) * len(out_shape),
        out_shape=out_shape,
        scratch_shapes=[pltpu.VMEM(DQ, F32)] if last else [],
        compiler_params=params(20),
        cost_estimate=cost(sum(e.shape[0] for e in es), 4, 0, 1),
        name="prompt_back",
    )(*operands, *after)


def self_back(shared, dq, key_comp, value_comp, e):
    return pl.pallas_call(
        self_back_kernel,
        in_specs=[VMEM] * 7,
        out_specs=(VMEM,) * 3,
        out_shape=(shape((CTOK, HD), BF16), shape((CTOK, HD), BF16), shape(DQ)),
        compiler_params=params(20),
        cost_estimate=cost(CTOK, 4, 0, 1),
        name="self_back",
    )(*shared, dq, key_comp, value_comp, e)


def combine(*arrays):
    return pl.pallas_call(
        combine_kernel,
        in_specs=[VMEM] * 4,
        out_specs=(VMEM,) * 4,
        out_shape=(shape((HALF, 2 * HD), BF16),) * 3 + (shape((HALF, 2 * HD)),),
        compiler_params=params(6),
        name="combine",
    )(*arrays)


def finish(*arrays):
    return pl.pallas_call(
        finish_kernel,
        in_specs=[VMEM] * 6,
        out_specs=(VMEM,) * 2,
        out_shape=(shape((HALF, HD), BF16),) * 2,
        compiler_params=params(6),
        name="finish",
    )(*arrays)


def behind(result, *blocks):
    return lax.optimization_barrier(blocks + (result,))[:-1]


def shards(query, key_comp, value_comp, key_prompt, value_prompt, out, d_out, steps):
    here, turned = pack(key_prompt, value_prompt)

    here_y = send(here, dy=1)
    left = send(here, dx=1)
    right = send(here, dx=-1)
    e_self, mt_self, m, l, query, d_out, norm = self_scores(query, key_comp, out, d_out, steps.reshape(1, CTOK))
    here_y, left, right = behind(m, here_y, left, right)
    far = send(left, dx=1)
    near = stack([turned, here_y, left, right])
    near_pair = send(near, dc=1)
    left_y = send(left, dy=1)
    right_y = send(right, dy=-1)
    split = (HALF, HALF, ROWS)
    e_near, mt_near, m, l = prompt_scores(norm, query, near, near_pair, 0, m, l, split)
    (far,) = behind(m, far)
    far_y = send(far, dy=-1)
    e_beside, mt_beside, m, l = prompt_scores(norm, query, near, near_pair, TILE, m, l)
    left_y, right_y = behind(m, left_y, right_y)
    corners = stack([left_y, right_y])
    corners_pair = send(corners, dc=1)
    (far_y,) = behind(m, far_y)
    opposite = stack([far, far_y])
    opposite_pair = send(opposite, dc=1)
    e_corners, mt_corners, m, l = prompt_scores(norm, query, corners, corners_pair, 0, m, l)
    (opposite_pair,) = behind(m, opposite_pair)
    blocks = [*e_near, *e_beside, *e_corners, e_self]
    tops = [mt_near, mt_beside, mt_corners, mt_self]
    earlier = [(0, at // 3) for at in range(6)] + [(top, at // 2) for top in (1, 2) for at in range(4)] + [(3, 0)]
    e_far, _, m, l, wq, wdo, *blocks = prompt_scores(
        norm, query, opposite, opposite_pair, 0, m, l, d_out=d_out, tops=tops, blocks=blocks, earlier=earlier
    )
    e_near, e_beside, e_corners, e_self = blocks[:6], blocks[6:10], blocks[10:14], blocks[14]

    shared = d_out, wq, wdo
    add = lambda *parts: sum(rows.astype(F32) for rows in parts)
    both = [(TILE, F32), (TILE, BF16)]
    tiles = [([(1, 0, 2), (1, ROWS, 3)], [1]), ([(0, 0, 0), (0, ROWS, 1)], [0])]
    mine, theirs, dq = prompt_back(shared, None, [opposite, opposite_pair], tiles, e_far, both)
    pair_far = send(theirs, dc=1)
    total = add(mine, pair_far).astype(BF16)
    far_right = send(total[:ROWS], dx=1)
    far_left = send(total[ROWS:], dx=-1)

    def side(at, dq, after):
        row = at * ROWS
        beside = TILE + row
        tiles = [
            ([(1, beside, 1), (3, row, 3)], [1]),
            ([(0, beside, 0), (2, row, 2)], [0]),
        ]
        es = [e_beside[at], e_beside[2 + at], e_corners[at], e_corners[2 + at]]
        kvs = [near, near_pair, corners, corners_pair]
        return prompt_back(shared, dq, kvs, tiles, es, both, after)

    mine_left, theirs, dq = side(0, dq, ())
    pair_left = send(theirs, dc=1)
    mine_right, theirs, dq = side(1, dq, (far_left, far_right))
    pair_right = send(theirs, dc=1)
    (pair_left,) = behind(theirs, pair_left)
    total = stack([add(mine_left[:ROWS], pair_left[:ROWS]), add(mine_left[ROWS:], pair_left[ROWS:], far_left)])
    from_right = send(total.astype(BF16), dx=-1)
    total = stack([add(mine_right[:ROWS], pair_right[:ROWS], far_right), add(mine_right[ROWS:], pair_right[ROWS:])])
    from_left = send(total.astype(BF16), dx=1)

    kvs = [near, near_pair]
    tiles = [([(1, 0, 1), (1, ROWS, 3)], [1]), ([(0, 0, 0), (0, ROWS, 2)], [0])]
    es = [e_near[0], e_near[3], e_near[2], e_near[5]]
    outs = [(HALF + ROWS, F32), (HALF + ROWS, BF16)]
    mine, theirs, dq = prompt_back(shared, dq, kvs, tiles, es, outs, (pair_right,))
    pair = send(theirs, dc=1)
    grad_key_comp, grad_value_comp, dq = self_back(shared, dq, key_comp, value_comp, e_self)
    pair, from_left, from_right = behind(grad_key_comp, pair, from_left, from_right)
    across, above, below, own = combine(mine, pair, from_left, from_right)
    across = send(across, dy=2)
    above = send(above, dy=1)
    below = send(below, dy=-1)
    tiles = [([(0, HALF, 0), (1, HALF, 1)], [0, 1])]
    es = [e_near[1], e_near[4]]
    outs = [(HALF, F32), (HALF, BF16)]
    mine, theirs, grad_query = prompt_back(shared, dq, kvs, tiles, es, outs, (own,), l)
    pair = send(theirs, dc=1)
    across, above, below = behind(mine, across, above, below)
    grad_key_prompt, grad_value_prompt = finish(own, mine, pair, across, above, below)
    return (grad_query, grad_key_comp, grad_value_comp, grad_key_prompt, grad_value_prompt)


def solution(mesh):
    rows = P(("blk", "req"), "head")
    return jax.shard_map(
        shards,
        mesh=mesh,
        in_specs=(rows, rows, rows, P("blk", "head"), P("blk", "head"), rows, rows, P(("blk", "req"))),
        out_specs=(rows,) * 5,
        check_vma=False,
    )
```

```python
import functools

import jax
import jax.numpy as jnp
from jax import lax
from jax.experimental import pallas as pl
from jax.experimental.pallas import tpu as pltpu
from jax.sharding import PartitionSpec as P

HD = 128
GROUP = 8
CTOK = 256
ROWS = 384
TILE = 2 * ROWS
HALF = ROWS // 2
X, Y, CORES = 4, 4, 2
SCALE = HD ** (-0.5)
EXP2_SCALE = SCALE * 1.4426950408889634
PLAIN = 60.0
STAT = (GROUP, CTOK)
WIDE = GROUP * CTOK
DQ = (HD, WIDE)
HEADS = 8
CHUNK = 256
F32 = jnp.float32
BF16 = jnp.bfloat16


def place(x, y, core):
    return ((x * 2 + y % 2) * CORES + core) * 2 + y // 2


def send(block, dx=0, dy=0, dc=0):
    route = []
    for x in range(X):
        for y in range(Y):
            for core in range(CORES):
                there = place((x + dx) % X, (y + dy) % Y, core ^ dc)
                route.append((place(x, y, core), there))
    return lax.ppermute(block, ("blk", "req"), route)


def part(ref, n, width):
    return ref[:, n * width : (n + 1) * width]


def dot(a, b, contract):
    return lax.dot_general(a, b, (contract, ((), ())), preferred_element_type=F32)


def largest_norm(rows):
    wide = rows.astype(F32)
    return jnp.max(jnp.sum(wide * wide, axis=1, keepdims=True))


def within(query_norm, key_norm):
    return query_norm * key_norm * (EXP2_SCALE * EXP2_SCALE) <= PLAIN * PLAIN


def put(e, n, parts, first=0):
    low = e.astype(BF16)
    start = 0
    for ref in parts:
        begin, end = max(start, first), min(start + ref.shape[0], first + e.shape[0])
        if begin < end:
            ref[begin - start : end - start, n * CTOK : (n + 1) * CTOK] = low[begin - first : end - first]
        start += ref.shape[0]


def plain_tile(keys, q_ref, visible, l_ref, parts, mt_ref, tile):
    mt_ref[tile] = jnp.zeros(STAT, F32)
    keys = jnp.concatenate([keys, keys], axis=1)
    for n in range(GROUP):
        total = l_ref[n : n + 1, :]
        for first in range(0, keys.shape[0], CHUNK):
            e = jnp.exp2(dot(keys[first : first + CHUNK], q_ref[n * CTOK : (n + 1) * CTOK, :], ((1,), (1,))))
            if visible is not None:
                e = jnp.where(visible, e, 0.0)
            total = total + jnp.sum(e, axis=0, keepdims=True)
            put(e, n, parts, first)
        l_ref[n : n + 1, :] = total


def general_tile(keys, q_ref, visible, m_ref, l_ref, parts, mt_ref, tile):
    keys = jnp.concatenate([keys, keys], axis=1)

    def one_head(n, carry):
        columns = pl.ds(pl.multiple_of(n * CTOK, CTOK), CTOK)
        row = pl.ds(n, 1)
        scores = dot(keys, q_ref[columns, :], ((1,), (1,)))
        if visible is not None:
            scores = jnp.where(visible, scores, -jnp.inf)
        m_old = m_ref[row, :]
        m_new = jnp.maximum(m_old, jnp.max(scores, axis=0, keepdims=True))
        e = jnp.exp2(scores - m_new)
        total = jnp.sum(e, axis=0, keepdims=True)
        l_ref[row, :] = l_ref[row, :] * jnp.exp2(m_old - m_new) + total
        m_ref[row, :] = m_new
        mt_ref[tile, row, :] = m_new
        start = 0
        for ref in parts:
            ref[:, columns] = e[start : start + ref.shape[0]].astype(BF16)
            start += ref.shape[0]
        return carry

    lax.fori_loop(0, GROUP, one_head, 0)


def bring_to(m_ref, members):
    change = functools.reduce(jnp.maximum, [jnp.abs(mt_ref[tile] - m_ref[...]) for _, mt_ref, tile in members])

    @pl.when(jnp.max(change) != 0.0)
    def _():
        for ref, mt_ref, tile in members:
            log_change = mt_ref[tile] - m_ref[...]
            factor = jnp.exp2(jnp.concatenate([log_change[n : n + 1] for n in range(GROUP)], axis=1))

            def some_rows(step, carry, ref=ref, factor=factor):
                rows = pl.ds(pl.multiple_of(step * 16, 16), 16)
                ref[rows, :] = (ref[rows, :].astype(F32) * factor).astype(BF16)
                return carry

            lax.fori_loop(0, ref.shape[0] // 16, some_rows, 0)


def y_place():
    y_high = lax.axis_index("req")
    y_low = lax.rem(lax.div(lax.axis_index("blk"), CORES), 2)
    return y_high, jnp.where(y_low == 0, y_high, 1 - y_high)


def half_rows(at):
    return pl.ds(pl.multiple_of(at * HALF, HALF), HALF)


def fetch(pairs, sems):
    copies = [pltpu.make_async_copy(far, near, sems.at[at]) for at, (far, near) in enumerate(pairs)]
    for copy in copies:
        copy.start()
    for copy in copies:
        copy.wait()


def pack_kernel(k_hbm, v_hbm, kv_ref, turned_ref, sems):
    y_high, _ = y_place()
    pairs = []
    for far, columns in ((k_hbm, slice(0, HD)), (v_hbm, slice(HD, 2 * HD))):
        pairs.append((far, kv_ref.at[:, columns]))
        pairs.append((far.at[half_rows(1 - y_high), :], turned_ref.at[:HALF, columns]))
        pairs.append((far.at[half_rows(y_high), :], turned_ref.at[HALF:, columns]))
    fetch(pairs, sems)


def self_scores_kernel(
    q_hbm, k_hbm, out_hbm, do_hbm, step_hbm, *refs
):
    e_ref, mt_ref, m_ref, l_ref, q_out, do_out, norm_ref, q_ref, k_ref, out_ref, do_ref, step_ref, sems = refs
    fetch(
        [(k_hbm, k_ref), (step_hbm, step_ref), (q_hbm, q_ref), (do_hbm, do_ref), (out_hbm, out_ref)], sems
    )
    keys = k_ref[...]
    step = jnp.broadcast_to(step_ref[...].astype(F32), (CTOK, CTOK))
    visible = step.T <= step
    lane = lax.broadcasted_iota(jnp.int32, (CTOK, HD), 1)
    norm = None
    for n in range(GROUP):
        do_n = part(do_ref, n, HD)
        left = jnp.sum(do_n.astype(F32) * part(out_ref, n, HD).astype(F32), axis=1, keepdims=True)
        terms = jnp.zeros((CTOK, HD), F32)
        for place_at in range(3):
            term = left.astype(BF16).astype(F32)
            terms = jnp.where(lane == place_at, -term, terms)
            left = left - term
        do_out[n * CTOK : (n + 1) * CTOK, :HD] = do_n
        do_out[n * CTOK : (n + 1) * CTOK, HD:] = terms.astype(BF16)
        scaled = part(q_ref, n, HD).astype(F32) * EXP2_SCALE
        high = scaled.astype(BF16)
        q_out[n * CTOK : (n + 1) * CTOK, :HD] = high
        q_out[n * CTOK : (n + 1) * CTOK, HD:] = (scaled - high.astype(F32)).astype(BF16)
        rows = largest_norm(part(q_ref, n, HD))
        norm = rows if norm is None else jnp.maximum(norm, rows)
    norm_ref[...] = jnp.full(norm_ref.shape, norm, F32)
    l_ref[...] = jnp.zeros(STAT, F32)
    m_ref[...] = jnp.zeros(STAT, F32)
    plain_tile(keys, q_out, visible, l_ref, [e_ref], mt_ref, 0)

    @pl.when(jnp.logical_not(within(norm, largest_norm(keys))))
    def _():
        l_ref[...] = jnp.zeros(STAT, F32)
        m_ref[...] = jnp.full(STAT, -1e30, F32)
        general_tile(keys, q_out, visible, m_ref, l_ref, [e_ref], mt_ref, 0)


def prompt_scores_kernel(pieces, rows, earlier, *refs):
    tiles = len(rows)
    norm_ref, q_ref, m_in, l_in, *refs = refs
    kv_refs, refs = refs[:tiles], refs[tiles:]
    if earlier:
        do_ref, *refs = refs
        tops = max(top for top, _ in earlier) + 1
        mt_refs, refs = refs[:tops], refs[tops + len(earlier) :]
    e_refs, refs = refs[: tiles * pieces], refs[tiles * pieces :]
    mt_ref, m_ref, l_ref, *refs = refs
    m_ref[...] = m_in[...]
    l_ref[...] = l_in[...]
    for tile, (kv_ref, row) in enumerate(zip(kv_refs, rows)):
        keys = kv_ref[row : row + TILE, :HD]
        parts = e_refs[tile * pieces : (tile + 1) * pieces]
        l_old = l_ref[...]
        plain = within(jnp.max(norm_ref[...]), largest_norm(keys)) & (jnp.max(jnp.abs(m_ref[...])) == 0.0)
        plain_tile(keys, q_ref, None, l_ref, parts, mt_ref, tile)

        @pl.when(jnp.logical_not(plain))
        def _():
            l_ref[...] = l_old
            general_tile(keys, q_ref, None, m_ref, l_ref, parts, mt_ref, tile)

    if earlier:
        wq_ref, wdo_ref, *blocks = refs
        for n in range(GROUP):
            weight = jnp.broadcast_to(1.0 / l_ref[n : n + 1, :], (HD, CTOK)).T
            heads = slice(n * CTOK, (n + 1) * CTOK)
            q_n = (q_ref[heads, :HD].astype(F32) + q_ref[heads, HD:].astype(F32)) * (1.0 / EXP2_SCALE)
            wq_ref[heads, :] = (q_n * weight).astype(BF16)
            wdo_ref[heads, :] = (do_ref[heads, :HD].astype(F32) * weight).astype(BF16)
        members = [(ref, mt_refs[top], tile) for ref, (top, tile) in zip(blocks, earlier)]
        members += [(ref, mt_ref, at // pieces) for at, ref in enumerate(e_refs)]
        bring_to(m_ref, members)


def stack(parts):
    return parts[0] if len(parts) == 1 else jnp.concatenate(parts, axis=0)


def back_rows(pieces, do_ref, wq_ref, wdo_ref, dq_ref):
    keys = stack([keys for keys, _, _ in pieces])
    values = stack([values for _, values, _ in pieces])
    lane = lax.broadcasted_iota(jnp.int32, values.shape, 1)
    ones = jnp.where(lane < 3, 1.0, 0.0).astype(BF16)
    values = jnp.concatenate([values, ones], axis=1)
    keys_t = keys.T
    grad_keys = grad_values = None
    for n in range(0, GROUP, HEADS):
        columns = slice(n * CTOK, (n + HEADS) * CTOK)
        e = stack([e_ref[:, columns] for _, _, e_ref in pieces])
        grad_prob = dot(values, do_ref[columns, :], ((1,), (1,)))
        part_value = dot(e, wdo_ref[columns, :], ((1,), (0,)))
        grad_score = e * grad_prob.astype(BF16)
        part_key = dot(grad_score, wq_ref[columns, :], ((1,), (0,)))
        dq_ref[:, columns] += dot(keys_t, grad_score, ((1,), (0,)))
        grad_keys = part_key if n == 0 else grad_keys + part_key
        grad_values = part_value if n == 0 else grad_values + part_value
    return grad_keys * SCALE, grad_values


def prompt_back_kernel(first, last, tiles, sources, blocks, unread, *refs):
    do_ref, wq_ref, wdo_ref, *refs = refs
    if not first:
        dq_in, *refs = refs
    if last:
        l_ref, *refs = refs
    kv_refs, refs = refs[:sources], refs[sources:]
    e_refs, refs = refs[:blocks], refs[blocks + unread :]
    *out_refs, dq_ref = refs
    if last:
        *out_refs, query_ref = out_refs
    dq_ref[...] = jnp.zeros_like(dq_ref) if first else dq_in[...]
    for members, outs in tiles:
        pieces = []
        for source, row, block in members:
            e_ref = e_refs[block]
            rows = slice(row, row + e_ref.shape[0])
            kv_ref = kv_refs[source]
            pieces.append((kv_ref[rows, :HD], kv_ref[rows, HD:], e_ref))
        grad_keys, grad_values = back_rows(pieces, do_ref, wq_ref, wdo_ref, dq_ref)
        start = 0
        for at in outs:
            ref = out_refs[at]
            rows = slice(start, start + ref.shape[0])
            ref[:, :HD] = grad_keys[rows].astype(ref.dtype)
            ref[:, HD:] = grad_values[rows].astype(ref.dtype)
            start += ref.shape[0]
    if last:
        for n in range(GROUP):
            weight = SCALE / l_ref[n : n + 1, :]
            query_ref[:, n * HD : (n + 1) * HD] = (part(dq_ref, n, CTOK) * weight).T.astype(BF16)


def self_back_kernel(do_ref, wq_ref, wdo_ref, dq_in, k_ref, v_ref, e_ref, dk_ref, dv_ref, dq_ref):
    dq_ref[...] = dq_in[...]
    pieces = [(k_ref[...], v_ref[...], e_ref)]
    grad_keys, grad_values = back_rows(pieces, do_ref, wq_ref, wdo_ref, dq_ref)
    dk_ref[...] = grad_keys.astype(BF16)
    dv_ref[...] = grad_values.astype(BF16)


def combine_kernel(mine_ref, pair_ref, left_ref, right_ref, across_ref, above_ref, below_ref, own_ref):
    y_high, up = y_place()

    def arrived(at):
        rows = half_rows(at)
        return left_ref[rows, :].astype(F32) + right_ref[rows, :].astype(F32)

    def leaving(at, beside):
        rows = half_rows(at)
        return (mine_ref[rows, :] + pair_ref[rows, :].astype(F32) + arrived(beside)).astype(BF16)

    across_ref[...] = leaving(0, 1 - y_high)
    above_ref[...] = leaving(1 + up, 2 + up)
    below_ref[...] = leaving(2 - up, 3 - up)
    own_ref[...] = arrived(y_high)


def finish_kernel(own_ref, mine_ref, pair_ref, across_ref, above_ref, below_ref, dk_ref, dv_ref):
    total = own_ref[...] + mine_ref[...]
    for ref in (pair_ref, across_ref, above_ref, below_ref):
        total = total + ref[...].astype(F32)
    dk_ref[...] = total[:, :HD].astype(BF16)
    dv_ref[...] = total[:, HD:].astype(BF16)


def params(mib):
    return pltpu.CompilerParams(vmem_limit_bytes=mib * 1024 * 1024)


VMEM = pl.BlockSpec(memory_space=pltpu.VMEM)
HBM = pl.BlockSpec(memory_space=pltpu.HBM)
SMEM = pl.BlockSpec(memory_space=pltpu.SMEM)
UNREAD = pl.BlockSpec(memory_space=pl.ANY)


def whole(dims):
    return pl.BlockSpec(dims, lambda *_: (0,) * len(dims))


def cost(rows, matmuls, exps, stored):
    return pl.CostEstimate(
        flops=2 * rows * WIDE * HD * matmuls,
        bytes_accessed=rows * WIDE * 2 * stored,
        transcendentals=rows * WIDE * exps,
    )


def shape(dims, dtype=F32):
    return jax.ShapeDtypeStruct(dims, dtype)


def pack(keys, values):
    return pl.pallas_call(
        pack_kernel,
        in_specs=[HBM] * 2,
        out_specs=(VMEM,) * 2,
        out_shape=(shape((ROWS, 2 * HD), BF16),) * 2,
        scratch_shapes=[pltpu.SemaphoreType.DMA((6,))],
        compiler_params=params(60),
        name="pack",
    )(keys, values)


def self_scores(query, key_comp, out, d_out, steps):
    return pl.pallas_call(
        self_scores_kernel,
        in_specs=[HBM] * 5,
        out_specs=(VMEM,) * 7,
        scratch_shapes=[
            pltpu.VMEM((CTOK, GROUP * HD), BF16),
            pltpu.VMEM((CTOK, HD), BF16),
            pltpu.VMEM((CTOK, GROUP * HD), BF16),
            pltpu.VMEM((CTOK, GROUP * HD), BF16),
            pltpu.VMEM((1, CTOK), jnp.int32),
            pltpu.SemaphoreType.DMA((5,)),
        ],
        out_shape=(
            shape((CTOK, WIDE), BF16),
            shape((1,) + STAT),
            shape(STAT),
            shape(STAT),
            shape((WIDE, 2 * HD), BF16),
            shape((WIDE, 2 * HD), BF16),
            shape((8, HD)),
        ),
        compiler_params=params(57),
        cost_estimate=cost(CTOK, 1, 1, 1),
        name="self_scores",
    )(query, key_comp, out, d_out, steps)


def prompt_scores(norm, query, m, l, kvs, rows, split=(ROWS, ROWS), d_out=None, tops=(), blocks=(), earlier=()):
    tiles = len(kvs)
    count = tiles * len(split)
    operands = [norm, query, m, l, *kvs] + ([d_out, *tops, *blocks] if blocks else [])
    out_shape = tuple(shape((count, WIDE), BF16) for count in split) * tiles
    out_shape += (shape((tiles,) + STAT), shape(STAT), shape(STAT))
    if blocks:
        out_shape += (shape((WIDE, HD), BF16),) * 2 + tuple(shape(block.shape, BF16) for block in blocks)
    first_in, first_out = len(operands) - len(blocks), len(out_shape) - len(blocks)
    results = pl.pallas_call(
        functools.partial(prompt_scores_kernel, len(split), rows, earlier),
        in_specs=[VMEM] * len(operands),
        out_specs=(VMEM,) * len(out_shape),
        out_shape=out_shape,
        input_output_aliases={first_in + at: first_out + at for at in range(len(blocks))},
        compiler_params=params(16),
        cost_estimate=cost(tiles * TILE, 1, 1, 1),
        name="prompt_scores",
    )(*operands)
    return results[:count], *results[count:]


def prompt_back(shared, dq, kvs, tiles, es, outs, after=(), l=None):
    first, last = dq is None, l is not None
    operands = [*shared] + ([] if first else [dq]) + ([l] if last else []) + [*kvs, *es]
    out_shape = tuple(shape((rows, 2 * HD), dtype) for rows, dtype in outs)
    out_shape += (shape((CTOK, GROUP * HD), BF16) if last else shape(DQ),)
    return pl.pallas_call(
        functools.partial(prompt_back_kernel, first, last, tiles, len(kvs), len(es), len(after)),
        in_specs=[VMEM] * len(operands) + [UNREAD] * len(after),
        out_specs=(VMEM,) * len(out_shape),
        out_shape=out_shape,
        scratch_shapes=[pltpu.VMEM(DQ, F32)] if last else [],
        compiler_params=params(20),
        cost_estimate=cost(sum(e.shape[0] for e in es), 4, 0, 1),
        name="prompt_back",
    )(*operands, *after)


def self_back(shared, dq, key_comp, value_comp, e):
    return pl.pallas_call(
        self_back_kernel,
        in_specs=[VMEM] * 7,
        out_specs=(VMEM,) * 3,
        out_shape=(shape((CTOK, HD), BF16), shape((CTOK, HD), BF16), shape(DQ)),
        compiler_params=params(20),
        cost_estimate=cost(CTOK, 4, 0, 1),
        name="self_back",
    )(*shared, dq, key_comp, value_comp, e)


def combine(*arrays):
    return pl.pallas_call(
        combine_kernel,
        in_specs=[VMEM] * 4,
        out_specs=(VMEM,) * 4,
        out_shape=(shape((HALF, 2 * HD), BF16),) * 3 + (shape((HALF, 2 * HD)),),
        compiler_params=params(6),
        name="combine",
    )(*arrays)


def finish(*arrays):
    return pl.pallas_call(
        finish_kernel,
        in_specs=[VMEM] * 6,
        out_specs=(VMEM,) * 2,
        out_shape=(shape((HALF, HD), BF16),) * 2,
        compiler_params=params(6),
        name="finish",
    )(*arrays)


def behind(result, *blocks):
    return lax.optimization_barrier(blocks + (result,))[:-1]


def shards(query, key_comp, value_comp, key_prompt, value_prompt, out, d_out, steps):
    here, turned = pack(key_prompt, value_prompt)

    here_y = send(here, dy=1)
    left = send(here, dx=1)
    right = send(here, dx=-1)
    e_self, mt_self, m, l, query, d_out, norm = self_scores(query, key_comp, out, d_out, steps.reshape(1, CTOK))
    here_y, left, right = behind(m, here_y, left, right)
    far = send(left, dx=1)
    near = stack([turned, here_y, left, right])
    near_pair = send(near, dc=1)
    left_y = send(left, dy=1)
    right_y = send(right, dy=-1)
    split = (HALF, HALF, ROWS)
    e_near, mt_near, m, l = prompt_scores(norm, query, m, l, [near, near_pair], (0, 0), split)
    (far,) = behind(m, far)
    far_y = send(far, dy=-1)
    left_y, right_y = behind(far, left_y, right_y)
    corners = stack([left_y, right_y])
    kvs = [near, near_pair, corners]
    e_beside, mt_beside, m, l = prompt_scores(norm, query, m, l, kvs, (TILE, TILE, 0))
    (far_y,) = behind(m, far_y)
    corners_pair = send(behind(m, corners)[0], dc=1)
    opposite = stack([far, far_y])
    opposite_pair = send(opposite, dc=1)
    e_others, mt_others, m, l = prompt_scores(norm, query, m, l, [corners_pair], (0,))
    (opposite_pair,) = behind(m, opposite_pair)
    blocks = [*e_near, *e_beside, *e_others, e_self]
    tops = [mt_near, mt_beside, mt_others, mt_self]
    earlier = [(0, at // 3) for at in range(6)] + [(1, at // 2) for at in range(6)] + [(2, 0), (2, 0), (3, 0)]
    kvs = [opposite, opposite_pair]
    e_far, _, m, l, wq, wdo, *blocks = prompt_scores(
        norm, query, m, l, kvs, (0, 0), d_out=d_out, tops=tops, blocks=blocks, earlier=earlier
    )
    e_near, e_beside, e_corners, e_self = blocks[:6], blocks[6:10], blocks[10:14], blocks[14]

    shared = d_out, wq, wdo
    add = lambda *parts: sum(rows.astype(F32) for rows in parts)
    both = [(TILE, F32), (TILE, BF16)]
    tiles = [([(1, 0, 2), (1, ROWS, 3)], [1]), ([(0, 0, 0), (0, ROWS, 1)], [0])]
    mine, theirs, dq = prompt_back(shared, None, [opposite, opposite_pair], tiles, e_far, both)
    pair_far = send(theirs, dc=1)
    total = add(mine, pair_far).astype(BF16)
    far_right = send(total[:ROWS], dx=1)
    far_left = send(total[ROWS:], dx=-1)

    def side(at, dq, after):
        row = at * ROWS
        beside = TILE + row
        tiles = [
            ([(1, beside, 1), (3, row, 3)], [1]),
            ([(0, beside, 0), (2, row, 2)], [0]),
        ]
        es = [e_beside[at], e_beside[2 + at], e_corners[at], e_corners[2 + at]]
        kvs = [near, near_pair, corners, corners_pair]
        return prompt_back(shared, dq, kvs, tiles, es, both, after)

    mine_left, theirs, dq = side(0, dq, ())
    pair_left = send(theirs, dc=1)
    mine_right, theirs, dq = side(1, dq, (far_left, far_right))
    pair_right = send(theirs, dc=1)
    (pair_left,) = behind(theirs, pair_left)
    total = stack([add(mine_left[:ROWS], pair_left[:ROWS]), add(mine_left[ROWS:], pair_left[ROWS:], far_left)])
    from_right = send(total.astype(BF16), dx=-1)
    total = stack([add(mine_right[:ROWS], pair_right[:ROWS], far_right), add(mine_right[ROWS:], pair_right[ROWS:])])
    from_left = send(total.astype(BF16), dx=1)

    kvs = [near, near_pair]
    tiles = [([(1, 0, 1), (1, ROWS, 3)], [1]), ([(0, 0, 0), (0, ROWS, 2)], [0])]
    es = [e_near[0], e_near[3], e_near[2], e_near[5]]
    outs = [(HALF + ROWS, F32), (HALF + ROWS, BF16)]
    mine, theirs, dq = prompt_back(shared, dq, kvs, tiles, es, outs, (pair_right,))
    pair = send(theirs, dc=1)
    grad_key_comp, grad_value_comp, dq = self_back(shared, dq, key_comp, value_comp, e_self)
    pair, from_left, from_right = behind(grad_key_comp, pair, from_left, from_right)
    across, above, below, own = combine(mine, pair, from_left, from_right)
    across = send(across, dy=2)
    above = send(above, dy=1)
    below = send(below, dy=-1)
    tiles = [([(0, HALF, 0), (1, HALF, 1)], [0, 1])]
    es = [e_near[1], e_near[4]]
    outs = [(HALF, F32), (HALF, BF16)]
    mine, theirs, grad_query = prompt_back(shared, dq, kvs, tiles, es, outs, (own,), l)
    pair = send(theirs, dc=1)
    across, above, below = behind(mine, across, above, below)
    grad_key_prompt, grad_value_prompt = finish(own, mine, pair, across, above, below)
    return (grad_query, grad_key_comp, grad_value_comp, grad_key_prompt, grad_value_prompt)


def solution(mesh):
    rows = P(("blk", "req"), "head")
    return jax.shard_map(
        shards,
        mesh=mesh,
        in_specs=(rows, rows, rows, P("blk", "head"), P("blk", "head"), rows, rows, P(("blk", "req"))),
        out_specs=(rows,) * 5,
        check_vma=False,
    )
```

```python
import functools

import jax
import jax.numpy as jnp
from jax import lax
from jax.experimental import pallas as pl
from jax.experimental.pallas import tpu as pltpu
from jax.sharding import PartitionSpec as P

HD = 128
GROUP = 8
CTOK = 256
ROWS = 384
TILE = 2 * ROWS
HALF = ROWS // 2
X, Y, CORES = 4, 4, 2
SCALE = HD ** (-0.5)
EXP2_SCALE = SCALE * 1.4426950408889634
PLAIN = 60.0
STAT = (GROUP, CTOK)
WIDE = GROUP * CTOK
DQ = (HD, WIDE)
HEADS = 8
CHUNK = 4
F32 = jnp.float32
BF16 = jnp.bfloat16


def place(x, y, core):
    return ((x * 2 + y % 2) * CORES + core) * 2 + y // 2


def send(block, dx=0, dy=0, dc=0):
    route = []
    for x in range(X):
        for y in range(Y):
            for core in range(CORES):
                there = place((x + dx) % X, (y + dy) % Y, core ^ dc)
                route.append((place(x, y, core), there))
    return lax.ppermute(block, ("blk", "req"), route)


def part(ref, n, width):
    return ref[:, n * width : (n + 1) * width]


def dot(a, b, contract):
    return lax.dot_general(a, b, (contract, ((), ())), preferred_element_type=F32)


def largest_norm(rows):
    wide = rows.astype(F32)
    return jnp.max(jnp.sum(wide * wide, axis=1, keepdims=True))


def within(query_norm, key_norm):
    return query_norm * key_norm * (EXP2_SCALE * EXP2_SCALE) <= PLAIN * PLAIN


def plain_tile(keys, q_ref, visible, l_ref, parts, mt_ref, tile):
    mt_ref[tile] = jnp.zeros(STAT, F32)
    keys = jnp.concatenate([keys, keys], axis=1)
    for n in range(0, GROUP, CHUNK):
        rows = slice(n * CTOK, (n + CHUNK) * CTOK)
        e = jnp.exp2(dot(keys, q_ref[rows, :], ((1,), (1,))))
        if visible is not None:
            e = jnp.where(jnp.concatenate([visible] * CHUNK, axis=1), e, 0.0)
        total = jnp.sum(e, axis=0, keepdims=True)
        for h in range(CHUNK):
            l_ref[n + h : n + h + 1, :] += total[:, h * CTOK : (h + 1) * CTOK]
        low = e.astype(BF16)
        start = 0
        for ref in parts:
            ref[:, rows] = low[start : start + ref.shape[0]]
            start += ref.shape[0]


def general_tile(keys, q_ref, visible, m_ref, l_ref, parts, mt_ref, tile):
    keys = jnp.concatenate([keys, keys], axis=1)

    def one_head(n, carry):
        columns = pl.ds(pl.multiple_of(n * CTOK, CTOK), CTOK)
        row = pl.ds(n, 1)
        scores = dot(keys, q_ref[columns, :], ((1,), (1,)))
        if visible is not None:
            scores = jnp.where(visible, scores, -jnp.inf)
        m_old = m_ref[row, :]
        m_new = jnp.maximum(m_old, jnp.max(scores, axis=0, keepdims=True))
        e = jnp.exp2(scores - m_new)
        total = jnp.sum(e, axis=0, keepdims=True)
        l_ref[row, :] = l_ref[row, :] * jnp.exp2(m_old - m_new) + total
        m_ref[row, :] = m_new
        mt_ref[tile, row, :] = m_new
        start = 0
        for ref in parts:
            ref[:, columns] = e[start : start + ref.shape[0]].astype(BF16)
            start += ref.shape[0]
        return carry

    lax.fori_loop(0, GROUP, one_head, 0)


def bring_to(m_ref, members):
    change = functools.reduce(jnp.maximum, [jnp.abs(mt_ref[tile] - m_ref[...]) for _, mt_ref, tile in members])

    @pl.when(jnp.max(change) != 0.0)
    def _():
        for ref, mt_ref, tile in members:
            log_change = mt_ref[tile] - m_ref[...]
            factor = jnp.exp2(jnp.concatenate([log_change[n : n + 1] for n in range(GROUP)], axis=1))

            def some_rows(step, carry, ref=ref, factor=factor):
                rows = pl.ds(pl.multiple_of(step * 16, 16), 16)
                ref[rows, :] = (ref[rows, :].astype(F32) * factor).astype(BF16)
                return carry

            lax.fori_loop(0, ref.shape[0] // 16, some_rows, 0)


def y_place():
    y_high = lax.axis_index("req")
    y_low = lax.rem(lax.div(lax.axis_index("blk"), CORES), 2)
    return y_high, jnp.where(y_low == 0, y_high, 1 - y_high)


def half_rows(at):
    return pl.ds(pl.multiple_of(at * HALF, HALF), HALF)


def fetch(pairs, sems):
    copies = [pltpu.make_async_copy(far, near, sems.at[at]) for at, (far, near) in enumerate(pairs)]
    for copy in copies:
        copy.start()
    for copy in copies:
        copy.wait()


def pack_kernel(k_hbm, v_hbm, kv_ref, turned_ref, sems):
    y_high, _ = y_place()
    pairs = []
    for far, columns in ((k_hbm, slice(0, HD)), (v_hbm, slice(HD, 2 * HD))):
        pairs.append((far, kv_ref.at[:, columns]))
        pairs.append((far.at[half_rows(1 - y_high), :], turned_ref.at[:HALF, columns]))
        pairs.append((far.at[half_rows(y_high), :], turned_ref.at[HALF:, columns]))
    fetch(pairs, sems)


def self_scores_kernel(
    q_hbm, k_hbm, out_hbm, do_hbm, step_hbm, *refs
):
    e_ref, mt_ref, m_ref, l_ref, q_out, do_out, norm_ref, q_ref, k_ref, out_ref, do_ref, step_ref, sems = refs
    fetch(
        [(k_hbm, k_ref), (step_hbm, step_ref), (q_hbm, q_ref), (do_hbm, do_ref), (out_hbm, out_ref)], sems
    )
    keys = k_ref[...]
    step = jnp.broadcast_to(step_ref[...].astype(F32), (CTOK, CTOK))
    visible = step.T <= step
    lane = lax.broadcasted_iota(jnp.int32, (CTOK, HD), 1)
    norm = None
    for n in range(GROUP):
        do_n = part(do_ref, n, HD)
        left = jnp.sum(do_n.astype(F32) * part(out_ref, n, HD).astype(F32), axis=1, keepdims=True)
        terms = jnp.zeros((CTOK, HD), F32)
        for place_at in range(3):
            term = left.astype(BF16).astype(F32)
            terms = jnp.where(lane == place_at, -term, terms)
            left = left - term
        do_out[n * CTOK : (n + 1) * CTOK, :HD] = do_n
        do_out[n * CTOK : (n + 1) * CTOK, HD:] = terms.astype(BF16)
        scaled = part(q_ref, n, HD).astype(F32) * EXP2_SCALE
        high = scaled.astype(BF16)
        q_out[n * CTOK : (n + 1) * CTOK, :HD] = high
        q_out[n * CTOK : (n + 1) * CTOK, HD:] = (scaled - high.astype(F32)).astype(BF16)
        rows = largest_norm(part(q_ref, n, HD))
        norm = rows if norm is None else jnp.maximum(norm, rows)
    norm_ref[...] = jnp.full(norm_ref.shape, norm, F32)
    l_ref[...] = jnp.zeros(STAT, F32)
    m_ref[...] = jnp.zeros(STAT, F32)
    plain_tile(keys, q_out, visible, l_ref, [e_ref], mt_ref, 0)

    @pl.when(jnp.logical_not(within(norm, largest_norm(keys))))
    def _():
        l_ref[...] = jnp.zeros(STAT, F32)
        m_ref[...] = jnp.full(STAT, -1e30, F32)
        general_tile(keys, q_out, visible, m_ref, l_ref, [e_ref], mt_ref, 0)


def prompt_scores_kernel(pieces, rows, earlier, *refs):
    tiles = len(rows)
    norm_ref, q_ref, m_in, l_in, *refs = refs
    kv_refs, refs = refs[:tiles], refs[tiles:]
    if earlier:
        do_ref, *refs = refs
        tops = max(top for top, _ in earlier) + 1
        mt_refs, refs = refs[:tops], refs[tops + len(earlier) :]
    e_refs, refs = refs[: tiles * pieces], refs[tiles * pieces :]
    mt_ref, m_ref, l_ref, *refs = refs
    m_ref[...] = m_in[...]
    l_ref[...] = l_in[...]
    for tile, (kv_ref, row) in enumerate(zip(kv_refs, rows)):
        keys = kv_ref[row : row + TILE, :HD]
        parts = e_refs[tile * pieces : (tile + 1) * pieces]
        l_old = l_ref[...]
        plain = within(jnp.max(norm_ref[...]), largest_norm(keys)) & (jnp.max(jnp.abs(m_ref[...])) == 0.0)
        plain_tile(keys, q_ref, None, l_ref, parts, mt_ref, tile)

        @pl.when(jnp.logical_not(plain))
        def _():
            l_ref[...] = l_old
            general_tile(keys, q_ref, None, m_ref, l_ref, parts, mt_ref, tile)

    if earlier:
        wq_ref, wdo_ref, *blocks = refs
        weights = (1.0 / l_ref[...]).T
        for n in range(GROUP):
            weight = jnp.broadcast_to(weights[:, n : n + 1], (CTOK, HD))
            heads = slice(n * CTOK, (n + 1) * CTOK)
            q_n = q_ref[heads, :HD].astype(F32) + q_ref[heads, HD:].astype(F32)
            wq_ref[heads, :] = (q_n * (weight * (1.0 / EXP2_SCALE))).astype(BF16)
            wdo_ref[heads, :] = (do_ref[heads, :HD].astype(F32) * weight).astype(BF16)
        members = [(ref, mt_refs[top], tile) for ref, (top, tile) in zip(blocks, earlier)]
        members += [(ref, mt_ref, at // pieces) for at, ref in enumerate(e_refs)]
        bring_to(m_ref, members)


def stack(parts):
    return parts[0] if len(parts) == 1 else jnp.concatenate(parts, axis=0)


def back_rows(pieces, do_ref, wq_ref, wdo_ref, dq_ref):
    keys = stack([keys for keys, _, _ in pieces])
    values = stack([values for _, values, _ in pieces])
    lane = lax.broadcasted_iota(jnp.int32, values.shape, 1)
    ones = jnp.where(lane < 3, 1.0, 0.0).astype(BF16)
    values = jnp.concatenate([values, ones], axis=1)
    keys_t = keys.T
    grad_keys = grad_values = None
    for n in range(0, GROUP, HEADS):
        columns = slice(n * CTOK, (n + HEADS) * CTOK)
        e = stack([e_ref[:, columns] for _, _, e_ref in pieces])
        grad_prob = dot(values, do_ref[columns, :], ((1,), (1,)))
        part_value = dot(e, wdo_ref[columns, :], ((1,), (0,)))
        grad_score = e * grad_prob.astype(BF16)
        part_key = dot(grad_score, wq_ref[columns, :], ((1,), (0,)))
        dq_ref[:, columns] += dot(keys_t, grad_score, ((1,), (0,)))
        grad_keys = part_key if n == 0 else grad_keys + part_key
        grad_values = part_value if n == 0 else grad_values + part_value
    return grad_keys * SCALE, grad_values


def prompt_back_kernel(first, last, tiles, sources, blocks, unread, *refs):
    do_ref, wq_ref, wdo_ref, *refs = refs
    if not first:
        dq_in, *refs = refs
    if last:
        l_ref, *refs = refs
    kv_refs, refs = refs[:sources], refs[sources:]
    e_refs, refs = refs[:blocks], refs[blocks + unread :]
    *out_refs, dq_ref = refs
    if last:
        *out_refs, query_ref = out_refs
    dq_ref[...] = jnp.zeros_like(dq_ref) if first else dq_in[...]
    for members, outs in tiles:
        pieces = []
        for source, row, block in members:
            e_ref = e_refs[block]
            rows = slice(row, row + e_ref.shape[0])
            kv_ref = kv_refs[source]
            pieces.append((kv_ref[rows, :HD], kv_ref[rows, HD:], e_ref))
        grad_keys, grad_values = back_rows(pieces, do_ref, wq_ref, wdo_ref, dq_ref)
        start = 0
        for at in outs:
            ref = out_refs[at]
            rows = slice(start, start + ref.shape[0])
            ref[:, :HD] = grad_keys[rows].astype(ref.dtype)
            ref[:, HD:] = grad_values[rows].astype(ref.dtype)
            start += ref.shape[0]
    if last:
        for n in range(GROUP):
            weight = SCALE / l_ref[n : n + 1, :]
            query_ref[:, n * HD : (n + 1) * HD] = (part(dq_ref, n, CTOK) * weight).T.astype(BF16)


def self_back_kernel(do_ref, wq_ref, wdo_ref, dq_in, k_ref, v_ref, e_ref, dk_ref, dv_ref, dq_ref):
    dq_ref[...] = dq_in[...]
    pieces = [(k_ref[...], v_ref[...], e_ref)]
    grad_keys, grad_values = back_rows(pieces, do_ref, wq_ref, wdo_ref, dq_ref)
    dk_ref[...] = grad_keys.astype(BF16)
    dv_ref[...] = grad_values.astype(BF16)


def combine_kernel(mine_ref, pair_ref, left_ref, right_ref, across_ref, above_ref, below_ref, own_ref):
    y_high, up = y_place()

    def arrived(at):
        rows = half_rows(at)
        return left_ref[rows, :].astype(F32) + right_ref[rows, :].astype(F32)

    def leaving(at, beside):
        rows = half_rows(at)
        return (mine_ref[rows, :] + pair_ref[rows, :].astype(F32) + arrived(beside)).astype(BF16)

    across_ref[...] = leaving(0, 1 - y_high)
    above_ref[...] = leaving(1 + up, 2 + up)
    below_ref[...] = leaving(2 - up, 3 - up)
    own_ref[...] = arrived(y_high)


def finish_kernel(own_ref, mine_ref, pair_ref, across_ref, above_ref, below_ref, dk_ref, dv_ref):
    total = own_ref[...] + mine_ref[...]
    for ref in (pair_ref, across_ref, above_ref, below_ref):
        total = total + ref[...].astype(F32)
    dk_ref[...] = total[:, :HD].astype(BF16)
    dv_ref[...] = total[:, HD:].astype(BF16)


def params(mib):
    return pltpu.CompilerParams(vmem_limit_bytes=mib * 1024 * 1024)


VMEM = pl.BlockSpec(memory_space=pltpu.VMEM)
HBM = pl.BlockSpec(memory_space=pltpu.HBM)
SMEM = pl.BlockSpec(memory_space=pltpu.SMEM)
UNREAD = pl.BlockSpec(memory_space=pl.ANY)


def whole(dims):
    return pl.BlockSpec(dims, lambda *_: (0,) * len(dims))


def cost(rows, matmuls, exps, stored):
    return pl.CostEstimate(
        flops=2 * rows * WIDE * HD * matmuls,
        bytes_accessed=rows * WIDE * 2 * stored,
        transcendentals=rows * WIDE * exps,
    )


def shape(dims, dtype=F32):
    return jax.ShapeDtypeStruct(dims, dtype)


def pack(keys, values):
    return pl.pallas_call(
        pack_kernel,
        in_specs=[HBM] * 2,
        out_specs=(VMEM,) * 2,
        out_shape=(shape((ROWS, 2 * HD), BF16),) * 2,
        scratch_shapes=[pltpu.SemaphoreType.DMA((6,))],
        compiler_params=params(60),
        name="pack",
    )(keys, values)


def self_scores(query, key_comp, out, d_out, steps):
    return pl.pallas_call(
        self_scores_kernel,
        in_specs=[HBM] * 5,
        out_specs=(VMEM,) * 7,
        scratch_shapes=[
            pltpu.VMEM((CTOK, GROUP * HD), BF16),
            pltpu.VMEM((CTOK, HD), BF16),
            pltpu.VMEM((CTOK, GROUP * HD), BF16),
            pltpu.VMEM((CTOK, GROUP * HD), BF16),
            pltpu.VMEM((1, CTOK), jnp.int32),
            pltpu.SemaphoreType.DMA((5,)),
        ],
        out_shape=(
            shape((CTOK, WIDE), BF16),
            shape((1,) + STAT),
            shape(STAT),
            shape(STAT),
            shape((WIDE, 2 * HD), BF16),
            shape((WIDE, 2 * HD), BF16),
            shape((8, HD)),
        ),
        compiler_params=params(57),
        cost_estimate=cost(CTOK, 1, 1, 1),
        name="self_scores",
    )(query, key_comp, out, d_out, steps)


def prompt_scores(norm, query, m, l, kvs, rows, split=(ROWS, ROWS), d_out=None, tops=(), blocks=(), earlier=()):
    tiles = len(kvs)
    count = tiles * len(split)
    operands = [norm, query, m, l, *kvs] + ([d_out, *tops, *blocks] if blocks else [])
    out_shape = tuple(shape((count, WIDE), BF16) for count in split) * tiles
    out_shape += (shape((tiles,) + STAT), shape(STAT), shape(STAT))
    if blocks:
        out_shape += (shape((WIDE, HD), BF16),) * 2 + tuple(shape(block.shape, BF16) for block in blocks)
    first_in, first_out = len(operands) - len(blocks), len(out_shape) - len(blocks)
    results = pl.pallas_call(
        functools.partial(prompt_scores_kernel, len(split), rows, earlier),
        in_specs=[VMEM] * len(operands),
        out_specs=(VMEM,) * len(out_shape),
        out_shape=out_shape,
        input_output_aliases={first_in + at: first_out + at for at in range(len(blocks))},
        compiler_params=params(16),
        cost_estimate=cost(tiles * TILE, 1, 1, 1),
        name="prompt_scores",
    )(*operands)
    return results[:count], *results[count:]


def prompt_back(shared, dq, kvs, tiles, es, outs, after=(), l=None):
    first, last = dq is None, l is not None
    operands = [*shared] + ([] if first else [dq]) + ([l] if last else []) + [*kvs, *es]
    out_shape = tuple(shape((rows, 2 * HD), dtype) for rows, dtype in outs)
    out_shape += (shape((CTOK, GROUP * HD), BF16) if last else shape(DQ),)
    return pl.pallas_call(
        functools.partial(prompt_back_kernel, first, last, tiles, len(kvs), len(es), len(after)),
        in_specs=[VMEM] * len(operands) + [UNREAD] * len(after),
        out_specs=(VMEM,) * len(out_shape),
        out_shape=out_shape,
        scratch_shapes=[pltpu.VMEM(DQ, F32)] if last else [],
        compiler_params=params(20),
        cost_estimate=cost(sum(e.shape[0] for e in es), 4, 0, 1),
        name="prompt_back",
    )(*operands, *after)


def self_back(shared, dq, key_comp, value_comp, e):
    return pl.pallas_call(
        self_back_kernel,
        in_specs=[VMEM] * 7,
        out_specs=(VMEM,) * 3,
        out_shape=(shape((CTOK, HD), BF16), shape((CTOK, HD), BF16), shape(DQ)),
        compiler_params=params(20),
        cost_estimate=cost(CTOK, 4, 0, 1),
        name="self_back",
    )(*shared, dq, key_comp, value_comp, e)


def combine(*arrays):
    return pl.pallas_call(
        combine_kernel,
        in_specs=[VMEM] * 4,
        out_specs=(VMEM,) * 4,
        out_shape=(shape((HALF, 2 * HD), BF16),) * 3 + (shape((HALF, 2 * HD)),),
        compiler_params=params(6),
        name="combine",
    )(*arrays)


def finish(*arrays):
    return pl.pallas_call(
        finish_kernel,
        in_specs=[VMEM] * 6,
        out_specs=(VMEM,) * 2,
        out_shape=(shape((HALF, HD), BF16),) * 2,
        compiler_params=params(6),
        name="finish",
    )(*arrays)


def behind(result, *blocks):
    return lax.optimization_barrier(blocks + (result,))[:-1]


def shards(query, key_comp, value_comp, key_prompt, value_prompt, out, d_out, steps):
    here, turned = pack(key_prompt, value_prompt)

    here_y = send(here, dy=1)
    left = send(here, dx=1)
    right = send(here, dx=-1)
    e_self, mt_self, m, l, query, d_out, norm = self_scores(query, key_comp, out, d_out, steps.reshape(1, CTOK))
    here_y, left, right = behind(m, here_y, left, right)
    far = send(left, dx=1)
    near = stack([turned, here_y, left, right])
    near_pair = send(near, dc=1)
    left_y = send(left, dy=1)
    right_y = send(right, dy=-1)
    split = (HALF, HALF, ROWS)
    e_near, mt_near, m, l = prompt_scores(norm, query, m, l, [near, near_pair], (0, 0), split)
    (far,) = behind(m, far)
    far_y = send(far, dy=-1)
    left_y, right_y = behind(far, left_y, right_y)
    corners = stack([left_y, right_y])
    kvs = [near, near_pair, corners]
    e_beside, mt_beside, m, l = prompt_scores(norm, query, m, l, kvs, (TILE, TILE, 0))
    (far_y,) = behind(m, far_y)
    corners_pair = send(behind(m, corners)[0], dc=1)
    opposite = stack([far, far_y])
    opposite_pair = send(opposite, dc=1)
    e_others, mt_others, m, l = prompt_scores(norm, query, m, l, [corners_pair], (0,))
    (opposite_pair,) = behind(m, opposite_pair)
    blocks = [*e_near, *e_beside, *e_others, e_self]
    tops = [mt_near, mt_beside, mt_others, mt_self]
    earlier = [(0, at // 3) for at in range(6)] + [(1, at // 2) for at in range(6)] + [(2, 0), (2, 0), (3, 0)]
    kvs = [opposite, opposite_pair]
    e_far, _, m, l, wq, wdo, *blocks = prompt_scores(
        norm, query, m, l, kvs, (0, 0), d_out=d_out, tops=tops, blocks=blocks, earlier=earlier
    )
    e_near, e_beside, e_corners, e_self = blocks[:6], blocks[6:10], blocks[10:14], blocks[14]

    shared = d_out, wq, wdo
    add = lambda *parts: sum(rows.astype(F32) for rows in parts)
    both = [(TILE, F32), (TILE, BF16)]
    tiles = [([(1, 0, 2), (1, ROWS, 3)], [1]), ([(0, 0, 0), (0, ROWS, 1)], [0])]
    mine, theirs, dq = prompt_back(shared, None, [opposite, opposite_pair], tiles, e_far, both)
    pair_far = send(theirs, dc=1)
    total = add(mine, pair_far).astype(BF16)
    far_right = send(total[:ROWS], dx=1)
    far_left = send(total[ROWS:], dx=-1)

    def side(at, dq, after):
        row = at * ROWS
        beside = TILE + row
        tiles = [
            ([(1, beside, 1), (3, row, 3)], [1]),
            ([(0, beside, 0), (2, row, 2)], [0]),
        ]
        es = [e_beside[at], e_beside[2 + at], e_corners[at], e_corners[2 + at]]
        kvs = [near, near_pair, corners, corners_pair]
        return prompt_back(shared, dq, kvs, tiles, es, both, after)

    mine_left, theirs, dq = side(0, dq, ())
    pair_left = send(theirs, dc=1)
    mine_right, theirs, dq = side(1, dq, (far_left, far_right))
    pair_right = send(theirs, dc=1)
    (pair_left,) = behind(theirs, pair_left)
    total = stack([add(mine_left[:ROWS], pair_left[:ROWS]), add(mine_left[ROWS:], pair_left[ROWS:], far_left)])
    from_right = send(total.astype(BF16), dx=-1)
    total = stack([add(mine_right[:ROWS], pair_right[:ROWS], far_right), add(mine_right[ROWS:], pair_right[ROWS:])])
    from_left = send(total.astype(BF16), dx=1)

    kvs = [near, near_pair]
    tiles = [([(1, 0, 1), (1, ROWS, 3)], [1]), ([(0, 0, 0), (0, ROWS, 2)], [0])]
    es = [e_near[0], e_near[3], e_near[2], e_near[5]]
    outs = [(HALF + ROWS, F32), (HALF + ROWS, BF16)]
    mine, theirs, dq = prompt_back(shared, dq, kvs, tiles, es, outs, (pair_right,))
    pair = send(theirs, dc=1)
    grad_key_comp, grad_value_comp, dq = self_back(shared, dq, key_comp, value_comp, e_self)
    pair, from_left, from_right = behind(grad_key_comp, pair, from_left, from_right)
    across, above, below, own = combine(mine, pair, from_left, from_right)
    across = send(across, dy=2)
    above = send(above, dy=1)
    below = send(below, dy=-1)
    tiles = [([(0, HALF, 0), (1, HALF, 1)], [0, 1])]
    es = [e_near[1], e_near[4]]
    outs = [(HALF, F32), (HALF, BF16)]
    mine, theirs, grad_query = prompt_back(shared, dq, kvs, tiles, es, outs, (own,), l)
    pair = send(theirs, dc=1)
    across, above, below = behind(mine, across, above, below)
    grad_key_prompt, grad_value_prompt = finish(own, mine, pair, across, above, below)
    return (grad_query, grad_key_comp, grad_value_comp, grad_key_prompt, grad_value_prompt)


def solution(mesh):
    rows = P(("blk", "req"), "head")
    return jax.shard_map(
        shards,
        mesh=mesh,
        in_specs=(rows, rows, rows, P("blk", "head"), P("blk", "head"), rows, rows, P(("blk", "req"))),
        out_specs=(rows,) * 5,
        check_vma=False,
    )
```

```python
import functools

import jax
import jax.numpy as jnp
from jax import lax
from jax.experimental import pallas as pl
from jax.experimental.pallas import tpu as pltpu
from jax.sharding import PartitionSpec as P

HD = 128
GROUP = 8
CTOK = 256
ROWS = 384
TILE = 2 * ROWS
HALF = ROWS // 2
X, Y, CORES = 4, 4, 2
SCALE = HD ** (-0.5)
EXP2_SCALE = SCALE * 1.4426950408889634
PLAIN = 60.0
STAT = (GROUP, CTOK)
WIDE = GROUP * CTOK
DQ = (HD, WIDE)
HEADS = 8
CHUNK = 4
F32 = jnp.float32
BF16 = jnp.bfloat16


def place(x, y, core):
    return ((x * 2 + y % 2) * CORES + core) * 2 + y // 2


def send(block, dx=0, dy=0, dc=0):
    route = []
    for x in range(X):
        for y in range(Y):
            for core in range(CORES):
                there = place((x + dx) % X, (y + dy) % Y, core ^ dc)
                route.append((place(x, y, core), there))
    return lax.ppermute(block, ("blk", "req"), route)


def part(ref, n, width):
    return ref[:, n * width : (n + 1) * width]


def dot(a, b, contract):
    return lax.dot_general(a, b, (contract, ((), ())), preferred_element_type=F32)


def largest_norm(rows):
    wide = rows.astype(F32)
    return jnp.max(jnp.sum(wide * wide, axis=1, keepdims=True))


def within(query_norm, key_norm):
    return query_norm * key_norm * (EXP2_SCALE * EXP2_SCALE) <= PLAIN * PLAIN


def plain_tile(keys, q_ref, visible, l_ref, parts, mt_ref, tile):
    mt_ref[tile] = jnp.zeros(STAT, F32)
    keys = jnp.concatenate([keys, keys], axis=1)
    for n in range(0, GROUP, CHUNK):
        rows = slice(n * CTOK, (n + CHUNK) * CTOK)
        e = jnp.exp2(dot(keys, q_ref[rows, :], ((1,), (1,))))
        if visible is not None:
            e = jnp.where(jnp.concatenate([visible] * CHUNK, axis=1), e, 0.0)
        total = jnp.sum(e, axis=0, keepdims=True)
        for h in range(CHUNK):
            l_ref[n + h : n + h + 1, :] += total[:, h * CTOK : (h + 1) * CTOK]
        low = e.astype(BF16)
        start = 0
        for ref in parts:
            ref[:, rows] = low[start : start + ref.shape[0]]
            start += ref.shape[0]


def general_tile(keys, q_ref, visible, m_ref, l_ref, parts, mt_ref, tile):
    keys = jnp.concatenate([keys, keys], axis=1)

    def one_head(n, carry):
        columns = pl.ds(pl.multiple_of(n * CTOK, CTOK), CTOK)
        row = pl.ds(n, 1)
        scores = dot(keys, q_ref[columns, :], ((1,), (1,)))
        if visible is not None:
            scores = jnp.where(visible, scores, -jnp.inf)
        m_old = m_ref[row, :]
        m_new = jnp.maximum(m_old, jnp.max(scores, axis=0, keepdims=True))
        e = jnp.exp2(scores - m_new)
        total = jnp.sum(e, axis=0, keepdims=True)
        l_ref[row, :] = l_ref[row, :] * jnp.exp2(m_old - m_new) + total
        m_ref[row, :] = m_new
        mt_ref[tile, row, :] = m_new
        start = 0
        for ref in parts:
            ref[:, columns] = e[start : start + ref.shape[0]].astype(BF16)
            start += ref.shape[0]
        return carry

    lax.fori_loop(0, GROUP, one_head, 0)


def bring_to(m_ref, members):
    change = functools.reduce(jnp.maximum, [jnp.abs(mt_ref[tile] - m_ref[...]) for _, mt_ref, tile in members])

    @pl.when(jnp.max(change) != 0.0)
    def _():
        for ref, mt_ref, tile in members:
            log_change = mt_ref[tile] - m_ref[...]
            factor = jnp.exp2(jnp.concatenate([log_change[n : n + 1] for n in range(GROUP)], axis=1))

            def some_rows(step, carry, ref=ref, factor=factor):
                rows = pl.ds(pl.multiple_of(step * 16, 16), 16)
                ref[rows, :] = (ref[rows, :].astype(F32) * factor).astype(BF16)
                return carry

            lax.fori_loop(0, ref.shape[0] // 16, some_rows, 0)


def y_place():
    y_high = lax.axis_index("req")
    y_low = lax.rem(lax.div(lax.axis_index("blk"), CORES), 2)
    return y_high, jnp.where(y_low == 0, y_high, 1 - y_high)


def half_rows(at):
    return pl.ds(pl.multiple_of(at * HALF, HALF), HALF)


def fetch(pairs, sems):
    copies = [pltpu.make_async_copy(far, near, sems.at[at]) for at, (far, near) in enumerate(pairs)]
    for copy in copies:
        copy.start()
    for copy in copies:
        copy.wait()


def pack_kernel(k_hbm, v_hbm, kv_ref, turned_ref, sems):
    y_high, _ = y_place()
    pairs = []
    for far, columns in ((k_hbm, slice(0, HD)), (v_hbm, slice(HD, 2 * HD))):
        pairs.append((far, kv_ref.at[:, columns]))
        pairs.append((far.at[half_rows(1 - y_high), :], turned_ref.at[:HALF, columns]))
        pairs.append((far.at[half_rows(y_high), :], turned_ref.at[HALF:, columns]))
    fetch(pairs, sems)


def self_scores_kernel(
    q_hbm, k_hbm, out_hbm, do_hbm, step_hbm, *refs
):
    e_ref, mt_ref, m_ref, l_ref, q_out, do_out, norm_ref, q_ref, k_ref, out_ref, do_ref, step_ref, sems = refs
    fetch(
        [(k_hbm, k_ref), (step_hbm, step_ref), (q_hbm, q_ref), (do_hbm, do_ref), (out_hbm, out_ref)], sems
    )
    keys = k_ref[...]
    step = jnp.broadcast_to(step_ref[...].astype(F32), (CTOK, CTOK))
    visible = step.T <= step
    lane = lax.broadcasted_iota(jnp.int32, (CTOK, HD), 1)
    norm = None
    for n in range(GROUP):
        do_n = part(do_ref, n, HD)
        left = jnp.sum(do_n.astype(F32) * part(out_ref, n, HD).astype(F32), axis=1, keepdims=True)
        terms = jnp.zeros((CTOK, HD), F32)
        for place_at in range(3):
            term = left.astype(BF16).astype(F32)
            terms = jnp.where(lane == place_at, -term, terms)
            left = left - term
        do_out[n * CTOK : (n + 1) * CTOK, :HD] = do_n
        do_out[n * CTOK : (n + 1) * CTOK, HD:] = terms.astype(BF16)
        scaled = part(q_ref, n, HD).astype(F32) * EXP2_SCALE
        high = scaled.astype(BF16)
        q_out[n * CTOK : (n + 1) * CTOK, :HD] = high
        q_out[n * CTOK : (n + 1) * CTOK, HD:] = (scaled - high.astype(F32)).astype(BF16)
        rows = largest_norm(part(q_ref, n, HD))
        norm = rows if norm is None else jnp.maximum(norm, rows)
    norm_ref[...] = jnp.full(norm_ref.shape, norm, F32)
    l_ref[...] = jnp.zeros(STAT, F32)
    m_ref[...] = jnp.zeros(STAT, F32)
    plain_tile(keys, q_out, visible, l_ref, [e_ref], mt_ref, 0)

    @pl.when(jnp.logical_not(within(norm, largest_norm(keys))))
    def _():
        l_ref[...] = jnp.zeros(STAT, F32)
        m_ref[...] = jnp.full(STAT, -1e30, F32)
        general_tile(keys, q_out, visible, m_ref, l_ref, [e_ref], mt_ref, 0)


def prompt_scores_kernel(pieces, rows, earlier, *refs):
    tiles = len(rows)
    norm_ref, q_ref, m_in, l_in, *refs = refs
    kv_refs, refs = refs[:tiles], refs[tiles:]
    if earlier:
        do_ref, *refs = refs
        tops = max(top for top, _ in earlier) + 1
        mt_refs, refs = refs[:tops], refs[tops + len(earlier) :]
    e_refs, refs = refs[: tiles * pieces], refs[tiles * pieces :]
    mt_ref, m_ref, l_ref, *refs = refs
    m_ref[...] = m_in[...]
    l_ref[...] = l_in[...]
    for tile, (kv_ref, row) in enumerate(zip(kv_refs, rows)):
        keys = kv_ref[row : row + TILE, :HD]
        parts = e_refs[tile * pieces : (tile + 1) * pieces]
        l_old = l_ref[...]
        plain = within(jnp.max(norm_ref[...]), largest_norm(keys)) & (jnp.max(jnp.abs(m_ref[...])) == 0.0)
        plain_tile(keys, q_ref, None, l_ref, parts, mt_ref, tile)

        @pl.when(jnp.logical_not(plain))
        def _():
            l_ref[...] = l_old
            general_tile(keys, q_ref, None, m_ref, l_ref, parts, mt_ref, tile)

    if earlier:
        wq_ref, wdo_ref, *blocks = refs
        weights = (1.0 / l_ref[...]).T
        for n in range(GROUP):
            weight = jnp.broadcast_to(weights[:, n : n + 1], (CTOK, HD))
            heads = slice(n * CTOK, (n + 1) * CTOK)
            q_n = q_ref[heads, :HD].astype(F32) + q_ref[heads, HD:].astype(F32)
            wq_ref[heads, :] = (q_n * (weight * (1.0 / EXP2_SCALE))).astype(BF16)
            wdo_ref[heads, :] = (do_ref[heads, :HD].astype(F32) * weight).astype(BF16)
        members = [(ref, mt_refs[top], tile) for ref, (top, tile) in zip(blocks, earlier)]
        members += [(ref, mt_ref, at // pieces) for at, ref in enumerate(e_refs)]
        bring_to(m_ref, members)


def stack(parts):
    return parts[0] if len(parts) == 1 else jnp.concatenate(parts, axis=0)


def back_rows(pieces, do_ref, wq_ref, wdo_ref, dq_ref):
    keys = stack([keys for keys, _, _ in pieces])
    values = stack([values for _, values, _ in pieces])
    lane = lax.broadcasted_iota(jnp.int32, values.shape, 1)
    ones = jnp.where(lane < 3, 1.0, 0.0).astype(BF16)
    values = jnp.concatenate([values, ones], axis=1)
    keys_t = keys.T
    grad_keys = grad_values = None
    for n in range(0, GROUP, HEADS):
        columns = slice(n * CTOK, (n + HEADS) * CTOK)
        e = stack([e_ref[:, columns] for _, _, e_ref in pieces])
        grad_prob = dot(values, do_ref[columns, :], ((1,), (1,)))
        part_value = dot(e, wdo_ref[columns, :], ((1,), (0,)))
        grad_score = e * grad_prob.astype(BF16)
        part_key = dot(grad_score, wq_ref[columns, :], ((1,), (0,)))
        dq_ref[:, columns] += dot(keys_t, grad_score, ((1,), (0,)))
        grad_keys = part_key if n == 0 else grad_keys + part_key
        grad_values = part_value if n == 0 else grad_values + part_value
    return grad_keys * SCALE, grad_values


def prompt_back_kernel(first, last, tiles, sources, blocks, unread, *refs):
    do_ref, wq_ref, wdo_ref, *refs = refs
    if not first:
        dq_in, *refs = refs
    if last:
        l_ref, *refs = refs
    kv_refs, refs = refs[:sources], refs[sources:]
    e_refs, refs = refs[:blocks], refs[blocks + unread :]
    *out_refs, dq_ref = refs
    if last:
        *out_refs, query_ref = out_refs
    dq_ref[...] = jnp.zeros_like(dq_ref) if first else dq_in[...]
    for members, outs in tiles:
        pieces = []
        for source, row, block in members:
            e_ref = e_refs[block]
            rows = slice(row, row + e_ref.shape[0])
            kv_ref = kv_refs[source]
            pieces.append((kv_ref[rows, :HD], kv_ref[rows, HD:], e_ref))
        grad_keys, grad_values = back_rows(pieces, do_ref, wq_ref, wdo_ref, dq_ref)
        start = 0
        for at in outs:
            ref = out_refs[at]
            rows = slice(start, start + ref.shape[0])
            ref[:, :HD] = grad_keys[rows].astype(ref.dtype)
            ref[:, HD:] = grad_values[rows].astype(ref.dtype)
            start += ref.shape[0]
    if last:
        for n in range(GROUP):
            weight = SCALE / l_ref[n : n + 1, :]
            query_ref[:, n * HD : (n + 1) * HD] = (part(dq_ref, n, CTOK) * weight).T.astype(BF16)


def self_back_kernel(do_ref, wq_ref, wdo_ref, dq_in, k_ref, v_ref, e_ref, *refs):
    dk_ref, dv_ref, dq_ref = refs[-3:]
    dq_ref[...] = dq_in[...]
    pieces = [(k_ref[...], v_ref[...], e_ref)]
    grad_keys, grad_values = back_rows(pieces, do_ref, wq_ref, wdo_ref, dq_ref)
    dk_ref[...] = grad_keys.astype(BF16)
    dv_ref[...] = grad_values.astype(BF16)


def combine_kernel(mine_ref, pair_ref, left_ref, right_ref, across_ref, above_ref, below_ref, own_ref):
    y_high, up = y_place()

    def arrived(at):
        rows = half_rows(at)
        return left_ref[rows, :].astype(F32) + right_ref[rows, :].astype(F32)

    def leaving(at, beside):
        rows = half_rows(at)
        return (mine_ref[rows, :] + pair_ref[rows, :].astype(F32) + arrived(beside)).astype(BF16)

    across_ref[...] = leaving(0, 1 - y_high)
    above_ref[...] = leaving(1 + up, 2 + up)
    below_ref[...] = leaving(2 - up, 3 - up)
    own_ref[...] = arrived(y_high)


def finish_kernel(own_ref, mine_ref, pair_ref, across_ref, above_ref, below_ref, dk_ref, dv_ref):
    total = own_ref[...] + mine_ref[...]
    for ref in (pair_ref, across_ref, above_ref, below_ref):
        total = total + ref[...].astype(F32)
    dk_ref[...] = total[:, :HD].astype(BF16)
    dv_ref[...] = total[:, HD:].astype(BF16)


def params(mib):
    return pltpu.CompilerParams(vmem_limit_bytes=mib * 1024 * 1024)


VMEM = pl.BlockSpec(memory_space=pltpu.VMEM)
HBM = pl.BlockSpec(memory_space=pltpu.HBM)
SMEM = pl.BlockSpec(memory_space=pltpu.SMEM)
UNREAD = pl.BlockSpec(memory_space=pl.ANY)


def whole(dims):
    return pl.BlockSpec(dims, lambda *_: (0,) * len(dims))


def cost(rows, matmuls, exps, stored):
    return pl.CostEstimate(
        flops=2 * rows * WIDE * HD * matmuls,
        bytes_accessed=rows * WIDE * 2 * stored,
        transcendentals=rows * WIDE * exps,
    )


def shape(dims, dtype=F32):
    return jax.ShapeDtypeStruct(dims, dtype)


def pack(keys, values):
    return pl.pallas_call(
        pack_kernel,
        in_specs=[HBM] * 2,
        out_specs=(VMEM,) * 2,
        out_shape=(shape((ROWS, 2 * HD), BF16),) * 2,
        scratch_shapes=[pltpu.SemaphoreType.DMA((6,))],
        compiler_params=params(60),
        name="pack",
    )(keys, values)


def self_scores(query, key_comp, out, d_out, steps):
    return pl.pallas_call(
        self_scores_kernel,
        in_specs=[HBM] * 5,
        out_specs=(VMEM,) * 7,
        scratch_shapes=[
            pltpu.VMEM((CTOK, GROUP * HD), BF16),
            pltpu.VMEM((CTOK, HD), BF16),
            pltpu.VMEM((CTOK, GROUP * HD), BF16),
            pltpu.VMEM((CTOK, GROUP * HD), BF16),
            pltpu.VMEM((1, CTOK), jnp.int32),
            pltpu.SemaphoreType.DMA((5,)),
        ],
        out_shape=(
            shape((CTOK, WIDE), BF16),
            shape((1,) + STAT),
            shape(STAT),
            shape(STAT),
            shape((WIDE, 2 * HD), BF16),
            shape((WIDE, 2 * HD), BF16),
            shape((8, HD)),
        ),
        compiler_params=params(57),
        cost_estimate=cost(CTOK, 1, 1, 1),
        name="self_scores",
    )(query, key_comp, out, d_out, steps)


def prompt_scores(norm, query, m, l, kvs, rows, split=(ROWS, ROWS), d_out=None, tops=(), blocks=(), earlier=()):
    tiles = len(kvs)
    count = tiles * len(split)
    operands = [norm, query, m, l, *kvs] + ([d_out, *tops, *blocks] if blocks else [])
    out_shape = tuple(shape((count, WIDE), BF16) for count in split) * tiles
    out_shape += (shape((tiles,) + STAT), shape(STAT), shape(STAT))
    if blocks:
        out_shape += (shape((WIDE, HD), BF16),) * 2 + tuple(shape(block.shape, BF16) for block in blocks)
    first_in, first_out = len(operands) - len(blocks), len(out_shape) - len(blocks)
    results = pl.pallas_call(
        functools.partial(prompt_scores_kernel, len(split), rows, earlier),
        in_specs=[VMEM] * len(operands),
        out_specs=(VMEM,) * len(out_shape),
        out_shape=out_shape,
        input_output_aliases={first_in + at: first_out + at for at in range(len(blocks))},
        compiler_params=params(16),
        cost_estimate=cost(tiles * TILE, 1, 1, 1),
        name="prompt_scores",
    )(*operands)
    return results[:count], *results[count:]


def prompt_back(shared, dq, kvs, tiles, es, outs, after=(), l=None):
    first, last = dq is None, l is not None
    operands = [*shared] + ([] if first else [dq]) + ([l] if last else []) + [*kvs, *es]
    out_shape = tuple(shape((rows, 2 * HD), dtype) for rows, dtype in outs)
    out_shape += (shape((CTOK, GROUP * HD), BF16) if last else shape(DQ),)
    return pl.pallas_call(
        functools.partial(prompt_back_kernel, first, last, tiles, len(kvs), len(es), len(after)),
        in_specs=[VMEM] * len(operands) + [UNREAD] * len(after),
        out_specs=(VMEM,) * len(out_shape),
        out_shape=out_shape,
        scratch_shapes=[pltpu.VMEM(DQ, F32)] if last else [],
        compiler_params=params(20),
        cost_estimate=cost(sum(e.shape[0] for e in es), 4, 0, 1),
        name="prompt_back",
    )(*operands, *after)


def self_back(shared, dq, key_comp, value_comp, e, after):
    return pl.pallas_call(
        self_back_kernel,
        in_specs=[VMEM] * 7 + [UNREAD] * len(after),
        out_specs=(VMEM,) * 3,
        out_shape=(shape((CTOK, HD), BF16), shape((CTOK, HD), BF16), shape(DQ)),
        compiler_params=params(20),
        cost_estimate=cost(CTOK, 4, 0, 1),
        name="self_back",
    )(*shared, dq, key_comp, value_comp, e, *after)


def combine(*arrays):
    return pl.pallas_call(
        combine_kernel,
        in_specs=[VMEM] * 4,
        out_specs=(VMEM,) * 4,
        out_shape=(shape((HALF, 2 * HD), BF16),) * 3 + (shape((HALF, 2 * HD)),),
        compiler_params=params(6),
        name="combine",
    )(*arrays)


def finish(*arrays):
    return pl.pallas_call(
        finish_kernel,
        in_specs=[VMEM] * 6,
        out_specs=(VMEM,) * 2,
        out_shape=(shape((HALF, HD), BF16),) * 2,
        compiler_params=params(6),
        name="finish",
    )(*arrays)


def behind(result, *blocks):
    return lax.optimization_barrier(blocks + (result,))[:-1]


def shards(query, key_comp, value_comp, key_prompt, value_prompt, out, d_out, steps):
    here, turned = pack(key_prompt, value_prompt)

    here_y = send(here, dy=1)
    left = send(here, dx=1)
    right = send(here, dx=-1)
    e_self, mt_self, m, l, query, d_out, norm = self_scores(query, key_comp, out, d_out, steps.reshape(1, CTOK))
    here_y, left, right = behind(m, here_y, left, right)
    far = send(left, dx=1)
    near = stack([turned, here_y, left, right])
    near_pair = send(near, dc=1)
    left_y = send(left, dy=1)
    right_y = send(right, dy=-1)
    split = (HALF, HALF, ROWS)
    e_near, mt_near, m, l = prompt_scores(norm, query, m, l, [near, near_pair], (0, 0), split)
    (far,) = behind(m, far)
    far_y = send(far, dy=-1)
    left_y, right_y = behind(far, left_y, right_y)
    corners = stack([left_y, right_y])
    kvs = [near, near_pair, corners]
    e_beside, mt_beside, m, l = prompt_scores(norm, query, m, l, kvs, (TILE, TILE, 0))
    (far_y,) = behind(m, far_y)
    corners_pair = send(behind(m, corners)[0], dc=1)
    opposite = stack([far, far_y])
    opposite_pair = send(opposite, dc=1)
    e_others, mt_others, m, l = prompt_scores(norm, query, m, l, [corners_pair], (0,))
    (opposite_pair,) = behind(m, opposite_pair)
    blocks = [*e_near, *e_beside, *e_others, e_self]
    tops = [mt_near, mt_beside, mt_others, mt_self]
    earlier = [(0, at // 3) for at in range(6)] + [(1, at // 2) for at in range(6)] + [(2, 0), (2, 0), (3, 0)]
    kvs = [opposite, opposite_pair]
    e_far, _, m, l, wq, wdo, *blocks = prompt_scores(
        norm, query, m, l, kvs, (0, 0), d_out=d_out, tops=tops, blocks=blocks, earlier=earlier
    )
    e_near, e_beside, e_corners, e_self = blocks[:6], blocks[6:10], blocks[10:14], blocks[14]

    shared = d_out, wq, wdo
    add = lambda *parts: sum(rows.astype(F32) for rows in parts)
    both = [(TILE, F32), (TILE, BF16)]
    def side(at, dq, after):
        row = at * ROWS
        beside = TILE + row
        tiles = [
            ([(1, beside, 1), (3, row, 3)], [1]),
            ([(0, beside, 0), (2, row, 2)], [0]),
        ]
        es = [e_beside[at], e_beside[2 + at], e_corners[at], e_corners[2 + at]]
        kvs = [near, near_pair, corners, corners_pair]
        return prompt_back(shared, dq, kvs, tiles, es, both, after)

    mine_left, theirs, dq = side(0, None, ())
    pair_left = send(theirs, dc=1)
    tiles = [([(1, 0, 2), (1, ROWS, 3)], [1]), ([(0, 0, 0), (0, ROWS, 1)], [0])]
    mine_far, theirs, dq = prompt_back(shared, dq, [opposite, opposite_pair], tiles, e_far, both)
    theirs, pair_left = lax.optimization_barrier((theirs, pair_left))
    pair_far = send(theirs, dc=1)
    from_right = send(add(mine_left, pair_left).astype(BF16), dx=-1)
    from_far = send(add(mine_far, pair_far).astype(BF16), dx=1)
    mine_right, theirs, dq = side(1, dq, ())
    pair_right = send(theirs, dc=1)
    after = (from_far, from_right)
    grad_key_comp, grad_value_comp, dq = self_back(shared, dq, key_comp, value_comp, e_self, after)
    (pair_right,) = behind(grad_key_comp, pair_right)
    from_left = send(add(mine_right, pair_right, from_far).astype(BF16), dx=1)

    kvs = [near, near_pair]
    tiles = [([(1, 0, 1), (1, ROWS, 3)], [1]), ([(0, 0, 0), (0, ROWS, 2)], [0])]
    es = [e_near[0], e_near[3], e_near[2], e_near[5]]
    outs = [(HALF + ROWS, F32), (HALF + ROWS, BF16)]
    mine, theirs, dq = prompt_back(shared, dq, kvs, tiles, es, outs, (pair_right,))
    pair = send(theirs, dc=1)
    (from_left,) = behind(mine, from_left)
    across, above, below, own = combine(mine, pair, from_left, from_right)
    across = send(across, dy=2)
    above = send(above, dy=1)
    below = send(below, dy=-1)
    tiles = [([(0, HALF, 0), (1, HALF, 1)], [0, 1])]
    es = [e_near[1], e_near[4]]
    outs = [(HALF, F32), (HALF, BF16)]
    mine, theirs, grad_query = prompt_back(shared, dq, kvs, tiles, es, outs, (own,), l)
    pair = send(theirs, dc=1)
    across, above, below = behind(mine, across, above, below)
    grad_key_prompt, grad_value_prompt = finish(own, mine, pair, across, above, below)
    return (grad_query, grad_key_comp, grad_value_comp, grad_key_prompt, grad_value_prompt)


def solution(mesh):
    rows = P(("blk", "req"), "head")
    return jax.shard_map(
        shards,
        mesh=mesh,
        in_specs=(rows, rows, rows, P("blk", "head"), P("blk", "head"), rows, rows, P(("blk", "req"))),
        out_specs=(rows,) * 5,
        check_vma=False,
    )
```
